32 devices in a mesh: grp: 4 (over x, core), seq: 2 (over y), dp: 4 (over z).
Axes of the slice: x: 2, y: 2, z: 4, core: 2. Of those that a mesh axis runs over, the one named last changes fastest.
Arguments:
- image: bfloat16 [16, 160, 3072], P(('grp', 'dp'), 'seq'), may hold values from -6 to 6
- noise: bfloat16 [16, 160, 3072], P(('grp', 'dp'), 'seq'), may hold values from -6 to 6
- text: bfloat16 [16, 96, 3072], P(('grp', 'dp'), 'seq'), may hold values from -6 to 6
- timestep: int32 [16], P(('grp', 'dp')), may hold values from 0 to 999
- guidance: float32 [16], P(('grp', 'dp')), may hold values from 1 to 5
- text_token_length: int32 [16], P(('grp', 'dp')), may hold values from 1 to 96
- image_projection_weight: bfloat16 [3072, 6144], P(None, 'seq'), may hold values from -0.109375 to 0.109375
- text_projection_weight: bfloat16 [3072, 4096], P(None, 'seq'), may hold values from -0.109375 to 0.109375
- modulation_weight: bfloat16 [256, 12288], P(None, 'seq'), may hold values from -0.375 to 0.375
- query_key_norm_gain: float32 [3, 128], replicated, may hold values from 0.5 to 1.5
- adapter_down_weight: bfloat16 [3072, 64], replicated, may hold values from -0.109375 to 0.109375
- adapter_up_weight: bfloat16 [64, 6144], P(None, 'seq'), may hold values from -0.75 to 0.75
Outputs:
- direction_a: float32 [3072, 64], replicated
- direction_b: float32 [64, 6144], P(None, 'seq')
- loss_mean: float32 [], replicated
The draws below stay inside these ranges and needn't reach their ends.
All inputs are finite; a program needn't handle non-finite values.
Results may differ from the reference program's by a relative error of at most 0.0032.
Values may be sent and summed in bfloat16 or wider, within the bound.
No kernel may reach another device: no remote copies, remote signals or barrier semaphores. Data moves between devices by JAX's collectives and lax.ppermute only.
A program may use at most 128 MiB of HBM per device.

```python
import math
import jax
import jax.numpy as jnp
from jax import lax

MODEL_WIDTH = 3072
HD = 128
HEADS = 16
ADAPTER_RANK = 64
EMB = 256
STEPS = 1000
IMG = 160
TXT = 96
SAMPLES = 16
QUERY_KEY_VALUE = 6144
KV = 4096


def set_ends(drawn, rng, low, high):
    place = [jax.random.randint(jax.random.fold_in(rng, axis), (), 0, length) for axis, length in enumerate(drawn.shape)]
    widest = drawn.shape.index(max(drawn.shape))
    beside = place[:widest] + [(place[widest] + 1) % drawn.shape[widest]] + place[widest + 1:]
    return drawn.at[tuple(place)].set(low).at[tuple(beside)].set(high)


def level_of(stream_key, extent, shards, low, high):
    def one(dim, shards_of):
        heights = jax.random.uniform(jax.random.fold_in(jax.random.fold_in(stream_key, 6), dim), (shards_of,), jnp.float32, low / len(shards), high / len(shards))
        return jnp.repeat(jnp.exp(heights), extent[dim] // shards_of).reshape((-1,) + (1,) * (len(extent) - dim - 1))

    level = one(*shards[0])
    for cut in shards[1:]:
        level = level * one(*cut)
    return level


def centred(own_key, extent, deviation, reach, cuts=(), kind=jnp.bfloat16):
    level = level_of(own_key, extent, cuts, -0.22, 0.18) if cuts else 1.0
    values = jax.random.normal(own_key, extent, jnp.float32) * deviation * level
    return jnp.minimum(jnp.maximum(values, -reach), reach).astype(kind)


def setup_inputs(seed: int = 0) -> dict:
    arg_keys = jax.random.split(jax.random.key(seed), 13)
    image = centred(arg_keys[0], (SAMPLES, IMG, MODEL_WIDTH), 1.0, 6.0, ((0, 16), (1, 2)))
    noise = centred(arg_keys[1], (SAMPLES, IMG, MODEL_WIDTH), 1.0, 6.0, ((0, 16), (1, 2)))
    text = centred(arg_keys[2], (SAMPLES, TXT, MODEL_WIDTH), 1.0, 6.0, ((0, 16), (1, 2)))
    timestep = set_ends(jax.random.randint(arg_keys[3], (SAMPLES,), 0, STEPS), jax.random.fold_in(arg_keys[3], 1), 0, STEPS - 1).astype(jnp.int32)
    guidance = jnp.clip(1.0 + 4.0 * jax.random.uniform(arg_keys[4], (SAMPLES,), jnp.float32) ** level_of(arg_keys[4], (SAMPLES,), ((0, 16),), -0.2, 0.2), 1.0, 5.0)
    text_token_length = set_ends(jax.random.randint(arg_keys[5], (SAMPLES,), 1, TXT + 1), jax.random.fold_in(arg_keys[5], 1), 1, TXT).astype(jnp.int32)
    image_projection_weight = centred(arg_keys[6], (MODEL_WIDTH, QUERY_KEY_VALUE), MODEL_WIDTH ** -0.5, 0.109375, ((1, 2),))
    text_projection_weight = centred(arg_keys[7], (MODEL_WIDTH, KV), MODEL_WIDTH ** -0.5, 0.109375, ((1, 2),))
    modulation_weight = centred(arg_keys[8], (EMB, 4 * MODEL_WIDTH), EMB ** -0.5, 0.375, ((1, 2),))
    query_key_norm_gain = jnp.clip(1.0 + 0.1 * jax.random.normal(arg_keys[9], (3, HD), jnp.float32), 0.5, 1.5)
    adapter_down_weight = centred(arg_keys[10], (MODEL_WIDTH, ADAPTER_RANK), MODEL_WIDTH ** -0.5, 0.109375)
    adapter_up_weight = centred(arg_keys[11], (ADAPTER_RANK, QUERY_KEY_VALUE), ADAPTER_RANK ** -0.5, 0.75, ((1, 2),))
    return {"image": image, "noise": noise, "text": text, "timestep": timestep, "guidance": guidance, "text_token_length": text_token_length, "image_projection_weight": image_projection_weight, "text_projection_weight": text_projection_weight, "modulation_weight": modulation_weight, "query_key_norm_gain": query_key_norm_gain, "adapter_down_weight": adapter_down_weight, "adapter_up_weight": adapter_up_weight}


def timing(value):
    count = EMB // 4
    freqs = jnp.exp(-math.log(10000.0) * jnp.arange(count, dtype=jnp.float32) / count)
    angles = 1000.0 * value * freqs
    return jnp.concatenate([jnp.cos(angles), jnp.sin(angles)])

def modulate(tokens, shift, scale):
    values = tokens.astype(jnp.float32)
    center = values - lax.optimization_barrier(jnp.mean(values, axis=1, keepdims=True))
    spread = lax.optimization_barrier(jnp.mean(center * center, axis=1, keepdims=True))
    return (center * lax.rsqrt(spread + 1e-06) * (1.0 + scale) + shift).astype(jnp.bfloat16)

def headnorm(vector, gain):
    return vector * lax.rsqrt(lax.optimization_barrier(jnp.mean(vector * vector, axis=-1, keepdims=True)) + 1e-06) * gain

def attend(kv_txt, qkv_img, query_key_norm_gain, keep):
    count = qkv_img.shape[1] // (3 * HD)
    img = qkv_img.reshape(qkv_img.shape[0], count, 3, HD)
    txt = kv_txt.reshape(kv_txt.shape[0], count, 2, HD)
    queries = headnorm(img[:, :, 0], query_key_norm_gain[0]).astype(jnp.bfloat16)
    keys = jnp.concatenate([headnorm(txt[:, :, 0], query_key_norm_gain[2]), headnorm(img[:, :, 1], query_key_norm_gain[1])], 0).astype(jnp.bfloat16)
    values = jnp.concatenate([txt[:, :, 1], img[:, :, 2]], 0).astype(jnp.bfloat16)
    scores = jnp.einsum('qhd,khd->hqk', queries.astype(jnp.float32), keys.astype(jnp.float32)) / math.sqrt(HD)
    scores = jnp.where(keep[None, None, :], scores, -1000000000.0)
    weights = jnp.exp(scores)
    probs = (weights / lax.optimization_barrier(jnp.sum(weights, axis=2, keepdims=True))).astype(jnp.bfloat16)
    out = jnp.einsum('hqk,khd->qhd', probs.astype(jnp.float32), values.astype(jnp.float32))
    return out.reshape(out.shape[0], count * HD)

def reference(image, noise, text, timestep, guidance, text_token_length, image_projection_weight, text_projection_weight, modulation_weight, query_key_norm_gain, adapter_down_weight, adapter_up_weight):

    def sample_terms(index):
        sigma = (timestep[index].astype(jnp.float32) + 1.0) / STEPS
        start = timing(sigma)
        emb_t = jax.nn.silu(jnp.concatenate([start, timing(guidance[index])])).astype(jnp.bfloat16)
        emb_s = jax.nn.silu(jnp.concatenate([start, jnp.zeros((EMB // 2,), jnp.float32)])).astype(jnp.bfloat16)
        mod_t = jnp.dot(emb_t[None], modulation_weight, preferred_element_type=jnp.float32)[0]
        mod_s = jnp.dot(emb_s[None], modulation_weight, preferred_element_type=jnp.float32)[0]
        noisy = ((1.0 - sigma) * image[index].astype(jnp.float32) + sigma * noise[index].astype(jnp.float32)).astype(jnp.bfloat16)
        words = text[index]
        h_img_t = modulate(noisy, mod_t[:MODEL_WIDTH], mod_t[MODEL_WIDTH:2 * MODEL_WIDTH])
        h_txt_t = modulate(words, mod_t[2 * MODEL_WIDTH:3 * MODEL_WIDTH], mod_t[3 * MODEL_WIDTH:])
        student_image_hidden = modulate(noisy, mod_s[:MODEL_WIDTH], mod_s[MODEL_WIDTH:2 * MODEL_WIDTH])
        h_txt_s = modulate(words, mod_s[2 * MODEL_WIDTH:3 * MODEL_WIDTH], mod_s[3 * MODEL_WIDTH:])
        adapter_output = jnp.dot(student_image_hidden, adapter_down_weight, preferred_element_type=jnp.float32).astype(jnp.bfloat16)
        qkv_t = jnp.dot(h_img_t, image_projection_weight, preferred_element_type=jnp.float32)
        student_query_key_value = jnp.dot(student_image_hidden, image_projection_weight, preferred_element_type=jnp.float32) + jnp.dot(adapter_output, adapter_up_weight, preferred_element_type=jnp.float32)
        kv_t = jnp.dot(h_txt_t, text_projection_weight, preferred_element_type=jnp.float32)
        kv_s = jnp.dot(h_txt_s, text_projection_weight, preferred_element_type=jnp.float32)
        position = jnp.arange(TXT + IMG, dtype=jnp.int32)
        keep = jnp.logical_or(position >= TXT, position < text_token_length[index])
        target = attend(kv_t, qkv_t, query_key_norm_gain, keep).astype(jnp.bfloat16)
        student, pull = jax.vjp(lambda inner: attend(kv_s, inner, query_key_norm_gain, keep), student_query_key_value)
        diff = student - target.astype(jnp.float32)
        loss_part = jnp.sum(diff * diff) / SAMPLES
        query_key_value_gradient, = pull(2.0 * diff / SAMPLES)
        query_key_value_gradient = query_key_value_gradient.astype(jnp.bfloat16)
        grad_b = jnp.dot(adapter_output.T, query_key_value_gradient, preferred_element_type=jnp.float32)
        adapter_gradient = jnp.dot(query_key_value_gradient, adapter_up_weight.T, preferred_element_type=jnp.float32)
        grad_a = jnp.dot(student_image_hidden.astype(jnp.float32).T, adapter_gradient, precision=lax.Precision.HIGHEST)
        return (grad_a, grad_b, loss_part)
    grads_a, grads_b, losses = lax.map(sample_terms, jnp.arange(SAMPLES, dtype=jnp.int32))
    grad_a = lax.optimization_barrier(jnp.sum(grads_a, axis=0))
    grad_b = lax.optimization_barrier(jnp.sum(grads_b, axis=0))
    loss_mean = jnp.sum(losses) / (IMG * HEADS * HD)
    direction_a = grad_a / jnp.sqrt(jnp.mean(grad_a * grad_a) + 1e-06)
    direction_b = grad_b / jnp.sqrt(jnp.mean(grad_b * grad_b) + 1e-06)
    return (direction_a, direction_b, loss_mean)
```

```python
import functools
import math

import jax
import jax.numpy as jnp
from jax import lax
from jax.experimental import pallas as pl
from jax.experimental.pallas import tpu as pltpu
from jax.sharding import PartitionSpec as P

HD = 128
HEADS = 16
STEPS = 1000
EPS = 1e-06
F32 = jnp.float32
BF16 = jnp.bfloat16
ROOT = 1.0 / math.sqrt(HD)


def timing(value, width):
    count = width // 4
    freqs = jnp.exp(-math.log(10000.0) * jnp.arange(count, dtype=F32) / count)
    angles = 1000.0 * value * freqs
    return jnp.concatenate([jnp.cos(angles), jnp.sin(angles)])


def nn(a, b):
    return lax.dot_general(a, b, (((1,), (0,)), ((), ())), preferred_element_type=F32)


def nt(a, b):
    return lax.dot_general(a, b, (((1,), (1,)), ((), ())), preferred_element_type=F32)


def tn(a, b):
    return lax.dot_general(a, b, (((0,), (0,)), ((), ())), preferred_element_type=F32)


def over(total, size, body):
    if total == size:
        body(0)
    else:

        @pl.loop(0, total // size)
        def _(i):
            body(pl.multiple_of(i * size, size))


def inverse_rms(x):
    return lax.rsqrt(jnp.mean(x * x, axis=-1, keepdims=True) + EPS)


def norm_pull(x, gain, dy):
    r = inverse_rms(x)
    u = gain * dy
    return r * (u - x * (r * r * jnp.mean(x * u, axis=-1, keepdims=True)))


def middle_kernel(
    n, steps, pair, samples, where_ref, mod_ref, bias_ref, gain_ref, down_ref, up_ref, wi_ref, wt_ref, *refs
):
    noisy, text = refs[:n], refs[n : 2 * n]
    send_a, keep_a, send_b, keep_b, loss_ref = refs[2 * n : 2 * n + 5]
    hi, ht, low, lowt, glt, qkv, kv, q_s, k_s, v_s, dk_s, dv_s, gq, whole = refs[2 * n + 5 :]
    step = pl.program_id(0)
    core = where_ref[0]
    img_part, txt_part = noisy[0].shape[0], text[0].shape[0]
    rows, trows = n * img_part, n * txt_part
    block = min(rows, 160)
    grp_rows = send_a.shape[1]

    def modulated(parts, dest, size, total, base):
        for k in range(n):

            @pl.loop(0, size // 16)
            def _(i, k=k):
                v = parts[k][pl.ds(pl.multiple_of(i * 16, 16), 16), :].astype(F32)
                center = v - jnp.mean(v, axis=1, keepdims=True)
                spread = jnp.mean(center * center, axis=1, keepdims=True)
                unit = center * lax.rsqrt(spread + EPS)
                for m in range(2):
                    row = 4 * m + base
                    h = unit * (1.0 + mod_ref[row + 1 : row + 2, :]) + mod_ref[row : row + 1, :]
                    at = pl.multiple_of(m * total + k * size + i * 16, 16)
                    dest[pl.ds(at, 16), :] = h.astype(BF16)

    @pl.when(step == 0)
    def _():
        modulated(noisy, hi, img_part, rows, 0)
        modulated(text, ht, txt_part, trows, 2)

        def adapter(start):
            low[pl.ds(start, block), :] = nn(hi[pl.ds(rows + start, block), :], down_ref[...]).astype(BF16)

        over(rows, block, adapter)
        lowt[...] = low[...].astype(F32).T.astype(BF16)
        glt[...] = jnp.zeros_like(glt)
        loss_ref[...] = jnp.zeros_like(loss_ref)

    def project_image(start):
        qkv[pl.ds(start, 2 * block), :] = nn(hi[pl.ds(start, 2 * block), :], wi_ref[...])

    def project_text(start):
        size = min(2 * trows, 192)
        kv[pl.ds(start, size), :] = nn(ht[pl.ds(start, size), :], wt_ref[...])

    def add_adapter(start):
        at = pl.ds(rows + start, block)
        qkv[at, :] = qkv[at, :] + nn(low[pl.ds(start, block), :], up_ref[...])

    over(2 * rows, 2 * block, project_image)
    over(2 * trows, min(2 * trows, 192), project_text)
    over(rows, block, add_adapter)

    gain_q, gain_k, gain_t = gain_ref[0:1, :], gain_ref[1:2, :], gain_ref[2:3, :]
    for j in range(pair):
        ic, tc = j * 3 * HD, j * 2 * HD
        for m in range(2):
            slot = 2 * j + m

            def image_part(start, m=m, slot=slot):
                src = pl.ds(m * rows + start, block)
                dst = pl.ds(start, block)
                q = qkv[src, ic : ic + HD]
                k = qkv[src, ic + HD : ic + 2 * HD]
                q_s[slot, dst, :] = (q * inverse_rms(q) * gain_q).astype(BF16)
                k_s[slot, dst, :] = (k * inverse_rms(k) * gain_k).astype(BF16)
                v_s[slot, dst, :] = qkv[src, ic + 2 * HD : ic + 3 * HD].astype(BF16)

            def text_part(start, m=m, slot=slot):
                size = min(trows, 96)
                src = pl.ds(m * trows + start, size)
                dst = pl.ds(rows + start, size)
                k = kv[src, tc : tc + HD]
                k_s[slot, dst, :] = (k * inverse_rms(k) * gain_t).astype(BF16)
                v_s[slot, dst, :] = kv[src, tc + HD : tc + 2 * HD].astype(BF16)

            over(rows, block, image_part)
            over(trows, min(trows, 96), text_part)

        teacher, student = 2 * j, 2 * j + 1
        if rows > block:
            dk_s[j] = jnp.zeros(dk_s.shape[1:], F32)
            dv_s[j] = jnp.zeros(dv_s.shape[1:], F32)

        def attend(start, j=j, ic=ic, teacher=teacher, student=student):
            at = pl.ds(start, block)

            def forward(slot):
                scores = nt(q_s[slot, at, :], k_s[slot]) * ROOT + bias_ref[...]
                weights = jnp.exp(scores)
                probs = weights * (1.0 / jnp.sum(weights, axis=1, keepdims=True))
                rounded = probs.astype(BF16)
                return probs, rounded, nn(rounded, v_s[slot])

            _, _, target = forward(teacher)
            probs, rounded, out = forward(student)
            diff = out - target.astype(BF16).astype(F32)
            loss_ref[...] += jnp.sum((diff * diff).reshape(block // 8, 8, HD), axis=0)
            dout = (diff * (2.0 / samples)).astype(BF16)
            dprobs = nt(dout, v_s[student]).astype(BF16).astype(F32)
            dscores = probs * (dprobs - jnp.sum(dprobs * probs, axis=1, keepdims=True))
            dscores = (dscores * ROOT).astype(BF16)
            dq = nn(dscores, k_s[student]).astype(BF16).astype(F32)
            q = qkv[pl.ds(rows + start, block), ic : ic + HD]
            gq[at, ic : ic + HD] = norm_pull(q, gain_q, dq).astype(BF16)
            dk = tn(dscores, q_s[student, at, :])[:rows]
            dv = tn(rounded, dout)[:rows]
            if rows > block:
                dk_s[j] += dk
                dv_s[j] += dv
            else:
                dk_s[j] = dk
                dv_s[j] = dv

        over(rows, block, attend)

        def finish(start, j=j, ic=ic):
            at = pl.ds(start, block)
            k = qkv[pl.ds(rows + start, block), ic + HD : ic + 2 * HD]
            dk = dk_s[j, at, :].astype(BF16).astype(F32)
            gq[at, ic + HD : ic + 2 * HD] = norm_pull(k, gain_k, dk).astype(BF16)
            gq[at, ic + 2 * HD : ic + 3 * HD] = dv_s[j, at, :].astype(BF16)

        over(rows, block, finish)

    def share(value, columns, send, keep):
        whole[:, columns] = value
        for x in range(2):
            keep[x] = whole[pl.ds(pl.multiple_of((2 * x + core) * grp_rows, 8), grp_rows), columns]
            send[x] = whole[pl.ds(pl.multiple_of((2 * x + 1 - core) * grp_rows, 8), grp_rows), columns]

    share(nn(lowt[...], gq[...]), slice(0, gq.shape[1]), send_b, keep_b)
    glt[...] += nt(up_ref[...], gq[...])

    @pl.when(step == steps - 1)
    def _():
        g = glt[...]
        g1 = g.astype(BF16)
        rest = g - g1.astype(F32)
        g2 = rest.astype(BF16)
        g3 = (rest - g2.astype(F32)).astype(BF16)
        stack = jnp.concatenate([g1, g2, g3], 0)
        rank = g.shape[0]
        full = nn(stack, hi[rows : 2 * rows, :])
        share(
            full[:rank] + full[rank : 2 * rank] + full[2 * rank :],
            slice(0, full.shape[1]),
            send_a,
            keep_a,
        )


def middle(n, where, mod, bias, gain, down, up, wi, wt, noisy, text):
    rank, img_cols = up.shape
    width = wi.shape[0]
    count = img_cols // (3 * HD)
    pair = 2 if count % 2 == 0 else 1
    steps = count // pair
    rows, trows = n * noisy[0].shape[0], n * text[0].shape[0]
    groups = rank // 4
    samples = lax.axis_size("grp") * lax.axis_size("dp")
    ic, tc = pair * 3 * HD, pair * 2 * HD

    def fixed(x):
        return pl.BlockSpec(x.shape, lambda s: (0,) * x.ndim, pipeline_mode=pl.Buffered(1))

    def columns(height, cols):
        if steps == 1:
            return pl.BlockSpec((height, cols), lambda s: (0, s), pipeline_mode=pl.Buffered(1))
        return pl.BlockSpec((height, cols), lambda s: (0, s))

    out_a = jax.ShapeDtypeStruct((2, groups, width), F32)
    out_b = jax.ShapeDtypeStruct((2, groups, img_cols), F32)
    spec_a = pl.BlockSpec(out_a.shape, lambda s: (0, 0, 0))
    spec_b = pl.BlockSpec((2, groups, ic), lambda s: (0, 0, s))
    flops = 4 * rows * width * img_cols + 4 * trows * width * wt.shape[1]
    return pl.pallas_call(
        functools.partial(middle_kernel, n, steps, pair, samples),
        grid=(steps,),
        in_specs=[pl.BlockSpec(memory_space=pltpu.SMEM)]
        + [fixed(mod), fixed(bias), fixed(gain), fixed(down)]
        + [columns(rank, ic), columns(width, ic), columns(width, tc)]
        + [fixed(x) for x in (*noisy, *text)],
        out_specs=[spec_a, spec_a, spec_b, spec_b, pl.BlockSpec((8, HD), lambda s: (0, 0))],
        out_shape=[out_a, out_a, out_b, out_b, jax.ShapeDtypeStruct((8, HD), F32)],
        scratch_shapes=[
            pltpu.VMEM((2 * rows, width), BF16),
            pltpu.VMEM((2 * trows, width), BF16),
            pltpu.VMEM((rows, rank), BF16),
            pltpu.VMEM((rank, rows), BF16),
            pltpu.VMEM((rank, rows), F32),
            pltpu.VMEM((2 * rows, ic), F32),
            pltpu.VMEM((2 * trows, tc), F32),
            pltpu.VMEM((2 * pair, rows, HD), BF16),
            pltpu.VMEM((2 * pair, rows + trows, HD), BF16),
            pltpu.VMEM((2 * pair, rows + trows, HD), BF16),
            pltpu.VMEM((pair, rows, HD), F32),
            pltpu.VMEM((pair, rows, HD), F32),
            pltpu.VMEM((rows, ic), BF16),
            pltpu.VMEM((rank, max(width, ic)), F32),
        ],
        compiler_params=pltpu.CompilerParams(
            dimension_semantics=("arbitrary",), vmem_limit_bytes=58 * 1024 * 1024
        ),
        cost_estimate=pl.CostEstimate(
            flops=flops,
            bytes_accessed=2 * (wi.size + wt.size),
            transcendentals=2 * count * rows * (rows + trows),
        ),
        name="middle",
    )(where, mod, bias, gain, down, up, wi, wt, *noisy, *text)


def swap(x, bit):
    size = lax.axis_size("grp")
    return lax.ppermute(x, "grp", [(i, i ^ bit) for i in range(size)])


def shifted(x, axis, k):
    size = lax.axis_size(axis)
    return lax.ppermute(x, axis, [(i, (i + k) % size) for i in range(size)])


def scatter_sum(x, axis, dim):
    size, me = lax.axis_size(axis), lax.axis_index(axis)
    each = x.shape[dim] // size
    block = lambda k: lax.dynamic_slice_in_dim(x, lax.rem(me + k, size) * each, each, dim)
    total = block(0)
    for k in range(1, size):
        total = total + shifted(block(k), axis, k)
    return total


def half_sum(x, bit):
    side = lax.div(lax.axis_index("grp"), bit)
    keep = lax.dynamic_index_in_dim(x, side, 0, keepdims=False)
    send = lax.dynamic_index_in_dim(x, 1 - side, 0, keepdims=False)
    return keep + swap(send, bit)


def pieces(value):
    first = lax.reduce_precision(value, 8, 7)
    second = lax.reduce_precision(value - first, 8, 7)
    return [first, second, value - first - second]


def on_device(
    image,
    noise,
    text,
    timestep,
    guidance,
    text_token_length,
    image_projection_weight,
    text_projection_weight,
    modulation_weight,
    query_key_norm_gain,
    adapter_down_weight,
    adapter_up_weight,
):
    width = image.shape[2]
    emb_width = modulation_weight.shape[0]
    n, me = lax.axis_size("seq"), lax.axis_index("seq")
    samples = lax.axis_size("grp") * lax.axis_size("dp")
    sigma = (timestep[0].astype(F32) + 1.0) / STEPS
    start = timing(sigma, emb_width)
    emb = jnp.stack(
        [
            jnp.concatenate([start, timing(guidance[0], emb_width)]),
            jnp.concatenate([start, jnp.zeros((emb_width // 2,), F32)]),
        ]
    )
    emb = jax.nn.silu(emb).astype(BF16)
    part = jnp.dot(emb, modulation_weight, preferred_element_type=F32)
    mods = [part] + [shifted(part, "seq", k) for k in range(1, n)]
    noisy = ((1.0 - sigma) * image[0].astype(F32) + sigma * noise[0].astype(F32)).astype(BF16)
    noisy_parts = [noisy] + [shifted(noisy, "seq", k) for k in range(1, n)]
    words = text[0]
    text_parts = [words] + [shifted(words, "seq", k) for k in range(1, n)]
    origin = [lax.rem(me + n - k, n) for k in range(n)]
    ordered = [
        functools.reduce(
            lambda so_far, k: jnp.where(origin[k] == j, mods[k], so_far), range(1, n), mods[0]
        )
        for j in range(n)
    ]
    mod = jnp.concatenate(ordered, 1).reshape(8, width)
    img_part, txt_part = noisy.shape[0], words.shape[0]
    place = jnp.concatenate(
        [jnp.zeros((n * img_part,), jnp.int32)]
        + [origin[k] * txt_part + jnp.arange(txt_part, dtype=jnp.int32) for k in range(n)]
    )
    bias = jnp.where(place < text_token_length[0], 0.0, -1000000000.0).astype(F32)[None]
    core = lax.rem(lax.axis_index("grp"), 2).astype(jnp.int32)
    send_a, keep_a, send_b, keep_b, loss = middle(
        n,
        core[None],
        mod,
        bias,
        query_key_norm_gain,
        adapter_down_weight,
        adapter_up_weight,
        image_projection_weight,
        text_projection_weight,
        noisy_parts,
        text_parts,
    )
    sum_a = keep_a + swap(send_a, 1)
    sum_b = keep_b + swap(send_b, 1)
    sum_a = scatter_sum(sum_a, "seq", 1)
    sum_b = half_sum(sum_b, 2)
    sum_a = half_sum(sum_a, 2)
    sum_b = scatter_sum(sum_b, "dp", 1)
    sum_a = scatter_sum(sum_a, "dp", 1)
    scalars = jnp.stack(pieces(jnp.sum(loss)) + pieces(jnp.sum(sum_b * sum_b)))
    extra = jnp.broadcast_to(jnp.pad(scalars, (0, HD - 6))[None], (sum_a.shape[0], HD))
    all_a = lax.all_gather(
        jnp.concatenate([sum_a, extra], 1).astype(BF16), ("grp", "seq", "dp")
    ).astype(F32)
    all_b = lax.all_gather(sum_b.astype(BF16), ("grp", "dp")).astype(F32)
    grps, dps = lax.axis_size("grp"), lax.axis_size("dp")
    scalars = jnp.sum(all_a[:, 0, -HD:], 0)
    loss_mean = jnp.sum(scalars[:3]) / samples / (n * img_part * HEADS * HD)
    squares_b = jnp.sum(scalars[3:6])
    grad_a = all_a[:, :, :-HD].reshape(grps * n, dps, sum_a.shape[0], sum_a.shape[1])
    grad_a = grad_a.transpose(1, 3, 0, 2).reshape(width, -1)
    grad_b = all_b.reshape(grps, dps, *sum_b.shape).transpose(0, 2, 1, 3)
    grad_b = grad_b.reshape(adapter_up_weight.shape)
    direction_a = grad_a * lax.rsqrt(jnp.mean(grad_a * grad_a) + EPS)
    direction_b = grad_b * lax.rsqrt(squares_b / (grad_b.size * n) + EPS)
    return (direction_a, direction_b, loss_mean)


def solution(mesh):
    in_specs = (
        P(("grp", "dp"), "seq", None),
        P(("grp", "dp"), "seq", None),
        P(("grp", "dp"), "seq", None),
        P(("grp", "dp")),
        P(("grp", "dp")),
        P(("grp", "dp")),
        P(None, "seq"),
        P(None, "seq"),
        P(None, "seq"),
        P(),
        P(),
        P(None, "seq"),
    )
    out_specs = (P(), P(None, "seq"), P())
    return jax.shard_map(
        on_device, mesh=mesh, in_specs=in_specs, out_specs=out_specs, check_vma=False
    )
```

```python
import functools
import math

import jax
import jax.numpy as jnp
from jax import lax
from jax.experimental import pallas as pl
from jax.experimental.pallas import tpu as pltpu
from jax.sharding import PartitionSpec as P

HD = 128
HEADS = 16
STEPS = 1000
EPS = 1e-06
F32 = jnp.float32
BF16 = jnp.bfloat16
ROOT = 1.0 / math.sqrt(HD)


def timing(value, width):
    count = width // 4
    freqs = jnp.exp(-math.log(10000.0) * jnp.arange(count, dtype=F32) / count)
    angles = 1000.0 * value * freqs
    return jnp.concatenate([jnp.cos(angles), jnp.sin(angles)])


def nn(a, b):
    return lax.dot_general(a, b, (((1,), (0,)), ((), ())), preferred_element_type=F32)


def nt(a, b):
    return lax.dot_general(a, b, (((1,), (1,)), ((), ())), preferred_element_type=F32)


def tn(a, b):
    return lax.dot_general(a, b, (((0,), (0,)), ((), ())), preferred_element_type=F32)


def over(total, size, body):
    if total == size:
        body(0)
    else:

        @pl.loop(0, total // size)
        def _(i):
            body(pl.multiple_of(i * size, size))


def inverse_rms(x):
    return lax.rsqrt(jnp.mean(x * x, axis=-1, keepdims=True) + EPS)


def norm_pull(x, gain, dy):
    r = inverse_rms(x)
    u = gain * dy
    return r * (u - x * (r * r * jnp.mean(x * u, axis=-1, keepdims=True)))


def middle_kernel(
    n, steps, pair, samples, where_ref, mod_ref, bias_ref, gain_ref, down_ref, up_ref, wi_ref, wt_ref, *refs
):
    noisy, text = refs[:n], refs[n : 2 * n]
    send_a, keep_a, send_b, keep_b, loss_ref = refs[2 * n : 2 * n + 5]
    hi, ht, low, lowt, glt, qkv, kv, q_s, k_s, v_s, dk_s, dv_s, gq, whole = refs[2 * n + 5 :]
    step = pl.program_id(0)
    core = where_ref[0]
    img_part, txt_part = noisy[0].shape[0], text[0].shape[0]
    rows, trows = n * img_part, n * txt_part
    block = min(rows, 160)
    half = send_a.shape[0]

    def modulated(parts, dest, size, total, base):
        for k in range(n):

            @pl.loop(0, size // 16)
            def _(i, k=k):
                v = parts[k][pl.ds(pl.multiple_of(i * 16, 16), 16), :].astype(F32)
                center = v - jnp.mean(v, axis=1, keepdims=True)
                spread = jnp.mean(center * center, axis=1, keepdims=True)
                unit = center * lax.rsqrt(spread + EPS)
                for m in range(2):
                    row = 4 * m + base
                    h = unit * (1.0 + mod_ref[row + 1 : row + 2, :]) + mod_ref[row : row + 1, :]
                    at = pl.multiple_of(m * total + k * size + i * 16, 16)
                    dest[pl.ds(at, 16), :] = h.astype(BF16)

    @pl.when(step == 0)
    def _():
        modulated(noisy, hi, img_part, rows, 0)
        modulated(text, ht, txt_part, trows, 2)

        def adapter(start):
            low[pl.ds(start, block), :] = nn(hi[pl.ds(rows + start, block), :], down_ref[...]).astype(BF16)

        over(rows, block, adapter)
        lowt[...] = low[...].astype(F32).T.astype(BF16)
        glt[...] = jnp.zeros_like(glt)
        loss_ref[...] = jnp.zeros_like(loss_ref)

    def project_image(start):
        qkv[pl.ds(start, 2 * block), :] = nn(hi[pl.ds(start, 2 * block), :], wi_ref[...])

    def project_text(start):
        size = min(2 * trows, 192)
        kv[pl.ds(start, size), :] = nn(ht[pl.ds(start, size), :], wt_ref[...])

    def add_adapter(start):
        at = pl.ds(rows + start, block)
        qkv[at, :] = qkv[at, :] + nn(low[pl.ds(start, block), :], up_ref[...])

    over(2 * rows, 2 * block, project_image)
    over(2 * trows, min(2 * trows, 192), project_text)
    over(rows, block, add_adapter)

    gain_q, gain_k, gain_t = gain_ref[0:1, :], gain_ref[1:2, :], gain_ref[2:3, :]
    for j in range(pair):
        ic, tc = j * 3 * HD, j * 2 * HD
        for m in range(2):
            slot = 2 * j + m

            def image_part(start, m=m, slot=slot):
                src = pl.ds(m * rows + start, block)
                dst = pl.ds(start, block)
                q = qkv[src, ic : ic + HD]
                k = qkv[src, ic + HD : ic + 2 * HD]
                q_s[slot, dst, :] = (q * inverse_rms(q) * gain_q).astype(BF16)
                k_s[slot, dst, :] = (k * inverse_rms(k) * gain_k).astype(BF16)
                v_s[slot, dst, :] = qkv[src, ic + 2 * HD : ic + 3 * HD].astype(BF16)

            def text_part(start, m=m, slot=slot):
                size = min(trows, 96)
                src = pl.ds(m * trows + start, size)
                dst = pl.ds(rows + start, size)
                k = kv[src, tc : tc + HD]
                k_s[slot, dst, :] = (k * inverse_rms(k) * gain_t).astype(BF16)
                v_s[slot, dst, :] = kv[src, tc + HD : tc + 2 * HD].astype(BF16)

            over(rows, block, image_part)
            over(trows, min(trows, 96), text_part)

        teacher, student = 2 * j, 2 * j + 1
        if rows > block:
            dk_s[j] = jnp.zeros(dk_s.shape[1:], F32)
            dv_s[j] = jnp.zeros(dv_s.shape[1:], F32)

        def attend(start, j=j, ic=ic, teacher=teacher, student=student):
            at = pl.ds(start, block)

            def forward(slot):
                scores = nt(q_s[slot, at, :], k_s[slot]) * ROOT + bias_ref[...]
                weights = jnp.exp(scores)
                probs = weights * (1.0 / jnp.sum(weights, axis=1, keepdims=True))
                rounded = probs.astype(BF16)
                return probs, rounded, nn(rounded, v_s[slot])

            _, _, target = forward(teacher)
            probs, rounded, out = forward(student)
            diff = out - target.astype(BF16).astype(F32)
            loss_ref[...] += jnp.sum((diff * diff).reshape(block // 8, 8, HD), axis=0)
            dout = (diff * (2.0 / samples)).astype(BF16)
            dprobs = nt(dout, v_s[student]).astype(BF16).astype(F32)
            dscores = probs * (dprobs - jnp.sum(dprobs * probs, axis=1, keepdims=True))
            dscores = (dscores * ROOT).astype(BF16)
            dq = nn(dscores, k_s[student]).astype(BF16).astype(F32)
            q = qkv[pl.ds(rows + start, block), ic : ic + HD]
            gq[at, ic : ic + HD] = norm_pull(q, gain_q, dq).astype(BF16)
            dk = tn(dscores, q_s[student, at, :])[:rows]
            dv = tn(rounded, dout)[:rows]
            if rows > block:
                dk_s[j] += dk
                dv_s[j] += dv
            else:
                dk_s[j] = dk
                dv_s[j] = dv

        over(rows, block, attend)

        def finish(start, j=j, ic=ic):
            at = pl.ds(start, block)
            k = qkv[pl.ds(rows + start, block), ic + HD : ic + 2 * HD]
            dk = dk_s[j, at, :].astype(BF16).astype(F32)
            gq[at, ic + HD : ic + 2 * HD] = norm_pull(k, gain_k, dk).astype(BF16)
            gq[at, ic + 2 * HD : ic + 3 * HD] = dv_s[j, at, :].astype(BF16)

        over(rows, block, finish)

    def share(value, columns, send, keep):
        whole[:, columns] = value
        keep[...] = whole[pl.ds(pl.multiple_of(core * half, 8), half), columns]
        send[...] = whole[pl.ds(pl.multiple_of((1 - core) * half, 8), half), columns].astype(send.dtype)

    share(nn(lowt[...], gq[...]), slice(0, gq.shape[1]), send_b, keep_b)
    glt[...] += nt(up_ref[...], gq[...])

    @pl.when(step == steps - 1)
    def _():
        g = glt[...]
        g1 = g.astype(BF16)
        rest = g - g1.astype(F32)
        g2 = rest.astype(BF16)
        g3 = (rest - g2.astype(F32)).astype(BF16)
        stack = jnp.concatenate([g1, g2, g3], 0)
        rank = g.shape[0]
        full = nn(stack, hi[rows : 2 * rows, :])
        share(
            full[:rank] + full[rank : 2 * rank] + full[2 * rank :],
            slice(0, full.shape[1]),
            send_a,
            keep_a,
        )


def middle(n, where, mod, bias, gain, down, up, wi, wt, noisy, text):
    rank, img_cols = up.shape
    width = wi.shape[0]
    count = img_cols // (3 * HD)
    pair = 2 if count % 2 == 0 else 1
    steps = count // pair
    rows, trows = n * noisy[0].shape[0], n * text[0].shape[0]
    half = rank // 2
    samples = lax.axis_size("grp") * lax.axis_size("dp")
    ic, tc = pair * 3 * HD, pair * 2 * HD

    def fixed(x):
        return pl.BlockSpec(x.shape, lambda s: (0,) * x.ndim, pipeline_mode=pl.Buffered(1))

    def columns(height, cols):
        if steps == 1:
            return pl.BlockSpec((height, cols), lambda s: (0, s), pipeline_mode=pl.Buffered(1))
        return pl.BlockSpec((height, cols), lambda s: (0, s))

    out_a, out_b = (half, width), (half, img_cols)
    spec_a = pl.BlockSpec(out_a, lambda s: (0, 0))
    spec_b = pl.BlockSpec((half, ic), lambda s: (0, s))
    flops = 4 * rows * width * img_cols + 4 * trows * width * wt.shape[1]
    return pl.pallas_call(
        functools.partial(middle_kernel, n, steps, pair, samples),
        grid=(steps,),
        in_specs=[pl.BlockSpec(memory_space=pltpu.SMEM)]
        + [fixed(mod), fixed(bias), fixed(gain), fixed(down)]
        + [columns(rank, ic), columns(width, ic), columns(width, tc)]
        + [fixed(x) for x in (*noisy, *text)],
        out_specs=[spec_a, spec_a, spec_b, spec_b, pl.BlockSpec((8, HD), lambda s: (0, 0))],
        out_shape=[
            jax.ShapeDtypeStruct(out_a, BF16),
            jax.ShapeDtypeStruct(out_a, F32),
            jax.ShapeDtypeStruct(out_b, BF16),
            jax.ShapeDtypeStruct(out_b, F32),
            jax.ShapeDtypeStruct((8, HD), F32),
        ],
        scratch_shapes=[
            pltpu.VMEM((2 * rows, width), BF16),
            pltpu.VMEM((2 * trows, width), BF16),
            pltpu.VMEM((rows, rank), BF16),
            pltpu.VMEM((rank, rows), BF16),
            pltpu.VMEM((rank, rows), F32),
            pltpu.VMEM((2 * rows, ic), F32),
            pltpu.VMEM((2 * trows, tc), F32),
            pltpu.VMEM((2 * pair, rows, HD), BF16),
            pltpu.VMEM((2 * pair, rows + trows, HD), BF16),
            pltpu.VMEM((2 * pair, rows + trows, HD), BF16),
            pltpu.VMEM((pair, rows, HD), F32),
            pltpu.VMEM((pair, rows, HD), F32),
            pltpu.VMEM((rows, ic), BF16),
            pltpu.VMEM((rank, max(width, ic)), F32),
        ],
        compiler_params=pltpu.CompilerParams(
            dimension_semantics=("arbitrary",), vmem_limit_bytes=58 * 1024 * 1024
        ),
        cost_estimate=pl.CostEstimate(
            flops=flops,
            bytes_accessed=2 * (wi.size + wt.size),
            transcendentals=2 * count * rows * (rows + trows),
        ),
        name="middle",
    )(where, mod, bias, gain, down, up, wi, wt, *noisy, *text)


def start_kernel(sigma_ref, image_ref, noise_ref, emb_ref, weight_ref, noisy_ref, part_ref):
    sigma = sigma_ref[0]
    clean, noise = image_ref[...].astype(F32), noise_ref[...].astype(F32)
    noisy_ref[...] = ((1.0 - sigma) * clean + sigma * noise).astype(BF16)
    part_ref[...] = nn(emb_ref[...], weight_ref[...])[: part_ref.shape[0]]


def start(sigma, image, noise, emb, weight):
    rows, width = image.shape
    depth, cols = weight.shape
    steps = 4 if width % 512 == 0 and cols % 512 == 0 else 1
    tokens = pl.BlockSpec((rows, width // steps), lambda s: (0, s))
    return pl.pallas_call(
        start_kernel,
        grid=(steps,),
        in_specs=[
            pl.BlockSpec(memory_space=pltpu.SMEM),
            tokens,
            tokens,
            pl.BlockSpec(emb.shape, lambda s: (0, 0)),
            pl.BlockSpec((depth, cols // steps), lambda s: (0, s)),
        ],
        out_specs=[tokens, pl.BlockSpec((2, cols // steps), lambda s: (0, s))],
        out_shape=[
            jax.ShapeDtypeStruct((rows, width), BF16),
            jax.ShapeDtypeStruct((2, cols), F32),
        ],
        compiler_params=pltpu.CompilerParams(
            dimension_semantics=("arbitrary",), vmem_limit_bytes=16 * 1024 * 1024
        ),
        cost_estimate=pl.CostEstimate(
            flops=4 * depth * cols, bytes_accessed=30_000_000, transcendentals=0
        ),
        name="start",
    )(sigma, image, noise, emb, weight)


def finish_kernel(scale_a, scale_b, scale_loss, a_ref, b_ref, sums_ref, out_a, out_b, loss_ref):
    half = HD // 2
    total = jnp.sum(sums_ref[...], axis=0, keepdims=True)
    loss_ref[...] = jnp.sum(total[:, :half], axis=1, keepdims=True) * scale_loss
    squares_b = jnp.sum(total[:, half:], axis=1, keepdims=True) * scale_b
    grad_a = a_ref[...].astype(F32)
    squares = jnp.sum(jnp.sum(grad_a * grad_a, axis=0, keepdims=True), axis=1, keepdims=True)
    unit_a = lax.rsqrt(squares * scale_a + EPS)
    out_b[...] = b_ref[...].astype(F32) * lax.rsqrt(squares_b + EPS)
    for c in range(0, a_ref.shape[1], HD):
        out_a[c : c + HD, :] = (a_ref[:, c : c + HD].astype(F32) * unit_a).T


def finish(grad_a, grad_b, sums, n, entries):
    (rank, width), cols = grad_a.shape, grad_b.shape[1]
    return pl.pallas_call(
        functools.partial(finish_kernel, 1.0 / (rank * width), 1.0 / (rank * cols * n), 1.0 / entries),
        out_shape=[
            jax.ShapeDtypeStruct((width, rank), F32),
            jax.ShapeDtypeStruct((rank, cols), F32),
            jax.ShapeDtypeStruct((1, 1), F32),
        ],
        name="finish",
    )(grad_a, grad_b, sums)


def shifted(x, axis, k):
    size = lax.axis_size(axis)
    return lax.ppermute(x, axis, [(i, (i + k) % size) for i in range(size)])


def side_of(axis, bit):
    return lax.rem(lax.div(lax.axis_index(axis), bit), 2)


def swap(arrays, axis, bit):
    pairs = [(i, i ^ bit) for i in range(lax.axis_size(axis))]
    if len(arrays) == 1 or any(x.shape[0] % 8 or x.shape[1] % HD for x in arrays):
        return [lax.ppermute(x, axis, pairs) for x in arrays]
    rows = [x[r : r + 8] for x in arrays for r in range(0, x.shape[0], 8)]
    got = lax.ppermute(jnp.concatenate(rows, 1), axis, pairs)
    out, at = [], 0
    for x in arrays:
        blocks = []
        for _ in range(0, x.shape[0], 8):
            blocks.append(got[:, at : at + x.shape[1]])
            at += x.shape[1]
        out.append(blocks[0] if len(blocks) == 1 else jnp.concatenate(blocks, 0))
    return out


def cut_of(x):
    if x.shape[0] % 16 == 0:
        return 0
    return 1 if x.shape[1] % (2 * HD) == 0 else 0


def halve(arrays, axis, bit, dtype):
    side = side_of(axis, bit)
    keep, send = [], []
    for x in arrays:
        dim = cut_of(x)
        first, second = jnp.split(x, 2, dim)
        keep.append(jnp.where(side == 0, first, second))
        send.append(jnp.where(side == 0, second, first).astype(dtype))
    got = swap(send, axis, bit)
    return [k + g.astype(F32) for k, g in zip(keep, got)]


def join(mine, theirs, side, dim):
    return jnp.concatenate(
        [jnp.where(side == 0, mine, theirs), jnp.where(side == 0, theirs, mine)], dim
    )


def pieces(value):
    first = lax.reduce_precision(value, 8, 7)
    rest = value - first
    second = lax.reduce_precision(rest, 8, 7)
    return jnp.concatenate([first, second, rest - second], 1).astype(BF16)


def rejoin(arrays, dims, sums, axis, bit):
    side = side_of(axis, bit)
    *got, other = swap([*arrays, pieces(sums)], axis, bit)
    other = other.astype(F32)
    sums = sums + (other[:, :HD] + other[:, HD : 2 * HD] + other[:, 2 * HD :])
    return [join(x, g, side, d) for x, g, d in zip(arrays, got, dims)], sums


def bits(axis):
    size = lax.axis_size(axis)
    return [1 << i for i in range(size.bit_length() - 1)]


def fold(x):
    half = HD // 2
    return functools.reduce(
        lambda total, c: total + x[:, c : c + half], range(half, x.shape[1], half), x[:, :half]
    )


def on_device(
    image,
    noise,
    text,
    timestep,
    guidance,
    text_token_length,
    image_projection_weight,
    text_projection_weight,
    modulation_weight,
    query_key_norm_gain,
    adapter_down_weight,
    adapter_up_weight,
):
    width = image.shape[2]
    emb_width = modulation_weight.shape[0]
    n, me = lax.axis_size("seq"), lax.axis_index("seq")
    samples = lax.axis_size("grp") * lax.axis_size("dp")
    sigma = (timestep[0].astype(F32) + 1.0) / STEPS
    time = timing(sigma, emb_width)
    emb = jnp.stack(
        [
            jnp.concatenate([time, timing(guidance[0], emb_width)]),
            jnp.concatenate([time, jnp.zeros((emb_width // 2,), F32)]),
        ]
    )
    emb = jnp.pad(jax.nn.silu(emb).astype(BF16), ((0, 14), (0, 0)))
    noisy, part = start(sigma[None], image[0], noise[0], emb, modulation_weight)
    mods = [part] + [shifted(part, "seq", k) for k in range(1, n)]
    noisy_parts = [noisy] + [shifted(noisy, "seq", k) for k in range(1, n)]
    words = text[0]
    text_parts = [words] + [shifted(words, "seq", k) for k in range(1, n)]
    origin = [lax.rem(me + n - k, n) for k in range(n)]
    ordered = [
        functools.reduce(
            lambda so_far, k: jnp.where(origin[k] == j, mods[k], so_far), range(1, n), mods[0]
        )
        for j in range(n)
    ]
    mod = jnp.concatenate(ordered, 1).reshape(8, width)
    img_part, txt_part = noisy.shape[0], words.shape[0]
    place = jnp.concatenate(
        [jnp.zeros((n * img_part,), jnp.int32)]
        + [origin[k] * txt_part + jnp.arange(txt_part, dtype=jnp.int32) for k in range(n)]
    )
    bias = jnp.where(place < text_token_length[0], 0.0, -1000000000.0).astype(F32)[None]
    core = lax.rem(lax.axis_index("grp"), 2).astype(jnp.int32)
    send_a, keep_a, send_b, keep_b, loss = middle(
        n,
        core[None],
        mod,
        bias,
        query_key_norm_gain,
        adapter_down_weight,
        adapter_up_weight,
        image_projection_weight,
        text_projection_weight,
        noisy_parts,
        text_parts,
    )
    (got_a,), (got_b,) = swap([send_a], "grp", 1), swap([send_b], "grp", 1)
    grad_a, grad_b = keep_a + got_a.astype(F32), keep_b + got_b.astype(F32)
    seq_dims, dp_dims = [], []
    for bit in reversed(bits("seq")):
        seq_dims.append(cut_of(grad_a))
        (grad_a,) = halve([grad_a], "seq", bit, BF16)
    x_dims = [cut_of(grad_a), cut_of(grad_b)]
    (grad_b,) = halve([grad_b], "grp", 2, BF16)
    (grad_a,) = halve([grad_a], "grp", 2, BF16)
    for bit in reversed(bits("dp")):
        dp_dims.append([cut_of(grad_a), cut_of(grad_b)])
        grad_a, grad_b = halve([grad_a, grad_b], "dp", bit, F32)
    squares = fold(grad_b * grad_b)
    squares = jnp.pad(squares, ((0, 8 - squares.shape[0]), (0, 0)))
    sums = jnp.concatenate([fold(loss), squares], 1)
    grads = [grad_a.astype(BF16), grad_b.astype(BF16)]
    for bit in bits("dp"):
        grads, sums = rejoin(grads, dp_dims.pop(), sums, "dp", bit)
    grads, sums = rejoin(grads, x_dims, sums, "grp", 2)
    for bit in bits("seq"):
        (grads[0],), sums = rejoin(grads[:1], [seq_dims.pop()], sums, "seq", bit)
    grads, sums = rejoin(grads, [0, 0], sums, "grp", 1)
    direction_a, direction_b, loss_mean = finish(
        *grads, sums, n, samples * n * img_part * HEADS * HD
    )
    return (direction_a, direction_b, loss_mean[0, 0])


def solution(mesh):
    in_specs = (
        P(("grp", "dp"), "seq", None),
        P(("grp", "dp"), "seq", None),
        P(("grp", "dp"), "seq", None),
        P(("grp", "dp")),
        P(("grp", "dp")),
        P(("grp", "dp")),
        P(None, "seq"),
        P(None, "seq"),
        P(None, "seq"),
        P(),
        P(),
        P(None, "seq"),
    )
    out_specs = (P(), P(None, "seq"), P())
    return jax.shard_map(
        on_device, mesh=mesh, in_specs=in_specs, out_specs=out_specs, check_vma=False
    )
```

```python
import functools
import math

import jax
import jax.numpy as jnp
from jax import lax
from jax.experimental import pallas as pl
from jax.experimental.pallas import tpu as pltpu
from jax.sharding import PartitionSpec as P

HD = 128
HEADS = 16
STEPS = 1000
EPS = 1e-06
F32 = jnp.float32
BF16 = jnp.bfloat16
ROOT = 1.0 / math.sqrt(HD)
LOG2E = 1.0 / math.log(2.0)


def timing(value, width):
    count = width // 4
    freqs = jnp.exp(-math.log(10000.0) * jnp.arange(count, dtype=F32) / count)
    angles = 1000.0 * value * freqs
    return jnp.concatenate([jnp.cos(angles), jnp.sin(angles)])


def nn(a, b):
    return lax.dot_general(a, b, (((1,), (0,)), ((), ())), preferred_element_type=F32)


def nt(a, b):
    return lax.dot_general(a, b, (((1,), (1,)), ((), ())), preferred_element_type=F32)


def tn(a, b):
    return lax.dot_general(a, b, (((0,), (0,)), ((), ())), preferred_element_type=F32)


def over(total, size, body):
    if total == size:
        body(0)
    else:

        @pl.loop(0, total // size)
        def _(i):
            body(pl.multiple_of(i * size, size))


def inverse_rms(x):
    return lax.rsqrt(jnp.mean(x * x, axis=-1, keepdims=True) + EPS)


def norm_pull(x, gain, dy):
    r = inverse_rms(x)
    u = gain * dy
    return r * (u - x * (r * r * jnp.mean(x * u, axis=-1, keepdims=True)))


def modulate(tokens, mod_ref, kind, width, dest, rows, base):
    size = tokens.shape[0]

    @pl.loop(0, size // 16)
    def _(i):
        v = tokens[pl.ds(pl.multiple_of(i * 16, 16), 16), :].astype(F32)
        center = v - jnp.mean(v, axis=1, keepdims=True)
        spread = jnp.mean(center * center, axis=1, keepdims=True)
        unit = center * lax.rsqrt(spread + EPS)
        for m in range(2):
            shift = mod_ref[m : m + 1, kind * width : (kind + 1) * width]
            scale = mod_ref[m : m + 1, (kind + 1) * width : (kind + 2) * width]
            at = pl.multiple_of(m * rows + base + i * 16, 16)
            dest[pl.ds(at, 16), :] = (unit * (1.0 + scale) + shift).astype(BF16)


def normed(x, gain):
    return (x * inverse_rms(x) * gain).astype(BF16)


def text_kernel(n, pair, mod_ref, gain_ref, w_ref, *refs):
    parts, (k_ref, v_ref, ht, kv) = refs[:n], refs[n:]
    rows = n * parts[0].shape[0]

    @pl.when(pl.program_id(0) == 0)
    def _():
        for k in range(n):
            modulate(parts[k], mod_ref, 2, w_ref.shape[0], ht, rows, k * parts[0].shape[0])

    size = min(2 * rows, 192)

    def project(start):
        kv[pl.ds(start, size), :] = nn(ht[pl.ds(start, size), :], w_ref[...])

    over(2 * rows, size, project)
    gain = gain_ref[2:3, :]
    for j in range(pair):
        for m in range(2):
            at = slice(m * rows, (m + 1) * rows)
            c = j * 2 * HD
            k_ref[j, m] = normed(kv[at, c : c + HD], gain)
            v_ref[j, m] = kv[at, c + HD : c + 2 * HD].astype(BF16)


def fixed(x):
    return pl.BlockSpec(x.shape, lambda s: (0,) * x.ndim, pipeline_mode=pl.Buffered(1))


def split(count):
    pair = 2 if count % 2 == 0 else 1
    return pair, count // pair


def params(mib):
    return pltpu.CompilerParams(
        dimension_semantics=("arbitrary",), vmem_limit_bytes=mib * 1024 * 1024
    )


def project_text(mod, gain, w, parts):
    n, width = len(parts), w.shape[0]
    pair, steps = split(w.shape[1] // (2 * HD))
    rows = n * parts[0].shape[0]
    out = jax.ShapeDtypeStruct((pair * steps, 2, rows, HD), BF16)
    spec = pl.BlockSpec((pair, 2, rows, HD), lambda s: (s, 0, 0, 0))
    cols = pair * 2 * HD
    return pl.pallas_call(
        functools.partial(text_kernel, n, pair),
        grid=(steps,),
        in_specs=[fixed(mod), fixed(gain), pl.BlockSpec((width, cols), lambda s: (0, s))]
        + [fixed(x) for x in parts],
        out_specs=[spec, spec],
        out_shape=[out, out],
        scratch_shapes=[pltpu.VMEM((2 * rows, width), BF16), pltpu.VMEM((2 * rows, cols), F32)],
        compiler_params=params(58),
        cost_estimate=pl.CostEstimate(
            flops=4 * rows * w.size, bytes_accessed=2 * w.size, transcendentals=0
        ),
        name="project_text",
    )(mod, gain, w, *parts)


def image_kernel(pair, past, mod_ref, gain_ref, down_ref, up_ref, w_ref, tokens, *refs):
    q_ref, k_ref, v_ref, x_ref, low_ref, hs_ref, hi, qkv = refs[past:]
    rows = tokens.shape[0]

    @pl.when(pl.program_id(0) == 0)
    def _():
        modulate(tokens, mod_ref, 0, w_ref.shape[0], hi, rows, 0)
        hs_ref[...] = hi[rows:, :]
        low_ref[...] = nt(hi[rows:, :], down_ref[...]).astype(BF16)

    qkv[...] = nn(hi[...], w_ref[...])
    qkv[rows:, :] = qkv[rows:, :] + nn(low_ref[...], up_ref[...])
    for j in range(pair):
        c = j * 3 * HD
        for m in range(2):
            at = slice(m * rows, (m + 1) * rows)
            q, k = qkv[at, c : c + HD], qkv[at, c + HD : c + 2 * HD]
            q_ref[j, m] = normed(q, gain_ref[0:1, :])
            k_ref[j, m] = normed(k, gain_ref[1:2, :])
            v_ref[j, m] = qkv[at, c + 2 * HD : c + 3 * HD].astype(BF16)
            if m == 1:
                x_ref[j, 0] = q
                x_ref[j, 1] = k


def project_image(part, n, before, mod, gain, down, up, w, tokens):
    (rows, width), rank = tokens.shape, up.shape[0]
    pair, steps = split(w.shape[1] // (3 * HD))
    cols = pair * 3 * HD
    heads = (pair * steps, 2, n * rows, HD)
    spec = pl.BlockSpec((pair, 2, rows, HD), lambda s: (s, 0, part, 0))
    whole = lambda s: (part, 0)
    shapes = [jax.ShapeDtypeStruct(heads, BF16)] * 3 + [
        jax.ShapeDtypeStruct(heads, F32),
        jax.ShapeDtypeStruct((n * rows, rank), BF16),
        jax.ShapeDtypeStruct((n * rows, width), BF16),
    ]
    return pl.pallas_call(
        functools.partial(image_kernel, pair, len(before)),
        grid=(steps,),
        in_specs=[fixed(mod), fixed(gain), fixed(down)]
        + [
            pl.BlockSpec((rank, cols), lambda s: (0, s)),
            pl.BlockSpec((width, cols), lambda s: (0, s)),
            fixed(tokens),
        ]
        + [pl.BlockSpec(memory_space=pl.ANY)] * len(before),
        out_specs=[spec] * 4 + [pl.BlockSpec((rows, rank), whole), pl.BlockSpec((rows, width), whole)],
        out_shape=shapes,
        input_output_aliases={6 + i: i for i in range(len(before))},
        scratch_shapes=[pltpu.VMEM((2 * rows, width), BF16), pltpu.VMEM((2 * rows, cols), F32)],
        compiler_params=params(58),
        cost_estimate=pl.CostEstimate(
            flops=4 * rows * w.size, bytes_accessed=2 * w.size, transcendentals=0
        ),
        name="project_image",
    )(mod, gain, down, up, w, tokens, *before)


def attend_kernel(
    steps, pair, samples, where_ref, bias_ref, gain_ref, up_ref, q_ref, k_ref, v_ref, x_ref, kt_ref, vt_ref,
    low_ref, hs_ref, send_a, keep_a, send_b, keep_b, loss_ref, lowt, glt, k_s, v_s, dk_s, dv_s, gq, whole
):
    step = pl.program_id(0)
    core = where_ref[0]
    rows, trows = q_ref.shape[2], kt_ref.shape[2]
    block = min(rows, 160)
    half = send_a.shape[0]
    heads = range(pair)

    @pl.when(step == 0)
    def _():
        lowt[...] = low_ref[...].astype(F32).T.astype(BF16)
        glt[...] = jnp.zeros_like(glt)
        loss_ref[...] = jnp.zeros_like(loss_ref)

    for j in heads:
        for m in range(2):
            k_s[j, m, :rows, :] = k_ref[j, m]
            k_s[j, m, rows:, :] = kt_ref[j, m]
            v_s[j, m, :rows, :] = v_ref[j, m]
            v_s[j, m, rows:, :] = vt_ref[j, m]
    if rows > block:
        dk_s[...] = jnp.zeros_like(dk_s)
        dv_s[...] = jnp.zeros_like(dv_s)
    gain_q, gain_k = gain_ref[0:1, :], gain_ref[1:2, :]

    def attend(start):
        at = pl.ds(start, block)
        both = [(j, m) for j in heads for m in range(2)]
        scores = {(j, m): nt(q_ref[j, m, at, :], k_s[j, m]) for j, m in both}
        weights = {i: jnp.exp2(scores[i] * (ROOT * LOG2E) + bias_ref[...]) for i in both}
        scale = {i: 1.0 / jnp.sum(weights[i], axis=1, keepdims=True) for i in both}
        probs = {i: weights[i] * scale[i] for i in both}
        rounded = {i: probs[i].astype(BF16) for i in both}
        out = {(j, m): nn(rounded[j, m], v_s[j, m]) for j, m in both}
        diff = [out[j, 1] - out[j, 0].astype(BF16).astype(F32) for j in heads]
        total = diff[0] * diff[0]
        for d in diff[1:]:
            total = total + d * d
        loss_ref[...] += jnp.sum(total.reshape(block // 8, 8, HD), axis=0)
        dout = [(d * (2.0 / samples)).astype(BF16) for d in diff]
        dprobs = [nt(dout[j], v_s[j, 1]).astype(BF16).astype(F32) for j in heads]
        dv = [tn(rounded[j, 1], dout[j]) for j in heads]
        inner = [jnp.sum(dprobs[j] * probs[j, 1], axis=1, keepdims=True) for j in heads]
        dscores = [(probs[j, 1] * (dprobs[j] - inner[j]) * ROOT).astype(BF16) for j in heads]
        dq = [nn(dscores[j], k_s[j, 1]).astype(BF16).astype(F32) for j in heads]
        dk = [tn(dscores[j], q_ref[j, 1, at, :]) for j in heads]
        for j in heads:
            c = j * 3 * HD
            gq[at, c : c + HD] = norm_pull(x_ref[j, 0, at, :], gain_q, dq[j]).astype(BF16)
            if rows > block:
                dk_s[j] += dk[j][:rows]
                dv_s[j] += dv[j][:rows]
            else:
                dk_s[j] = dk[j][:rows]
                dv_s[j] = dv[j][:rows]

    over(rows, block, attend)

    def rest(start):
        at = pl.ds(start, block)
        for j in heads:
            c = j * 3 * HD
            dk = dk_s[j, at, :].astype(BF16).astype(F32)
            gq[at, c + HD : c + 2 * HD] = norm_pull(x_ref[j, 1, at, :], gain_k, dk).astype(BF16)
            gq[at, c + 2 * HD : c + 3 * HD] = dv_s[j, at, :].astype(BF16)

    over(rows, block, rest)

    def share(value, columns, send, keep):
        whole[:, columns] = value
        keep[...] = whole[pl.ds(pl.multiple_of(core * half, 8), half), columns]
        send[...] = whole[pl.ds(pl.multiple_of((1 - core) * half, 8), half), columns].astype(send.dtype)

    share(nn(lowt[...], gq[...]), slice(0, gq.shape[1]), send_b, keep_b)
    glt[...] += nt(up_ref[...], gq[...])

    @pl.when(step == steps - 1)
    def _():
        g = glt[...]
        g1 = g.astype(BF16)
        rest = g - g1.astype(F32)
        g2 = rest.astype(BF16)
        g3 = (rest - g2.astype(F32)).astype(BF16)
        stack = jnp.concatenate([g1, g2, g3], 0)
        rank = g.shape[0]
        full = nn(stack, hs_ref[...])
        share(
            full[:rank] + full[rank : 2 * rank] + full[2 * rank :],
            slice(0, full.shape[1]),
            send_a,
            keep_a,
        )


def attend(where, bias, gain, up, image, text):
    q, k, v, x, low, hs = image
    kt, vt = text
    (rank, img_cols), width = up.shape, hs.shape[1]
    count, _, rows, _ = q.shape
    trows = kt.shape[2]
    pair, steps = split(count)
    half, ic = rank // 2, pair * 3 * HD
    samples = lax.axis_size("grp") * lax.axis_size("dp")
    out_a, out_b = (half, width), (half, img_cols)
    spec_a = pl.BlockSpec(out_a, lambda s: (0, 0))
    spec_b = pl.BlockSpec((half, ic), lambda s: (0, s))
    by_head = lambda a: pl.BlockSpec((pair, *a.shape[1:]), lambda s: (s, 0, 0, 0))
    return pl.pallas_call(
        functools.partial(attend_kernel, steps, pair, samples),
        grid=(steps,),
        in_specs=[pl.BlockSpec(memory_space=pltpu.SMEM), fixed(bias), fixed(gain)]
        + [pl.BlockSpec((rank, ic), lambda s: (0, s))]
        + [by_head(a) for a in (q, k, v, x, kt, vt)]
        + [fixed(low), fixed(hs)],
        out_specs=[spec_a, spec_a, spec_b, spec_b, pl.BlockSpec((8, HD), lambda s: (0, 0))],
        out_shape=[
            jax.ShapeDtypeStruct(out_a, BF16),
            jax.ShapeDtypeStruct(out_a, F32),
            jax.ShapeDtypeStruct(out_b, BF16),
            jax.ShapeDtypeStruct(out_b, F32),
            jax.ShapeDtypeStruct((8, HD), F32),
        ],
        scratch_shapes=[
            pltpu.VMEM((rank, rows), BF16),
            pltpu.VMEM((rank, rows), F32),
            pltpu.VMEM((pair, 2, rows + trows, HD), BF16),
            pltpu.VMEM((pair, 2, rows + trows, HD), BF16),
            pltpu.VMEM((pair, rows, HD), F32),
            pltpu.VMEM((pair, rows, HD), F32),
            pltpu.VMEM((rows, ic), BF16),
            pltpu.VMEM((rank, max(width, ic)), F32),
        ],
        compiler_params=params(40),
        cost_estimate=pl.CostEstimate(
            flops=16 * count * rows * (rows + trows) * HD,
            bytes_accessed=8_000_000,
            transcendentals=2 * count * rows * (rows + trows),
        ),
        name="attend",
    )(where, bias, gain, up, q, k, v, x, kt, vt, low, hs)


def start_kernel(sigma_ref, image_ref, noise_ref, emb_ref, weight_ref, noisy_ref, part_ref):
    sigma = sigma_ref[0]
    clean, noise = image_ref[...].astype(F32), noise_ref[...].astype(F32)
    noisy_ref[...] = ((1.0 - sigma) * clean + sigma * noise).astype(BF16)
    part_ref[...] = nn(emb_ref[...], weight_ref[...])[: part_ref.shape[0]]


def start(sigma, image, noise, emb, weight):
    rows, width = image.shape
    depth, cols = weight.shape
    steps = 4 if width % 512 == 0 and cols % 512 == 0 else 1
    tokens = pl.BlockSpec((rows, width // steps), lambda s: (0, s))
    return pl.pallas_call(
        start_kernel,
        grid=(steps,),
        in_specs=[
            pl.BlockSpec(memory_space=pltpu.SMEM),
            tokens,
            tokens,
            pl.BlockSpec(emb.shape, lambda s: (0, 0)),
            pl.BlockSpec((depth, cols // steps), lambda s: (0, s)),
        ],
        out_specs=[tokens, pl.BlockSpec((2, cols // steps), lambda s: (0, s))],
        out_shape=[
            jax.ShapeDtypeStruct((rows, width), BF16),
            jax.ShapeDtypeStruct((2, cols), F32),
        ],
        compiler_params=params(60),
        cost_estimate=pl.CostEstimate(
            flops=4 * depth * cols, bytes_accessed=2 * weight.size + 6 * image.size, transcendentals=0
        ),
        name="start",
    )(sigma, image, noise, emb, weight)


def finish_kernel(scale_a, scale_b, scale_loss, a_ref, b_ref, sums_ref, out_a, out_b, loss_ref):
    half = HD // 2
    total = jnp.sum(sums_ref[...], axis=0, keepdims=True)
    loss_ref[...] = jnp.sum(total[:, :half], axis=1, keepdims=True) * scale_loss
    squares_b = jnp.sum(total[:, half:], axis=1, keepdims=True) * scale_b
    grad_a = a_ref[...].astype(F32)
    squares = jnp.sum(jnp.sum(grad_a * grad_a, axis=0, keepdims=True), axis=1, keepdims=True)
    unit_a = lax.rsqrt(squares * scale_a + EPS)
    out_b[...] = b_ref[...].astype(F32) * lax.rsqrt(squares_b + EPS)
    out_a[...] = grad_a * unit_a


def finish(grad_a, grad_b, sums, n, entries):
    (rank, width), cols = grad_a.shape, grad_b.shape[1]
    return pl.pallas_call(
        functools.partial(finish_kernel, 1.0 / (rank * width), 1.0 / (rank * cols * n), 1.0 / entries),
        out_shape=[
            jax.ShapeDtypeStruct((rank, width), F32),
            jax.ShapeDtypeStruct((rank, cols), F32),
            jax.ShapeDtypeStruct((1, 1), F32),
        ],
        name="finish",
    )(grad_a, grad_b, sums)


def shifted(x, axis, k):
    size = lax.axis_size(axis)
    return lax.ppermute(x, axis, [(i, (i + k) % size) for i in range(size)])


def side_of(axis, bit):
    return lax.rem(lax.div(lax.axis_index(axis), bit), 2)


def swap(arrays, axis, bit):
    pairs = [(i, i ^ bit) for i in range(lax.axis_size(axis))]
    if len(arrays) == 1 or any(x.shape[0] % 8 or x.shape[1] % HD for x in arrays):
        return [lax.ppermute(x, axis, pairs) for x in arrays]
    rows = [x[r : r + 8] for x in arrays for r in range(0, x.shape[0], 8)]
    got = lax.ppermute(jnp.concatenate(rows, 1), axis, pairs)
    out, at = [], 0
    for x in arrays:
        blocks = []
        for _ in range(0, x.shape[0], 8):
            blocks.append(got[:, at : at + x.shape[1]])
            at += x.shape[1]
        out.append(blocks[0] if len(blocks) == 1 else jnp.concatenate(blocks, 0))
    return out


def cut_of(x):
    if x.shape[0] % 16 == 0:
        return 0
    return 1 if x.shape[1] % (2 * HD) == 0 else 0


def halve(arrays, axis, bit, dtype):
    side = side_of(axis, bit)
    keep, send = [], []
    for x in arrays:
        dim = cut_of(x)
        first, second = jnp.split(x, 2, dim)
        keep.append(jnp.where(side == 0, first, second))
        send.append(jnp.where(side == 0, second, first).astype(dtype))
    got = swap(send, axis, bit)
    return [k + g.astype(F32) for k, g in zip(keep, got)]


def join(mine, theirs, side, dim):
    return jnp.concatenate(
        [jnp.where(side == 0, mine, theirs), jnp.where(side == 0, theirs, mine)], dim
    )


def pieces(value):
    first = lax.reduce_precision(value, 8, 7)
    rest = value - first
    second = lax.reduce_precision(rest, 8, 7)
    return jnp.concatenate([first, second, rest - second], 1).astype(BF16)


def rejoin(arrays, dims, sums, axis, bit):
    side = side_of(axis, bit)
    *got, other = swap([*arrays, pieces(sums)], axis, bit)
    other = other.astype(F32)
    sums = sums + (other[:, :HD] + other[:, HD : 2 * HD] + other[:, 2 * HD :])
    return [join(x, g, side, d) for x, g, d in zip(arrays, got, dims)], sums


def bits(axis):
    size = lax.axis_size(axis)
    return [1 << i for i in range(size.bit_length() - 1)]


def fold(x):
    half = HD // 2
    return functools.reduce(
        lambda total, c: total + x[:, c : c + half], range(half, x.shape[1], half), x[:, :half]
    )


def on_device(
    image,
    noise,
    text,
    timestep,
    guidance,
    text_token_length,
    image_projection_weight,
    text_projection_weight,
    modulation_weight,
    query_key_norm_gain,
    adapter_down_weight,
    adapter_up_weight,
):
    emb_width = modulation_weight.shape[0]
    n, me = lax.axis_size("seq"), lax.axis_index("seq")
    samples = lax.axis_size("grp") * lax.axis_size("dp")
    sigma = (timestep[0].astype(F32) + 1.0) / STEPS
    time = timing(sigma, emb_width)
    emb = jnp.stack(
        [
            jnp.concatenate([time, timing(guidance[0], emb_width)]),
            jnp.concatenate([time, jnp.zeros((emb_width // 2,), F32)]),
        ]
    )
    emb = jnp.pad(jax.nn.silu(emb).astype(BF16), ((0, 14), (0, 0)))
    noisy, part = start(sigma[None], image[0], noise[0], emb, modulation_weight)
    mods = [part] + [shifted(part, "seq", k) for k in range(1, n)]
    noisy_parts = [noisy] + [shifted(noisy, "seq", k) for k in range(1, n)]
    words = text[0]
    text_parts = [words] + [shifted(words, "seq", k) for k in range(1, n)]
    origin = [lax.rem(me + n - k, n) for k in range(n)]
    ordered = [
        functools.reduce(
            lambda so_far, k: jnp.where(origin[k] == j, mods[k], so_far), range(1, n), mods[0]
        )
        for j in range(n)
    ]
    mod = jnp.concatenate(ordered, 1)
    img_part, txt_part = noisy.shape[0], words.shape[0]
    place = jnp.concatenate(
        [jnp.zeros((n * img_part,), jnp.int32)]
        + [origin[k] * txt_part + jnp.arange(txt_part, dtype=jnp.int32) for k in range(n)]
    )
    bias = jnp.where(place < text_token_length[0], 0.0, -1000000000.0).astype(F32)[None]
    core = lax.rem(lax.axis_index("grp"), 2).astype(jnp.int32)
    gain = query_key_norm_gain
    text_heads = project_text(mod, gain, text_projection_weight, text_parts)
    image_heads = []
    for k in range(n):
        image_heads = project_image(
            k,
            n,
            image_heads,
            mod,
            gain,
            adapter_down_weight.T,
            adapter_up_weight,
            image_projection_weight,
            noisy_parts[k],
        )
    send_a, keep_a, send_b, keep_b, loss = attend(
        core[None], bias, gain, adapter_up_weight, image_heads, text_heads
    )
    (got_a,), (got_b,) = swap([send_a], "grp", 1), swap([send_b], "grp", 1)
    grad_a, grad_b = keep_a + got_a.astype(F32), keep_b + got_b.astype(F32)
    seq_dims, dp_dims = [], []
    for bit in reversed(bits("seq")):
        seq_dims.append(cut_of(grad_a))
        (grad_a,) = halve([grad_a], "seq", bit, BF16)
    x_dims = [cut_of(grad_a), cut_of(grad_b)]
    (grad_b,) = halve([grad_b], "grp", 2, BF16)
    (grad_a,) = halve([grad_a], "grp", 2, BF16)
    for bit in bits("dp"):
        dp_dims.append([cut_of(grad_a), cut_of(grad_b)])
        grad_a, grad_b = halve([grad_a, grad_b], "dp", bit, F32)
    squares = fold(grad_b * grad_b)
    squares = jnp.pad(squares, ((0, 8 - squares.shape[0]), (0, 0)))
    sums = jnp.concatenate([fold(loss), squares], 1)
    grads = [grad_a.astype(BF16), grad_b.astype(BF16)]
    for bit in reversed(bits("dp")):
        grads, sums = rejoin(grads, dp_dims.pop(), sums, "dp", bit)
    grads, sums = rejoin(grads, x_dims, sums, "grp", 2)
    for bit in bits("seq"):
        (grads[0],), sums = rejoin(grads[:1], [seq_dims.pop()], sums, "seq", bit)
    grads, sums = rejoin(grads, [0, 0], sums, "grp", 1)
    direction_a, direction_b, loss_mean = finish(
        *grads, sums, n, samples * n * img_part * HEADS * HD
    )
    return (direction_a.T, direction_b, loss_mean[0, 0])


def solution(mesh):
    in_specs = (
        P(("grp", "dp"), "seq", None),
        P(("grp", "dp"), "seq", None),
        P(("grp", "dp"), "seq", None),
        P(("grp", "dp")),
        P(("grp", "dp")),
        P(("grp", "dp")),
        P(None, "seq"),
        P(None, "seq"),
        P(None, "seq"),
        P(),
        P(),
        P(None, "seq"),
    )
    out_specs = (P(), P(None, "seq"), P())
    return jax.shard_map(
        on_device, mesh=mesh, in_specs=in_specs, out_specs=out_specs, check_vma=False
    )
```

```python
import functools
import math

import jax
import jax.numpy as jnp
from jax import lax
from jax.experimental import pallas as pl
from jax.experimental.pallas import tpu as pltpu
from jax.sharding import PartitionSpec as P

HD = 128
HEADS = 16
STEPS = 1000
EPS = 1e-06
F32 = jnp.float32
BF16 = jnp.bfloat16
ROOT = 1.0 / math.sqrt(HD)
LOG2E = 1.0 / math.log(2.0)
SMALL = 10 * 1024 * 1024


def timing(value, width):
    count = width // 4
    freqs = jnp.exp(-math.log(10000.0) * jnp.arange(count, dtype=F32) / count)
    angles = 1000.0 * value * freqs
    return jnp.concatenate([jnp.cos(angles), jnp.sin(angles)])


def nn(a, b):
    return lax.dot_general(a, b, (((1,), (0,)), ((), ())), preferred_element_type=F32)


def nt(a, b):
    return lax.dot_general(a, b, (((1,), (1,)), ((), ())), preferred_element_type=F32)


def tn(a, b):
    return lax.dot_general(a, b, (((0,), (0,)), ((), ())), preferred_element_type=F32)


def over(total, size, body):
    if total == size:
        body(0)
    else:

        @pl.loop(0, total // size)
        def _(i):
            body(pl.multiple_of(i * size, size))


def inverse_rms(x):
    return lax.rsqrt(jnp.mean(x * x, axis=-1, keepdims=True) + EPS)


def norm_pull(x, gain, dy):
    r = inverse_rms(x)
    u = gain * dy
    return r * (u - x * (r * r * jnp.mean(x * u, axis=-1, keepdims=True)))


def modulate(tokens, mod_ref, kind, width, dest, rows, base):
    size = tokens.shape[0]

    @pl.loop(0, size // 16)
    def _(i):
        v = tokens[pl.ds(pl.multiple_of(i * 16, 16), 16), :].astype(F32)
        center = v - jnp.mean(v, axis=1, keepdims=True)
        spread = jnp.mean(center * center, axis=1, keepdims=True)
        unit = center * lax.rsqrt(spread + EPS)
        for m in range(2):
            shift = mod_ref[m : m + 1, kind * width : (kind + 1) * width]
            scale = mod_ref[m : m + 1, (kind + 1) * width : (kind + 2) * width]
            at = pl.multiple_of(m * rows + base + i * 16, 16)
            dest[pl.ds(at, 16), :] = (unit * (1.0 + scale) + shift).astype(BF16)


def normed(x, gain):
    return (x * inverse_rms(x) * gain).astype(BF16)


def text_kernel(pair, index, past, mod_ref, gain_ref, w_ref, tokens, *refs):
    k_ref, v_ref, ht = refs[past + min(index, 1) :]
    rows = tokens.shape[0]
    part = slice(index * rows, (index + 1) * rows)
    modulate(tokens, mod_ref, 2, w_ref.shape[0], ht, rows, 0)
    cols = pair * 2 * HD

    @pl.loop(0, w_ref.shape[1] // cols)
    def _(step):
        kv = nn(ht[...], w_ref[:, pl.ds(pl.multiple_of(step * cols, cols), cols)])
        for j in range(pair):
            head, c = step * pair + j, j * 2 * HD
            for m in range(2):
                at = slice(m * rows, (m + 1) * rows)
                k_ref[head, m, part, :] = normed(kv[at, c : c + HD], gain_ref[2:3, :])
                v_ref[head, m, part, :] = kv[at, c + HD : c + 2 * HD].astype(BF16)


def fixed(x):
    return pl.BlockSpec(x.shape, lambda s: (0,) * x.ndim, pipeline_mode=pl.Buffered(1))


def split(count):
    pair = 2 if count % 2 == 0 else 1
    return pair, count // pair


def params(mib):
    return pltpu.CompilerParams(
        dimension_semantics=("arbitrary",), vmem_limit_bytes=mib * 1024 * 1024
    )


VMEM = pl.BlockSpec(memory_space=pltpu.VMEM)
HELD = pl.BlockSpec(memory_space=pltpu.HBM)


def project_text(part, n, before, mod, gain, w, tokens, after):
    after = [after] * min(part, 1)
    rows, width = tokens.shape
    pair, steps = split(w.shape[1] // (2 * HD))
    out = pltpu.VMEM((pair * steps, 2, n * rows, HD), BF16)
    return pl.pallas_call(
        functools.partial(text_kernel, pair, part, len(before)),
        in_specs=[VMEM] * (4 + len(before)) + [pl.BlockSpec(memory_space=pl.ANY)] * len(after),
        out_specs=[VMEM] * 2,
        out_shape=[out, out],
        input_output_aliases={4 + i: i for i in range(len(before))},
        scratch_shapes=[pltpu.VMEM((2 * rows, width), BF16)],
        compiler_params=pltpu.CompilerParams(vmem_limit_bytes=SMALL),
        cost_estimate=pl.CostEstimate(
            flops=4 * rows * w.size, bytes_accessed=2 * w.size, transcendentals=0
        ),
        name="project_text",
    )(mod, gain, w, tokens, *before, *after)


def fetch_kernel(after_ref, w_ref, out_ref, sems):
    for copy in fetches(w_ref, out_ref, sems):
        copy.start()
    for copy in fetches(w_ref, out_ref, sems):
        copy.wait()


def fetches(w_ref, out_ref, sems):
    cols = w_ref.shape[1] // sems.shape[0]
    return [
        pltpu.make_async_copy(
            w_ref.at[:, i * cols : (i + 1) * cols], out_ref.at[:, i * cols : (i + 1) * cols], sems.at[i]
        )
        for i in range(sems.shape[0])
    ]


def held(x):
    return pltpu.with_memory_space_constraint(x, pltpu.HBM)


def fetch(w, steps, after):
    return pl.pallas_call(
        fetch_kernel,
        in_specs=[pl.BlockSpec(memory_space=pl.ANY), HELD],
        out_specs=VMEM,
        out_shape=pltpu.VMEM(w.shape, w.dtype),
        scratch_shapes=[pltpu.SemaphoreType.DMA((steps,))],
        compiler_params=pltpu.CompilerParams(vmem_limit_bytes=SMALL),
        cost_estimate=pl.CostEstimate(flops=0, bytes_accessed=4 * w.size, transcendentals=0),
        name="fetch",
    )(after, w)


def image_kernel(pair, index, past, mod_ref, gain_ref, down_ref, up_ref, w_ref, tokens, *refs):
    first = past == 0
    q_ref, k_ref, v_ref, x_ref, low_ref, hs_ref, *rest = refs[past + first :]
    weights, copies = w_ref, None
    if first:
        weights, hi, sems = rest
        copies = fetches(w_ref, weights, sems)
        for copy in copies:
            copy.start()
    else:
        (hi,) = rest
    rows = tokens.shape[0]
    part = slice(index * rows, (index + 1) * rows)
    modulate(tokens, mod_ref, 0, w_ref.shape[0], hi, rows, 0)
    hs_ref[part, :] = hi[rows:, :]
    low_ref[part, :] = nt(hi[rows:, :], down_ref[...]).astype(BF16)
    cols = pair * 3 * HD

    def project(step):
        columns = pl.ds(step * cols, cols)
        if not isinstance(step, int):
            columns = pl.ds(pl.multiple_of(step * cols, cols), cols)
        qkv = nn(hi[...], weights[:, columns])
        student = qkv[rows:] + nn(low_ref[part, :], up_ref[:, columns])
        for j in range(pair):
            head, c = step * pair + j, j * 3 * HD
            for m, own in enumerate((qkv[:rows], student)):
                q, k = own[:, c : c + HD], own[:, c + HD : c + 2 * HD]
                q_ref[head, m, part, :] = normed(q, gain_ref[0:1, :])
                k_ref[head, m, part, :] = normed(k, gain_ref[1:2, :])
                v_ref[head, m, part, :] = own[:, c + 2 * HD : c + 3 * HD].astype(BF16)
                if m == 1:
                    x_ref[head, 0, part, :] = q
                    x_ref[head, 1, part, :] = k

    if copies is None:
        pl.loop(0, w_ref.shape[1] // cols)(project)
    else:
        for step, copy in enumerate(copies):
            copy.wait()
            project(step)


def project_image(part, n, before, mod, gain, down, up, w, tokens, after):
    after = [] if before else [after]
    (rows, width), rank = tokens.shape, up.shape[0]
    pair, steps = split(w.shape[1] // (3 * HD))
    heads = (pair * steps, 2, n * rows, HD)
    shapes = [pltpu.VMEM(heads, BF16)] * 3 + [
        pltpu.VMEM(heads, F32),
        pltpu.VMEM((n * rows, rank), BF16),
        pltpu.VMEM((n * rows, width), BF16),
    ]
    scratch = [pltpu.VMEM((2 * rows, width), BF16)]
    if not before:
        shapes.append(pltpu.VMEM(w.shape, w.dtype))
        scratch.append(pltpu.SemaphoreType.DMA((steps,)))
    return pl.pallas_call(
        functools.partial(image_kernel, pair, part, len(before)),
        in_specs=[VMEM] * 4
        + [VMEM if before else HELD]
        + [VMEM] * (1 + len(before))
        + [pl.BlockSpec(memory_space=pl.ANY)] * len(after),
        out_specs=[VMEM] * len(shapes),
        out_shape=shapes,
        input_output_aliases={6 + i: i for i in range(len(before))},
        scratch_shapes=scratch,
        compiler_params=pltpu.CompilerParams(vmem_limit_bytes=SMALL),
        cost_estimate=pl.CostEstimate(
            flops=4 * rows * w.size, bytes_accessed=2 * w.size, transcendentals=0
        ),
        name="project_image",
    )(mod, gain, down, up, w, tokens, *before, *after)


def attend_kernel(
    steps, pair, samples, where_ref, bias_ref, gain_ref, up_ref, q_ref, k_ref, v_ref, x_ref, kt_ref, vt_ref,
    low_ref, hs_ref, send_a, keep_a, send_b, keep_b, loss_ref, lowt, glt, k_s, v_s, dk_s, dv_s, gq, whole
):
    core = where_ref[0]
    half = send_a.shape[0]
    lowt[...] = low_ref[...].astype(F32).T.astype(BF16)
    glt[...] = jnp.zeros_like(glt)
    loss_ref[...] = jnp.zeros_like(loss_ref)

    def share(value, columns, send, keep):
        whole[:, : value.shape[1]] = value
        mine = pl.ds(pl.multiple_of(core * half, 8), half)
        other = pl.ds(pl.multiple_of((1 - core) * half, 8), half)
        keep[:, columns] = whole[mine, : value.shape[1]]
        send[:, columns] = whole[other, : value.shape[1]].astype(send.dtype)

    @pl.loop(0, steps)
    def _(step):
        columns = pl.ds(pl.multiple_of(step * gq.shape[1], HD), gq.shape[1])
        group = pl.ds(step * pair, pair)
        attend_heads(
            pair, samples, bias_ref, gain_ref, *[r.at[group] for r in (q_ref, k_ref, v_ref, x_ref, kt_ref, vt_ref)],
            loss_ref, k_s, v_s, dk_s, dv_s, gq,
        )
        share(nn(lowt[...], gq[...]), columns, send_b, keep_b)
        glt[...] += nt(up_ref[:, columns], gq[...])

    g = glt[...]
    g1 = g.astype(BF16)
    rest = g - g1.astype(F32)
    g2 = rest.astype(BF16)
    g3 = (rest - g2.astype(F32)).astype(BF16)
    stack = jnp.concatenate([g1, g2, g3], 0)
    rank = g.shape[0]
    full = nn(stack, hs_ref[...])
    share(full[:rank] + full[rank : 2 * rank] + full[2 * rank :], slice(0, full.shape[1]), send_a, keep_a)


def attend_heads(
    pair, samples, bias_ref, gain_ref, q_ref, k_ref, v_ref, x_ref, kt_ref, vt_ref, loss_ref, k_s, v_s, dk_s, dv_s, gq
):
    rows = q_ref.shape[2]
    block = min(rows, 160)
    heads = range(pair)
    for j in heads:
        for m in range(2):
            k_s[j, m, :rows, :] = k_ref[j, m]
            k_s[j, m, rows:, :] = kt_ref[j, m]
            v_s[j, m, :rows, :] = v_ref[j, m]
            v_s[j, m, rows:, :] = vt_ref[j, m]
    if rows > block:
        dk_s[...] = jnp.zeros_like(dk_s)
        dv_s[...] = jnp.zeros_like(dv_s)
    gain_q, gain_k = gain_ref[0:1, :], gain_ref[1:2, :]

    def attend(start):
        at = pl.ds(start, block)
        both = [(j, m) for j in heads for m in range(2)]
        scores = {(j, m): nt(q_ref[j, m, at, :], k_s[j, m]) for j, m in both}
        weights = {i: jnp.exp2(scores[i] * (ROOT * LOG2E) + bias_ref[...]) for i in both}
        scale = {i: 1.0 / jnp.sum(weights[i], axis=1, keepdims=True) for i in both}
        probs = {i: weights[i] * scale[i] for i in both}
        rounded = {i: probs[i].astype(BF16) for i in both}
        out = {(j, m): nn(rounded[j, m], v_s[j, m]) for j, m in both}
        diff = [out[j, 1] - out[j, 0].astype(BF16).astype(F32) for j in heads]
        total = diff[0] * diff[0]
        for d in diff[1:]:
            total = total + d * d
        loss_ref[...] += jnp.sum(total.reshape(block // 8, 8, HD), axis=0)
        dout = [(d * (2.0 / samples)).astype(BF16) for d in diff]
        dprobs = [nt(dout[j], v_s[j, 1]).astype(BF16).astype(F32) for j in heads]
        dv = [tn(rounded[j, 1], dout[j]) for j in heads]
        inner = [jnp.sum(dprobs[j] * probs[j, 1], axis=1, keepdims=True) for j in heads]
        dscores = [(probs[j, 1] * (dprobs[j] - inner[j]) * ROOT).astype(BF16) for j in heads]
        dq = [nn(dscores[j], k_s[j, 1]).astype(BF16).astype(F32) for j in heads]
        dk = [tn(dscores[j], q_ref[j, 1, at, :]) for j in heads]
        for j in heads:
            c = j * 3 * HD
            gq[at, c : c + HD] = norm_pull(x_ref[j, 0, at, :], gain_q, dq[j]).astype(BF16)
            if rows > block:
                dk_s[j] += dk[j][:rows]
                dv_s[j] += dv[j][:rows]
            else:
                dk_s[j] = dk[j][:rows]
                dv_s[j] = dv[j][:rows]

    over(rows, block, attend)

    def rest(start):
        at = pl.ds(start, block)
        for j in heads:
            c = j * 3 * HD
            dk = dk_s[j, at, :].astype(BF16).astype(F32)
            gq[at, c + HD : c + 2 * HD] = norm_pull(x_ref[j, 1, at, :], gain_k, dk).astype(BF16)
            gq[at, c + 2 * HD : c + 3 * HD] = dv_s[j, at, :].astype(BF16)

    over(rows, block, rest)


def attend(where, bias, gain, up, image, text):
    q, k, v, x, low, hs = image
    kt, vt = text
    (rank, img_cols), width = up.shape, hs.shape[1]
    count, _, rows, _ = q.shape
    trows = kt.shape[2]
    pair, steps = split(count)
    half, ic = rank // 2, pair * 3 * HD
    samples = lax.axis_size("grp") * lax.axis_size("dp")
    out_a, out_b = (half, width), (half, img_cols)
    return pl.pallas_call(
        functools.partial(attend_kernel, steps, pair, samples),
        in_specs=[pl.BlockSpec(memory_space=pltpu.SMEM)] + [VMEM] * 11,
        out_specs=[VMEM] * 5,
        out_shape=[
            jax.ShapeDtypeStruct(out_a, BF16),
            jax.ShapeDtypeStruct(out_a, F32),
            jax.ShapeDtypeStruct(out_b, BF16),
            jax.ShapeDtypeStruct(out_b, F32),
            jax.ShapeDtypeStruct((8, HD), F32),
        ],
        scratch_shapes=[
            pltpu.VMEM((rank, rows), BF16),
            pltpu.VMEM((rank, rows), F32),
            pltpu.VMEM((pair, 2, rows + trows, HD), BF16),
            pltpu.VMEM((pair, 2, rows + trows, HD), BF16),
            pltpu.VMEM((pair, rows, HD), F32),
            pltpu.VMEM((pair, rows, HD), F32),
            pltpu.VMEM((rows, ic), BF16),
            pltpu.VMEM((rank, max(width, ic)), F32),
        ],
        compiler_params=pltpu.CompilerParams(vmem_limit_bytes=2 * SMALL),
        cost_estimate=pl.CostEstimate(
            flops=16 * count * rows * (rows + trows) * HD,
            bytes_accessed=8_000_000,
            transcendentals=2 * count * rows * (rows + trows),
        ),
        name="attend",
    )(where, bias, gain, up, q, k, v, x, kt, vt, low, hs)


def start_kernel(sigma_ref, image_ref, noise_ref, emb_ref, weight_ref, noisy_ref, part_ref):
    sigma = sigma_ref[0]
    clean, noise = image_ref[...].astype(F32), noise_ref[...].astype(F32)
    noisy_ref[...] = ((1.0 - sigma) * clean + sigma * noise).astype(BF16)
    part_ref[...] = nn(emb_ref[...], weight_ref[...])[: part_ref.shape[0]]


def start(sigma, image, noise, emb, weight):
    rows, width = image.shape
    depth, cols = weight.shape
    steps = 2 if width % 256 == 0 and cols % 256 == 0 else 1
    tokens = pl.BlockSpec((rows, width // steps), lambda s: (0, s))
    return pl.pallas_call(
        start_kernel,
        grid=(steps,),
        in_specs=[
            pl.BlockSpec(memory_space=pltpu.SMEM),
            tokens,
            tokens,
            pl.BlockSpec(emb.shape, lambda s: (0, 0)),
            pl.BlockSpec((depth, cols // steps), lambda s: (0, s)),
        ],
        out_specs=[tokens, pl.BlockSpec((2, cols // steps), lambda s: (0, s))],
        out_shape=[
            jax.ShapeDtypeStruct((rows, width), BF16),
            jax.ShapeDtypeStruct((2, cols), F32),
        ],
        compiler_params=params(10),
        cost_estimate=pl.CostEstimate(
            flops=4 * depth * cols, bytes_accessed=2 * weight.size + 6 * image.size, transcendentals=0
        ),
        name="start",
    )(sigma, held(image), held(noise), emb, held(weight))


def finish_kernel(scale_a, scale_b, scale_loss, a_ref, b_ref, sums_ref, out_a, out_b, loss_ref):
    half = HD // 2
    total = jnp.sum(sums_ref[...], axis=0, keepdims=True)
    loss_ref[...] = jnp.sum(total[:, :half], axis=1, keepdims=True) * scale_loss
    squares_b = jnp.sum(total[:, half:], axis=1, keepdims=True) * scale_b
    grad_a = a_ref[...].astype(F32)
    squares = jnp.sum(jnp.sum(grad_a * grad_a, axis=0, keepdims=True), axis=1, keepdims=True)
    unit_a = lax.rsqrt(squares * scale_a + EPS)
    out_b[...] = b_ref[...].astype(F32) * lax.rsqrt(squares_b + EPS)
    out_a[...] = grad_a * unit_a


def finish(grad_a, grad_b, sums, n, entries):
    (rank, width), cols = grad_a.shape, grad_b.shape[1]
    return pl.pallas_call(
        functools.partial(finish_kernel, 1.0 / (rank * width), 1.0 / (rank * cols * n), 1.0 / entries),
        out_shape=[
            jax.ShapeDtypeStruct((rank, width), F32),
            jax.ShapeDtypeStruct((rank, cols), F32),
            jax.ShapeDtypeStruct((1, 1), F32),
        ],
        name="finish",
    )(grad_a, grad_b, sums)


def shifted(x, axis, k):
    size = lax.axis_size(axis)
    return lax.ppermute(x, axis, [(i, (i + k) % size) for i in range(size)])


def side_of(axis, bit):
    return lax.rem(lax.div(lax.axis_index(axis), bit), 2)


def swap(arrays, axis, bit):
    pairs = [(i, i ^ bit) for i in range(lax.axis_size(axis))]
    if len(arrays) == 1 or any(x.shape[0] % 8 or x.shape[1] % HD for x in arrays):
        return [lax.ppermute(x, axis, pairs) for x in arrays]
    rows = [x[r : r + 8] for x in arrays for r in range(0, x.shape[0], 8)]
    got = lax.ppermute(jnp.concatenate(rows, 1), axis, pairs)
    out, at = [], 0
    for x in arrays:
        blocks = []
        for _ in range(0, x.shape[0], 8):
            blocks.append(got[:, at : at + x.shape[1]])
            at += x.shape[1]
        out.append(blocks[0] if len(blocks) == 1 else jnp.concatenate(blocks, 0))
    return out


def cut_of(x):
    if x.shape[0] % 16 == 0:
        return 0
    return 1 if x.shape[1] % (2 * HD) == 0 else 0


def halve(arrays, axis, bit, dtype):
    side = side_of(axis, bit)
    keep, send = [], []
    for x in arrays:
        dim = cut_of(x)
        first, second = jnp.split(x, 2, dim)
        keep.append(jnp.where(side == 0, first, second))
        send.append(jnp.where(side == 0, second, first).astype(dtype))
    got = swap(send, axis, bit)
    return [k + g.astype(F32) for k, g in zip(keep, got)]


def join(mine, theirs, side, dim):
    return jnp.concatenate(
        [jnp.where(side == 0, mine, theirs), jnp.where(side == 0, theirs, mine)], dim
    )


def pieces(value):
    first = lax.reduce_precision(value, 8, 7)
    rest = value - first
    second = lax.reduce_precision(rest, 8, 7)
    return jnp.concatenate([first, second, rest - second], 1).astype(BF16)


def rejoin(arrays, dims, sums, axis, bit):
    side = side_of(axis, bit)
    *got, other = swap([*arrays, pieces(sums)], axis, bit)
    other = other.astype(F32)
    sums = sums + (other[:, :HD] + other[:, HD : 2 * HD] + other[:, 2 * HD :])
    return [join(x, g, side, d) for x, g, d in zip(arrays, got, dims)], sums


def bits(axis):
    size = lax.axis_size(axis)
    return [1 << i for i in range(size.bit_length() - 1)]


def fold(x):
    half = HD // 2
    return functools.reduce(
        lambda total, c: total + x[:, c : c + half], range(half, x.shape[1], half), x[:, :half]
    )


def on_device(
    image,
    noise,
    text,
    timestep,
    guidance,
    text_token_length,
    image_projection_weight,
    text_projection_weight,
    modulation_weight,
    query_key_norm_gain,
    adapter_down_weight,
    adapter_up_weight,
):
    emb_width = modulation_weight.shape[0]
    n, me = lax.axis_size("seq"), lax.axis_index("seq")
    samples = lax.axis_size("grp") * lax.axis_size("dp")
    sigma = (timestep[0].astype(F32) + 1.0) / STEPS
    time = timing(sigma, emb_width)
    guide = jnp.where(jnp.arange(16)[:, None] == 0, timing(guidance[0], emb_width)[None], 0.0)
    emb = jnp.concatenate([jnp.broadcast_to(time[None], guide.shape), guide], 1)
    emb = jax.nn.silu(emb).astype(BF16)
    noisy, part = start(sigma[None], image[0], noise[0], emb, modulation_weight)
    mods = [part] + [shifted(part, "seq", k) for k in range(1, n)]
    noisy_parts = [noisy] + [shifted(noisy, "seq", k) for k in range(1, n)]
    words = text[0]
    text_parts = [words] + [shifted(words, "seq", k) for k in range(1, n)]
    origin = [lax.rem(me + n - k, n) for k in range(n)]
    ordered = [
        functools.reduce(
            lambda so_far, k: jnp.where(origin[k] == j, mods[k], so_far), range(1, n), mods[0]
        )
        for j in range(n)
    ]
    mod = jnp.concatenate(ordered, 1)
    img_part, txt_part = noisy.shape[0], words.shape[0]
    place = jnp.concatenate(
        [jnp.zeros((n * img_part,), jnp.int32)]
        + [origin[k] * txt_part + jnp.arange(txt_part, dtype=jnp.int32) for k in range(n)]
    )
    bias = jnp.where(place < text_token_length[0], 0.0, -1000000000.0).astype(F32)[None]
    core = lax.rem(lax.axis_index("grp"), 2).astype(jnp.int32)
    gain = query_key_norm_gain
    image_weight = held(image_projection_weight)
    text_steps = split(text_projection_weight.shape[1] // (2 * HD))[1]
    text_weight = fetch(held(text_projection_weight), text_steps, part)
    down = adapter_down_weight.T

    def text_part(k, after):
        return project_text(k, n, text_heads, mod, gain, text_weight, text_parts[k], after)

    def image_part(k, after):
        return project_image(
            k, n, image_heads, mod, gain, down, adapter_up_weight, image_weight, noisy_parts[k], after
        )

    text_heads, image_heads = [], []
    text_heads = text_part(0, None)
    *image_heads, image_weight = image_part(0, text_heads[0])
    for k in range(1, n):
        image_heads = image_part(k, None)
        text_heads = text_part(k, image_heads[0])
    send_a, keep_a, send_b, keep_b, loss = attend(
        core[None], bias, gain, adapter_up_weight, image_heads, text_heads
    )
    (got_a,), (got_b,) = swap([send_a], "grp", 1), swap([send_b], "grp", 1)
    grad_a, grad_b = keep_a + got_a.astype(F32), keep_b + got_b.astype(F32)
    seq_dims, dp_dims = [], []
    for bit in reversed(bits("seq")):
        seq_dims.append(cut_of(grad_a))
        (grad_a,) = halve([grad_a], "seq", bit, BF16)
    x_dims = [cut_of(grad_a), cut_of(grad_b)]
    (grad_b,) = halve([grad_b], "grp", 2, BF16)
    (grad_a,) = halve([grad_a], "grp", 2, BF16)
    for bit in bits("dp"):
        dp_dims.append([cut_of(grad_a), cut_of(grad_b)])
        grad_a, grad_b = halve([grad_a, grad_b], "dp", bit, F32)
    squares = fold(grad_b * grad_b)
    squares = jnp.pad(squares, ((0, 8 - squares.shape[0]), (0, 0)))
    sums = jnp.concatenate([fold(loss), squares], 1)
    grads = [grad_a.astype(BF16), grad_b.astype(BF16)]
    for bit in reversed(bits("dp")):
        grads, sums = rejoin(grads, dp_dims.pop(), sums, "dp", bit)
    grads, sums = rejoin(grads, x_dims, sums, "grp", 2)
    for bit in bits("seq"):
        (grads[0],), sums = rejoin(grads[:1], [seq_dims.pop()], sums, "seq", bit)
    grads, sums = rejoin(grads, [0, 0], sums, "grp", 1)
    direction_a, direction_b, loss_mean = finish(
        *grads, sums, n, samples * n * img_part * HEADS * HD
    )
    return (direction_a.T, direction_b, loss_mean[0, 0])


def solution(mesh):
    in_specs = (
        P(("grp", "dp"), "seq", None),
        P(("grp", "dp"), "seq", None),
        P(("grp", "dp"), "seq", None),
        P(("grp", "dp")),
        P(("grp", "dp")),
        P(("grp", "dp")),
        P(None, "seq"),
        P(None, "seq"),
        P(None, "seq"),
        P(),
        P(),
        P(None, "seq"),
    )
    out_specs = (P(), P(None, "seq"), P())
    return jax.shard_map(
        on_device, mesh=mesh, in_specs=in_specs, out_specs=out_specs, check_vma=False
    )
```

```python
import functools
import math

import jax
import jax.numpy as jnp
from jax import lax
from jax.experimental import pallas as pl
from jax.experimental.pallas import tpu as pltpu
from jax.sharding import PartitionSpec as P

HD = 128
HEADS = 16
STEPS = 1000
EPS = 1e-06
F32 = jnp.float32
BF16 = jnp.bfloat16
ROOT = 1.0 / math.sqrt(HD)
LOG2E = 1.0 / math.log(2.0)
SMALL = 10 * 1024 * 1024


def timing(value, width):
    count = width // 4
    freqs = jnp.exp(-math.log(10000.0) * jnp.arange(count, dtype=F32) / count)
    angles = 1000.0 * value * freqs
    return jnp.concatenate([jnp.cos(angles), jnp.sin(angles)])


def nn(a, b):
    return lax.dot_general(a, b, (((1,), (0,)), ((), ())), preferred_element_type=F32)


def nt(a, b):
    return lax.dot_general(a, b, (((1,), (1,)), ((), ())), preferred_element_type=F32)


def tn(a, b):
    return lax.dot_general(a, b, (((0,), (0,)), ((), ())), preferred_element_type=F32)


def over(total, size, body):
    if total == size:
        body(0)
    else:

        @pl.loop(0, total // size)
        def _(i):
            body(pl.multiple_of(i * size, size))


def inverse_rms(x):
    return lax.rsqrt(jnp.mean(x * x, axis=-1, keepdims=True) + EPS)


def norm_pull(x, gain, dy):
    r = inverse_rms(x)
    u = gain * dy
    return r * (u - x * (r * r * jnp.mean(x * u, axis=-1, keepdims=True)))


def modulate(tokens, mod_ref, kind, width, dest, rows, base):
    size = tokens.shape[0]

    @pl.loop(0, size // 16)
    def _(i):
        v = tokens[pl.ds(pl.multiple_of(i * 16, 16), 16), :].astype(F32)
        center = v - jnp.mean(v, axis=1, keepdims=True)
        spread = jnp.mean(center * center, axis=1, keepdims=True)
        unit = center * lax.rsqrt(spread + EPS)
        for m in range(2):
            shift = mod_ref[m : m + 1, kind * width : (kind + 1) * width]
            scale = mod_ref[m : m + 1, (kind + 1) * width : (kind + 2) * width]
            at = pl.multiple_of(m * rows + base + i * 16, 16)
            dest[pl.ds(at, 16), :] = (unit * (1.0 + scale) + shift).astype(BF16)


def normed(x, gain):
    return (x * inverse_rms(x) * gain).astype(BF16)


def fetches(w_ref, out_ref, sems):
    cols = w_ref.shape[1] // sems.shape[0]
    return [
        pltpu.make_async_copy(
            w_ref.at[:, i * cols : (i + 1) * cols], out_ref.at[:, i * cols : (i + 1) * cols], sems.at[i]
        )
        for i in range(sems.shape[0])
    ]


def held(x):
    return pltpu.with_memory_space_constraint(x, pltpu.HBM)


def text_kernel(n, pair, mod_ref, gain_ref, w_ref, after_ref, *refs):
    parts, (k_ref, v_ref, ht, weights, sems) = refs[:n], refs[n:]
    copies = fetches(w_ref, weights, sems)
    for copy in copies:
        copy.start()
    rows = n * parts[0].shape[0]
    for k in range(n):
        modulate(parts[k], mod_ref, 2, w_ref.shape[0], ht, rows, k * parts[0].shape[0])
    cols = pair * 2 * HD
    size = min(rows, 96)
    for step, copy in enumerate(copies):
        copy.wait()

        def project(start, step=step):
            w = weights[:, step * cols : (step + 1) * cols]
            if size == rows:
                both = nn(ht[...], w)
                own = [both[:rows], both[rows:]]
            else:
                own = [nn(ht[pl.ds(m * rows + start, size), :], w) for m in range(2)]
            for m, kv in enumerate(own):
                for j in range(pair):
                    head, c = step * pair + j, j * 2 * HD
                    k_ref[head, m, pl.ds(start, size), :] = normed(kv[:, c : c + HD], gain_ref[2:3, :])
                    v_ref[head, m, pl.ds(start, size), :] = kv[:, c + HD : c + 2 * HD].astype(BF16)

        over(rows, size, project)


def split(count):
    pair = 2 if count % 2 == 0 else 1
    return pair, count // pair


def params(mib):
    return pltpu.CompilerParams(
        dimension_semantics=("arbitrary",), vmem_limit_bytes=mib * 1024 * 1024
    )


VMEM = pl.BlockSpec(memory_space=pltpu.VMEM)
HELD = pl.BlockSpec(memory_space=pltpu.HBM)


def project_text(mod, gain, w, after, parts):
    n, (part, width) = len(parts), parts[0].shape
    pair, steps = split(w.shape[1] // (2 * HD))
    out = pltpu.VMEM((pair * steps, 2, n * part, HD), BF16)
    return pl.pallas_call(
        functools.partial(text_kernel, n, pair),
        in_specs=[VMEM, VMEM, HELD, pl.BlockSpec(memory_space=pl.ANY)] + [VMEM] * n,
        out_specs=[VMEM] * 2,
        out_shape=[out, out],
        scratch_shapes=[
            pltpu.VMEM((2 * n * part, width), BF16),
            pltpu.VMEM(w.shape, w.dtype),
            pltpu.SemaphoreType.DMA((steps,)),
        ],
        compiler_params=pltpu.CompilerParams(vmem_limit_bytes=2 * SMALL),
        cost_estimate=pl.CostEstimate(
            flops=4 * n * part * w.size, bytes_accessed=2 * w.size, transcendentals=0
        ),
        name="project_text",
    )(mod, gain, w, after, *parts)


def image_kernel(pair, index, past, mod_ref, gain_ref, down_ref, up_ref, w_ref, tokens, *refs):
    first = past == 0
    q_ref, k_ref, v_ref, x_ref, low_ref, hs_ref, *rest = refs[past:]
    weights, copies = w_ref, None
    if first:
        weights, hi, sems = rest
        copies = fetches(w_ref, weights, sems)
        for copy in copies:
            copy.start()
    else:
        (hi,) = rest
    rows = tokens.shape[0]
    part = slice(index * rows, (index + 1) * rows)
    modulate(tokens, mod_ref, 0, w_ref.shape[0], hi, rows, 0)
    hs_ref[part, :] = hi[rows:, :]
    low_ref[part, :] = nt(hi[rows:, :], down_ref[...]).astype(BF16)
    cols = pair * 3 * HD

    def project(step):
        columns = pl.ds(step * cols, cols)
        if not isinstance(step, int):
            columns = pl.ds(pl.multiple_of(step * cols, cols), cols)
        qkv = nn(hi[...], weights[:, columns])
        student = qkv[rows:] + nn(low_ref[part, :], up_ref[:, columns])
        for j in range(pair):
            head, c = step * pair + j, j * 3 * HD
            for m, own in enumerate((qkv[:rows], student)):
                q, k = own[:, c : c + HD], own[:, c + HD : c + 2 * HD]
                q_ref[head, m, part, :] = normed(q, gain_ref[0:1, :])
                k_ref[head, m, part, :] = normed(k, gain_ref[1:2, :])
                v_ref[head, m, part, :] = own[:, c + 2 * HD : c + 3 * HD].astype(BF16)
                if m == 1:
                    x_ref[head, 0, part, :] = q
                    x_ref[head, 1, part, :] = k

    if copies is None:
        pl.loop(0, w_ref.shape[1] // cols)(project)
    else:
        for step, copy in enumerate(copies):
            copy.wait()
            project(step)


def project_image(part, n, before, mod, gain, down, up, w, tokens):
    (rows, width), rank = tokens.shape, up.shape[0]
    pair, steps = split(w.shape[1] // (3 * HD))
    heads = (pair * steps, 2, n * rows, HD)
    shapes = [pltpu.VMEM(heads, BF16)] * 3 + [
        pltpu.VMEM(heads, F32),
        pltpu.VMEM((n * rows, rank), BF16),
        pltpu.VMEM((n * rows, width), BF16),
    ]
    scratch = [pltpu.VMEM((2 * rows, width), BF16)]
    if not before:
        shapes.append(pltpu.VMEM(w.shape, w.dtype))
        scratch.append(pltpu.SemaphoreType.DMA((steps,)))
    return pl.pallas_call(
        functools.partial(image_kernel, pair, part, len(before)),
        in_specs=[VMEM] * 4
        + [VMEM if before else HELD]
        + [VMEM] * (1 + len(before)),
        out_specs=[VMEM] * len(shapes),
        out_shape=shapes,
        input_output_aliases={6 + i: i for i in range(len(before))},
        scratch_shapes=scratch,
        compiler_params=pltpu.CompilerParams(vmem_limit_bytes=SMALL),
        cost_estimate=pl.CostEstimate(
            flops=4 * rows * w.size, bytes_accessed=2 * w.size, transcendentals=0
        ),
        name="project_image",
    )(mod, gain, down, up, w, tokens, *before)


def attend_kernel(
    steps, pair, samples, where_ref, bias_ref, gain_ref, up_ref, q_ref, k_ref, v_ref, x_ref, kt_ref, vt_ref,
    low_ref, hs_ref, send_a, keep_a, send_b, keep_b, loss_ref, lowt, glt, k_s, v_s, dk_s, dv_s, gq, whole
):
    core = where_ref[0]
    half = send_a.shape[0]
    lowt[...] = low_ref[...].astype(F32).T.astype(BF16)
    glt[...] = jnp.zeros_like(glt)
    loss_ref[...] = jnp.zeros_like(loss_ref)

    def share(value, columns, send, keep):
        whole[:, : value.shape[1]] = value
        mine = pl.ds(pl.multiple_of(core * half, 8), half)
        other = pl.ds(pl.multiple_of((1 - core) * half, 8), half)
        keep[:, columns] = whole[mine, : value.shape[1]]
        send[:, columns] = whole[other, : value.shape[1]].astype(send.dtype)

    @pl.loop(0, steps)
    def _(step):
        columns = pl.ds(pl.multiple_of(step * gq.shape[1], HD), gq.shape[1])
        group = pl.ds(step * pair, pair)
        attend_heads(
            pair, samples, bias_ref, gain_ref, *[r.at[group] for r in (q_ref, k_ref, v_ref, x_ref, kt_ref, vt_ref)],
            loss_ref, k_s, v_s, dk_s, dv_s, gq,
        )
        share(nn(lowt[...], gq[...]), columns, send_b, keep_b)
        glt[...] += nt(up_ref[:, columns], gq[...])

    g = glt[...]
    g1 = g.astype(BF16)
    rest = g - g1.astype(F32)
    g2 = rest.astype(BF16)
    g3 = (rest - g2.astype(F32)).astype(BF16)
    stack = jnp.concatenate([g1, g2, g3], 0)
    rank = g.shape[0]
    full = nn(stack, hs_ref[...])
    share(full[:rank] + full[rank : 2 * rank] + full[2 * rank :], slice(0, full.shape[1]), send_a, keep_a)


def attend_heads(
    pair, samples, bias_ref, gain_ref, q_ref, k_ref, v_ref, x_ref, kt_ref, vt_ref, loss_ref, k_s, v_s, dk_s, dv_s, gq
):
    rows = q_ref.shape[2]
    block = min(rows, 160)
    heads = range(pair)
    for j in heads:
        for m in range(2):
            k_s[j, m, :rows, :] = k_ref[j, m]
            k_s[j, m, rows:, :] = kt_ref[j, m]
            v_s[j, m, :rows, :] = v_ref[j, m]
            v_s[j, m, rows:, :] = vt_ref[j, m]
    if rows > block:
        dk_s[...] = jnp.zeros_like(dk_s)
        dv_s[...] = jnp.zeros_like(dv_s)
    gain_q, gain_k = gain_ref[0:1, :], gain_ref[1:2, :]

    def attend(start):
        at = pl.ds(start, block)
        both = [(j, m) for j in heads for m in range(2)]
        scores = {(j, m): nt(q_ref[j, m, at, :], k_s[j, m]) for j, m in both}
        weights = {i: jnp.exp2(scores[i] * (ROOT * LOG2E) + bias_ref[...]) for i in both}
        scale = {i: 1.0 / jnp.sum(weights[i], axis=1, keepdims=True) for i in both}
        probs = {i: weights[i] * scale[i] for i in both}
        rounded = {i: probs[i].astype(BF16) for i in both}
        out = {(j, m): nn(rounded[j, m], v_s[j, m]) for j, m in both}
        diff = [out[j, 1] - out[j, 0].astype(BF16).astype(F32) for j in heads]
        total = diff[0] * diff[0]
        for d in diff[1:]:
            total = total + d * d
        loss_ref[...] += jnp.sum(total.reshape(block // 8, 8, HD), axis=0)
        dout = [(d * (2.0 / samples)).astype(BF16) for d in diff]
        dprobs = [nt(dout[j], v_s[j, 1]).astype(BF16).astype(F32) for j in heads]
        dv = [tn(rounded[j, 1], dout[j]) for j in heads]
        inner = [jnp.sum(dprobs[j] * probs[j, 1], axis=1, keepdims=True) for j in heads]
        dscores = [(probs[j, 1] * (dprobs[j] - inner[j]) * ROOT).astype(BF16) for j in heads]
        dq = [nn(dscores[j], k_s[j, 1]).astype(BF16).astype(F32) for j in heads]
        dk = [tn(dscores[j], q_ref[j, 1, at, :]) for j in heads]
        for j in heads:
            c = j * 3 * HD
            gq[at, c : c + HD] = norm_pull(x_ref[j, 0, at, :], gain_q, dq[j]).astype(BF16)
            if rows > block:
                dk_s[j] += dk[j][:rows]
                dv_s[j] += dv[j][:rows]
            else:
                dk_s[j] = dk[j][:rows]
                dv_s[j] = dv[j][:rows]

    over(rows, block, attend)

    def rest(start):
        at = pl.ds(start, block)
        for j in heads:
            c = j * 3 * HD
            dk = dk_s[j, at, :].astype(BF16).astype(F32)
            gq[at, c + HD : c + 2 * HD] = norm_pull(x_ref[j, 1, at, :], gain_k, dk).astype(BF16)
            gq[at, c + 2 * HD : c + 3 * HD] = dv_s[j, at, :].astype(BF16)

    over(rows, block, rest)


def attend(where, bias, gain, up, image, text):
    q, k, v, x, low, hs = image
    kt, vt = text
    (rank, img_cols), width = up.shape, hs.shape[1]
    count, _, rows, _ = q.shape
    trows = kt.shape[2]
    pair, steps = split(count)
    half, ic = rank // 2, pair * 3 * HD
    samples = lax.axis_size("grp") * lax.axis_size("dp")
    out_a, out_b = (half, width), (half, img_cols)
    return pl.pallas_call(
        functools.partial(attend_kernel, steps, pair, samples),
        in_specs=[pl.BlockSpec(memory_space=pltpu.SMEM)] + [VMEM] * 11,
        out_specs=[VMEM] * 5,
        out_shape=[
            jax.ShapeDtypeStruct(out_a, BF16),
            jax.ShapeDtypeStruct(out_a, F32),
            jax.ShapeDtypeStruct(out_b, BF16),
            jax.ShapeDtypeStruct(out_b, F32),
            jax.ShapeDtypeStruct((8, HD), F32),
        ],
        scratch_shapes=[
            pltpu.VMEM((rank, rows), BF16),
            pltpu.VMEM((rank, rows), F32),
            pltpu.VMEM((pair, 2, rows + trows, HD), BF16),
            pltpu.VMEM((pair, 2, rows + trows, HD), BF16),
            pltpu.VMEM((pair, rows, HD), F32),
            pltpu.VMEM((pair, rows, HD), F32),
            pltpu.VMEM((rows, ic), BF16),
            pltpu.VMEM((rank, max(width, ic)), F32),
        ],
        compiler_params=pltpu.CompilerParams(vmem_limit_bytes=2 * SMALL),
        cost_estimate=pl.CostEstimate(
            flops=16 * count * rows * (rows + trows) * HD,
            bytes_accessed=8_000_000,
            transcendentals=2 * count * rows * (rows + trows),
        ),
        name="attend",
    )(where, bias, gain, up, q, k, v, x, kt, vt, low, hs)


def start_kernel(sigma_ref, image_ref, noise_ref, emb_ref, weight_ref, noisy_ref, part_ref):
    sigma = sigma_ref[0]
    clean, noise = image_ref[...].astype(F32), noise_ref[...].astype(F32)
    noisy_ref[...] = ((1.0 - sigma) * clean + sigma * noise).astype(BF16)
    part_ref[...] = nn(emb_ref[...], weight_ref[...])[: part_ref.shape[0]]


def start(sigma, image, noise, emb, weight):
    rows, width = image.shape
    depth, cols = weight.shape
    steps = 2 if width % 256 == 0 and cols % 256 == 0 else 1
    tokens = pl.BlockSpec((rows, width // steps), lambda s: (0, s))
    return pl.pallas_call(
        start_kernel,
        grid=(steps,),
        in_specs=[
            pl.BlockSpec(memory_space=pltpu.SMEM),
            tokens,
            tokens,
            pl.BlockSpec(emb.shape, lambda s: (0, 0)),
            pl.BlockSpec((depth, cols // steps), lambda s: (0, s)),
        ],
        out_specs=[tokens, pl.BlockSpec((2, cols // steps), lambda s: (0, s))],
        out_shape=[
            jax.ShapeDtypeStruct((rows, width), BF16),
            jax.ShapeDtypeStruct((2, cols), F32),
        ],
        compiler_params=params(10),
        cost_estimate=pl.CostEstimate(
            flops=4 * depth * cols, bytes_accessed=2 * weight.size + 6 * image.size, transcendentals=0
        ),
        name="start",
    )(sigma, held(image), held(noise), emb, held(weight))


def finish_kernel(scale_a, scale_b, scale_loss, side_ref, a_ref, b_ref, sums_ref, got_ref, out_a, out_b, loss_ref):
    half = HD // 2
    rows, width, cols = a_ref.shape[0], a_ref.shape[1], b_ref.shape[1]
    at = rows // 8 * (width + cols)
    other = [got_ref[:, at + i * HD : at + (i + 1) * HD].astype(F32) for i in range(3)]
    total = jnp.sum(sums_ref[...] + (other[0] + other[1] + other[2]), axis=0, keepdims=True)
    loss_ref[...] = jnp.sum(total[:, :half], axis=1, keepdims=True) * scale_loss
    squares_b = jnp.sum(total[:, half:], axis=1, keepdims=True) * scale_b
    unit_b = lax.rsqrt(squares_b + EPS)
    blocks = range(rows // 8)
    mine = [lambda b=b: a_ref[8 * b : 8 * b + 8, :].astype(F32) for b in blocks]
    theirs = [lambda b=b: got_ref[:, b * width : (b + 1) * width].astype(F32) for b in blocks]

    def squares(parts):
        each = functools.reduce(lambda x, y: x + y, [p() * p() for p in parts])
        return jnp.sum(jnp.sum(each, axis=0, keepdims=True), axis=1, keepdims=True)

    unit_a = lax.rsqrt((squares(mine) + squares(theirs)) * scale_a + EPS)
    side = side_ref[0]
    at = rows // 8 * width
    for b in blocks:
        own = pl.ds(pl.multiple_of(side * rows + 8 * b, 8), 8)
        far = pl.ds(pl.multiple_of((1 - side) * rows + 8 * b, 8), 8)
        out_a[own, :] = mine[b]() * unit_a
        out_a[far, :] = theirs[b]() * unit_a
        out_b[own, :] = b_ref[8 * b : 8 * b + 8, :].astype(F32) * unit_b
        out_b[far, :] = got_ref[:, at + b * cols : at + (b + 1) * cols].astype(F32) * unit_b


def finish(side, grad_a, grad_b, sums, got, n, entries):
    (half, width), cols = grad_a.shape, grad_b.shape[1]
    rank = 2 * half
    return pl.pallas_call(
        functools.partial(finish_kernel, 1.0 / (rank * width), 1.0 / (rank * cols * n), 1.0 / entries),
        in_specs=[pl.BlockSpec(memory_space=pltpu.SMEM)] + [VMEM] * 4,
        out_shape=[
            jax.ShapeDtypeStruct((rank, width), F32),
            jax.ShapeDtypeStruct((rank, cols), F32),
            jax.ShapeDtypeStruct((1, 1), F32),
        ],
        name="finish",
    )(side, grad_a, grad_b, sums, got)


def shifted(x, axis, k):
    size = lax.axis_size(axis)
    return lax.ppermute(x, axis, [(i, (i + k) % size) for i in range(size)])


def packed(arrays):
    return len(arrays) > 1 and all(x.shape[0] % 8 == 0 and x.shape[1] % HD == 0 for x in arrays)


def pack(arrays):
    return jnp.concatenate([x[r : r + 8] for x in arrays for r in range(0, x.shape[0], 8)], 1)


def unpack(message, arrays):
    out, at = [], 0
    for x in arrays:
        blocks = []
        for _ in range(0, x.shape[0], 8):
            blocks.append(message[:, at : at + x.shape[1]])
            at += x.shape[1]
        out.append(blocks[0] if len(blocks) == 1 else jnp.concatenate(blocks, 0))
    return out


def send(arrays, group, hop):
    pairs = [(i, i ^ group.mask(hop)) for i in range(group.size)]
    if not packed(arrays):
        return [lax.ppermute(x, group.axes, pairs) for x in arrays]
    return unpack(lax.ppermute(pack(arrays), group.axes, pairs), arrays)


class Group:
    def __init__(self, *places):
        self.axes = tuple(a for a in ("grp", "seq", "dp") if any(a == p[0] for p in places))
        self.size = math.prod(lax.axis_size(a) for a in self.axes)
        self.places = places
        self.count = 1 << len(places)
        sides = [lax.rem(lax.div(lax.axis_index(a), bit), 2) for a, bit in places]
        self.me = functools.reduce(lambda total, side: 2 * total + side, sides, 0)

    def mask(self, hop):
        total = 0
        for i, (axis, bit) in enumerate(reversed(self.places)):
            if hop >> i & 1:
                below = self.axes[self.axes.index(axis) + 1 :]
                total ^= bit * math.prod(lax.axis_size(a) for a in below)
        return total


def cut_of(x, count):
    if x.shape[0] % (8 * count) == 0:
        return 0
    return 1 if x.shape[1] % (count * HD) == 0 else 0


def block(x, dim, count, index):
    each = x.shape[dim] // count
    return lax.dynamic_slice_in_dim(x, index * each, each, dim)


def scatter(wide, narrow=()):
    arrays, group = wide
    more, part = narrow or ([], None)
    dims = [cut_of(x, group.count) for x in arrays]
    more_dims = [cut_of(x, part.count) for x in more]
    sums = [block(x, d, group.count, group.me) for x, d in zip(arrays, dims)]
    more_sums = [block(x, d, part.count, part.me) for x, d in zip(more, more_dims)]
    for hop in range(1, group.count):
        out = [block(x, d, group.count, group.me ^ hop).astype(BF16) for x, d in zip(arrays, dims)]
        join = part is not None and hop < part.count
        if join:
            out += [block(x, d, part.count, part.me ^ hop).astype(BF16) for x, d in zip(more, more_dims)]
        got = [g.astype(F32) for g in send(out, group, hop)]
        sums = [t + g for t, g in zip(sums, got)]
        if join:
            more_sums = [t + g for t, g in zip(more_sums, got[len(sums) :])]
    return sums, dims, more_sums, more_dims


def ordered(parts, me):
    return [
        functools.reduce(
            lambda so_far, hop: jnp.where(me == j ^ hop, parts[hop], so_far), range(1, len(parts)), parts[0]
        )
        for j in range(len(parts))
    ]


def gather(wide, sums, narrow=()):
    arrays, dims, group = wide
    more, more_dims, part = narrow or ([], [], None)
    parts = [[x] for x in arrays]
    more_parts = [[x] for x in more]
    totals = [sums]
    for hop in range(1, group.count):
        join = part is not None and hop < part.count
        out = [*arrays, *(more if join else []), pieces(sums)]
        *got, other = send(out, group, hop)
        other = other.astype(F32)
        totals.append(other[:, :HD] + other[:, HD : 2 * HD] + other[:, 2 * HD :])
        for so_far, g in zip(parts + (more_parts if join else []), got):
            so_far.append(g)
    totals = ordered(totals, group.me)
    sums = functools.reduce(lambda x, y: x + y, totals)
    whole = [jnp.concatenate(ordered(p, group.me), d) for p, d in zip(parts, dims)]
    more_whole = [jnp.concatenate(ordered(p, part.me), d) for p, d in zip(more_parts, more_dims)]
    return whole, more_whole, sums


def pieces(value):
    first = lax.reduce_precision(value, 8, 7)
    rest = value - first
    second = lax.reduce_precision(rest, 8, 7)
    return jnp.concatenate([first, second, rest - second], 1).astype(BF16)


def bits(axis):
    size = lax.axis_size(axis)
    return [1 << i for i in range(size.bit_length() - 1)]


def fold(x):
    half = HD // 2
    return functools.reduce(
        lambda total, c: total + x[:, c : c + half], range(half, x.shape[1], half), x[:, :half]
    )


def on_device(
    image,
    noise,
    text,
    timestep,
    guidance,
    text_token_length,
    image_projection_weight,
    text_projection_weight,
    modulation_weight,
    query_key_norm_gain,
    adapter_down_weight,
    adapter_up_weight,
):
    emb_width = modulation_weight.shape[0]
    n, me = lax.axis_size("seq"), lax.axis_index("seq")
    samples = lax.axis_size("grp") * lax.axis_size("dp")
    sigma = (timestep[0].astype(F32) + 1.0) / STEPS
    time = timing(sigma, emb_width)
    guide = jnp.where(jnp.arange(16)[:, None] == 0, timing(guidance[0], emb_width)[None], 0.0)
    emb = jnp.concatenate([jnp.broadcast_to(time[None], guide.shape), guide], 1)
    emb = jax.nn.silu(emb).astype(BF16)
    noisy, part = start(sigma[None], image[0], noise[0], emb, modulation_weight)
    mods = [part] + [shifted(part, "seq", k) for k in range(1, n)]
    noisy_parts = [noisy] + [shifted(noisy, "seq", k) for k in range(1, n)]
    words = text[0]
    text_parts = [words] + [shifted(words, "seq", k) for k in range(1, n)]
    origin = [lax.rem(me + n - k, n) for k in range(n)]
    ordered = [
        functools.reduce(
            lambda so_far, k: jnp.where(origin[k] == j, mods[k], so_far), range(1, n), mods[0]
        )
        for j in range(n)
    ]
    mod = jnp.concatenate(ordered, 1)
    img_part, txt_part = noisy.shape[0], words.shape[0]
    place = jnp.concatenate(
        [jnp.zeros((n * img_part,), jnp.int32)]
        + [origin[k] * txt_part + jnp.arange(txt_part, dtype=jnp.int32) for k in range(n)]
    )
    bias = jnp.where(place < text_token_length[0], 0.0, -1000000000.0).astype(F32)[None]
    core = lax.rem(lax.axis_index("grp"), 2).astype(jnp.int32)
    gain = query_key_norm_gain
    down = adapter_down_weight.T
    image_weight, image_heads = held(image_projection_weight), []
    for k in range(n):
        image_heads = project_image(
            k, n, image_heads, mod, gain, down, adapter_up_weight, image_weight, noisy_parts[k]
        )
        if k == 0:
            *image_heads, image_weight = image_heads
    text_heads = project_text(mod, gain, held(text_projection_weight), image_heads[0], text_parts)
    send_a, keep_a, send_b, keep_b, loss = attend(
        core[None], bias, gain, adapter_up_weight, image_heads, text_heads
    )
    cores = Group(("grp", 1))
    (got_a,), (got_b,) = send([send_a], cores, 1), send([send_b], cores, 1)
    grad_a, grad_b = keep_a + got_a.astype(F32), keep_b + got_b.astype(F32)
    last, *far = bits("seq")
    far = [(Group(("seq", bit)), []) for bit in reversed(far)]
    for group, dims in far:
        (grad_a,), dims[:], _, _ = scatter(([grad_a], group))
    near, across = Group(("seq", last), ("grp", 2)), Group(("grp", 2))
    (grad_a,), dims_a, (grad_b,), dims_b = scatter(([grad_a], near), ([grad_b], across))
    line = Group(*[("dp", bit) for bit in reversed(bits("dp"))])
    (grad_a, grad_b), dims_z, _, _ = scatter(([grad_a, grad_b], line))
    squares = fold(jnp.sum(grad_b.reshape(-1, min(grad_b.shape[0], 8), grad_b.shape[1]) ** 2, 0))
    squares = jnp.pad(squares, ((0, 8 - squares.shape[0]), (0, 0)))
    sums = jnp.concatenate([fold(loss), squares], 1)
    grads, _, sums = gather(([grad_a.astype(BF16), grad_b.astype(BF16)], dims_z, line), sums)
    (grad_a,), (grad_b,), sums = gather(
        (grads[:1], dims_a, near), sums, (grads[1:], dims_b, across)
    )
    for group, dims in reversed(far):
        (grad_a,), _, sums = gather(([grad_a], dims, group), sums)
    pairs = [(i, i ^ 1) for i in range(cores.size)]
    got = lax.ppermute(pack([grad_a, grad_b, pieces(sums)]), "grp", pairs)
    direction_a, direction_b, loss_mean = finish(
        core[None], grad_a, grad_b, sums, got, n, samples * n * img_part * HEADS * HD
    )
    return (direction_a.T, direction_b, loss_mean[0, 0])


def solution(mesh):
    in_specs = (
        P(("grp", "dp"), "seq", None),
        P(("grp", "dp"), "seq", None),
        P(("grp", "dp"), "seq", None),
        P(("grp", "dp")),
        P(("grp", "dp")),
        P(("grp", "dp")),
        P(None, "seq"),
        P(None, "seq"),
        P(None, "seq"),
        P(),
        P(),
        P(None, "seq"),
    )
    out_specs = (P(), P(None, "seq"), P())
    return jax.shard_map(
        on_device, mesh=mesh, in_specs=in_specs, out_specs=out_specs, check_vma=False
    )
```

```python
import functools
import math

import jax
import jax.numpy as jnp
from jax import lax
from jax.experimental import pallas as pl
from jax.experimental.pallas import tpu as pltpu
from jax.sharding import PartitionSpec as P

HD = 128
HEADS = 16
STEPS = 1000
EPS = 1e-06
F32 = jnp.float32
BF16 = jnp.bfloat16
ROOT = 1.0 / math.sqrt(HD)
LOG2E = 1.0 / math.log(2.0)
SMALL = 10 * 1024 * 1024


def timing(value, width):
    count = width // 4
    freqs = jnp.exp(-math.log(10000.0) * jnp.arange(count, dtype=F32) / count)
    angles = 1000.0 * value * freqs
    return jnp.concatenate([jnp.cos(angles), jnp.sin(angles)])


def nn(a, b):
    return lax.dot_general(a, b, (((1,), (0,)), ((), ())), preferred_element_type=F32)


def nt(a, b):
    return lax.dot_general(a, b, (((1,), (1,)), ((), ())), preferred_element_type=F32)


def tn(a, b):
    return lax.dot_general(a, b, (((0,), (0,)), ((), ())), preferred_element_type=F32)


def over(total, size, body):
    if total == size:
        body(0)
    else:

        @pl.loop(0, total // size)
        def _(i):
            body(pl.multiple_of(i * size, size))


def inverse_rms(x):
    return lax.rsqrt(jnp.mean(x * x, axis=-1, keepdims=True) + EPS)


def norm_pull(x, gain, dy):
    r = inverse_rms(x)
    u = gain * dy
    return r * (u - x * (r * r * jnp.mean(x * u, axis=-1, keepdims=True)))


def modulate(tokens, mod_ref, kind, width, dest, rows, base):
    size = tokens.shape[0]

    @pl.loop(0, size // 16)
    def _(i):
        v = tokens[pl.ds(pl.multiple_of(i * 16, 16), 16), :].astype(F32)
        center = v - jnp.mean(v, axis=1, keepdims=True)
        spread = jnp.mean(center * center, axis=1, keepdims=True)
        unit = center * lax.rsqrt(spread + EPS)
        for m in range(2):
            shift = mod_ref[m : m + 1, kind * width : (kind + 1) * width]
            scale = mod_ref[m : m + 1, (kind + 1) * width : (kind + 2) * width]
            at = pl.multiple_of(m * rows + base + i * 16, 16)
            dest[pl.ds(at, 16), :] = (unit * (1.0 + scale) + shift).astype(BF16)


def normed(x, gain):
    return (x * inverse_rms(x) * gain).astype(BF16)


def fetches(w_ref, out_ref, sems):
    cols = w_ref.shape[1] // sems.shape[0]
    return [
        pltpu.make_async_copy(
            w_ref.at[:, i * cols : (i + 1) * cols], out_ref.at[:, i * cols : (i + 1) * cols], sems.at[i]
        )
        for i in range(sems.shape[0])
    ]


def held(x):
    return pltpu.with_memory_space_constraint(x, pltpu.HBM)


def text_kernel(n, pair, mod_ref, gain_ref, w_ref, after_ref, *refs):
    parts, (k_ref, v_ref, ht, weights, sems) = refs[:n], refs[n:]
    copies = fetches(w_ref, weights, sems)
    for copy in copies:
        copy.start()
    rows = n * parts[0].shape[0]
    for k in range(n):
        modulate(parts[k], mod_ref, 2, w_ref.shape[0], ht, rows, k * parts[0].shape[0])
    cols = pair * 2 * HD
    size = min(rows, 96)
    for step, copy in enumerate(copies):
        copy.wait()

        def project(start, step=step):
            for j in range(pair):
                head, c = step * pair + j, step * cols + j * 2 * HD
                w = weights[:, c : c + 2 * HD]
                if size == rows:
                    both = nn(ht[...], w)
                    own = [both[:rows], both[rows:]]
                else:
                    own = [nn(ht[pl.ds(m * rows + start, size), :], w) for m in range(2)]
                for m, kv in enumerate(own):
                    k_ref[head, m, pl.ds(start, size), :] = normed(kv[:, :HD], gain_ref[2:3, :])
                    v_ref[head, m, pl.ds(start, size), :] = kv[:, HD:].astype(BF16)

        over(rows, size, project)


def split(count):
    pair = 2 if count % 2 == 0 else 1
    return pair, count // pair


def params(mib):
    return pltpu.CompilerParams(
        dimension_semantics=("arbitrary",), vmem_limit_bytes=mib * 1024 * 1024
    )


VMEM = pl.BlockSpec(memory_space=pltpu.VMEM)
HELD = pl.BlockSpec(memory_space=pltpu.HBM)


def project_text(mod, gain, w, after, parts):
    n, (part, width) = len(parts), parts[0].shape
    pair, steps = split(w.shape[1] // (2 * HD))
    out = pltpu.VMEM((pair * steps, 2, n * part, HD), BF16)
    return pl.pallas_call(
        functools.partial(text_kernel, n, pair),
        in_specs=[VMEM, VMEM, HELD, pl.BlockSpec(memory_space=pl.ANY)] + [VMEM] * n,
        out_specs=[VMEM] * 2,
        out_shape=[out, out],
        scratch_shapes=[
            pltpu.VMEM((2 * n * part, width), BF16),
            pltpu.VMEM(w.shape, w.dtype),
            pltpu.SemaphoreType.DMA((steps,)),
        ],
        compiler_params=pltpu.CompilerParams(vmem_limit_bytes=2 * SMALL),
        cost_estimate=pl.CostEstimate(
            flops=4 * n * part * w.size, bytes_accessed=2 * w.size, transcendentals=0
        ),
        name="project_text",
    )(mod, gain, w, after, *parts)


def image_kernel(pair, index, past, mod_ref, gain_ref, down_ref, up_ref, w_ref, tokens, *refs):
    first = past == 0
    q_ref, k_ref, v_ref, x_ref, low_ref, hs_ref, *rest = refs[past:]
    weights, copies = w_ref, None
    if first:
        weights, *small, hi, sems, small_sems = rest
        given = (gain_ref, down_ref, up_ref)
        fetched = [
            pltpu.make_async_copy(g, s, small_sems.at[i]) for i, (g, s) in enumerate(zip(given, small))
        ]
        gain_ref, down_ref, up_ref = small
        copies = fetches(w_ref, weights, sems)
        for copy in fetched + copies:
            copy.start()
    else:
        (hi,) = rest
    rows = tokens.shape[0]
    part = slice(index * rows, (index + 1) * rows)
    modulate(tokens, mod_ref, 0, w_ref.shape[0], hi, rows, 0)
    if first:
        for copy in fetched:
            copy.wait()
    hs_ref[part, :] = hi[rows:, :]
    low_ref[part, :] = nt(hi[rows:, :], down_ref[...]).astype(BF16)
    cols = pair * 3 * HD
    piece = 2 * HD if cols % (2 * HD) == 0 else HD

    def project(step):
        for at in range(0, cols, piece):
            columns = pl.ds(step * cols + at, piece)
            if not isinstance(step, int):
                columns = pl.ds(pl.multiple_of(step * cols + at, HD), piece)
            out = nn(hi[...], weights[:, columns])
            student = out[rows:] + nn(low_ref[part, :], up_ref[:, columns])
            for c in range(at, at + piece, HD):
                head, kind = step * pair + c // (3 * HD), c // HD % 3
                for m, own in enumerate((out[:rows], student)):
                    x = own[:, c - at : c - at + HD]
                    if kind == 2:
                        v_ref[head, m, part, :] = x.astype(BF16)
                    else:
                        dest = (q_ref, k_ref)[kind]
                        dest[head, m, part, :] = normed(x, gain_ref[kind : kind + 1, :])
                        if m == 1:
                            x_ref[head, kind, part, :] = x

    if copies is None:
        pl.loop(0, w_ref.shape[1] // cols)(project)
    else:
        for step, copy in enumerate(copies):
            copy.wait()
            project(step)


def project_image(part, n, before, mod, gain, down, up, w, tokens):
    (rows, width), rank = tokens.shape, up.shape[0]
    pair, steps = split(w.shape[1] // (3 * HD))
    heads = (pair * steps, 2, n * rows, HD)
    shapes = [pltpu.VMEM(heads, BF16)] * 3 + [
        pltpu.VMEM(heads, F32),
        pltpu.VMEM((n * rows, rank), BF16),
        pltpu.VMEM((n * rows, width), BF16),
    ]
    scratch = [pltpu.VMEM((2 * rows, width), BF16)]
    if not before:
        shapes += [pltpu.VMEM(x.shape, x.dtype) for x in (w, gain, down, up)]
        scratch += [pltpu.SemaphoreType.DMA((steps,)), pltpu.SemaphoreType.DMA((3,))]
    return pl.pallas_call(
        functools.partial(image_kernel, pair, part, len(before)),
        in_specs=[VMEM] + [VMEM if before else HELD] * 4 + [VMEM] * (1 + len(before)),
        out_specs=[VMEM] * len(shapes),
        out_shape=shapes,
        input_output_aliases={6 + i: i for i in range(len(before))},
        scratch_shapes=scratch,
        compiler_params=pltpu.CompilerParams(vmem_limit_bytes=SMALL),
        cost_estimate=pl.CostEstimate(
            flops=4 * rows * w.size, bytes_accessed=2 * w.size, transcendentals=0
        ),
        name="project_image",
    )(mod, gain, down, up, w, tokens, *before)


def attend_kernel(
    steps, pair, samples, where_ref, bias_ref, gain_ref, up_ref, q_ref, k_ref, v_ref, x_ref, kt_ref, vt_ref,
    low_ref, hs_ref, send_a, keep_a, send_b, keep_b, loss_ref, lowt, glt, k_s, v_s, dk_s, dv_s, gq, whole
):
    core = where_ref[0]
    half = send_a.shape[0]
    lowt[...] = low_ref[...].astype(F32).T.astype(BF16)
    glt[...] = jnp.zeros_like(glt)
    loss_ref[...] = jnp.zeros_like(loss_ref)

    def share(value, columns, send, keep):
        whole[:, : value.shape[1]] = value
        mine = pl.ds(pl.multiple_of(core * half, 8), half)
        other = pl.ds(pl.multiple_of((1 - core) * half, 8), half)
        keep[:, columns] = whole[mine, : value.shape[1]]
        send[:, columns] = whole[other, : value.shape[1]].astype(send.dtype)

    @pl.loop(0, steps)
    def _(step):
        columns = pl.ds(pl.multiple_of(step * gq.shape[1], HD), gq.shape[1])
        group = pl.ds(step * pair, pair)
        attend_heads(
            pair, samples, bias_ref, gain_ref, *[r.at[group] for r in (q_ref, k_ref, v_ref, x_ref, kt_ref, vt_ref)],
            loss_ref, k_s, v_s, dk_s, dv_s, gq,
        )
        share(nn(lowt[...], gq[...]), columns, send_b, keep_b)
        glt[...] += nt(up_ref[:, columns], gq[...])

    g = glt[...]
    g1 = g.astype(BF16)
    rest = g - g1.astype(F32)
    g2 = rest.astype(BF16)
    g3 = (rest - g2.astype(F32)).astype(BF16)
    stack = jnp.concatenate([g1, g2, g3], 0)
    rank = g.shape[0]
    full = nn(stack, hs_ref[...])
    share(full[:rank] + full[rank : 2 * rank] + full[2 * rank :], slice(0, full.shape[1]), send_a, keep_a)


def attend_heads(
    pair, samples, bias_ref, gain_ref, q_ref, k_ref, v_ref, x_ref, kt_ref, vt_ref, loss_ref, k_s, v_s, dk_s, dv_s, gq
):
    rows = q_ref.shape[2]
    block = min(rows, 160)
    heads = range(pair)
    for j in heads:
        for m in range(2):
            k_s[j, m, :rows, :] = k_ref[j, m]
            k_s[j, m, rows:, :] = kt_ref[j, m]
            v_s[j, m, :rows, :] = v_ref[j, m]
            v_s[j, m, rows:, :] = vt_ref[j, m]
    if rows > block:
        dk_s[...] = jnp.zeros_like(dk_s)
        dv_s[...] = jnp.zeros_like(dv_s)
    gain_q, gain_k = gain_ref[0:1, :], gain_ref[1:2, :]

    def attend(start):
        at = pl.ds(start, block)
        both = [(j, m) for j in heads for m in range(2)]
        scores = {(j, m): nt(q_ref[j, m, at, :], k_s[j, m]) for j, m in both}
        weights = {i: jnp.exp2(scores[i] * (ROOT * LOG2E) + bias_ref[...]) for i in both}
        scale = {i: 1.0 / jnp.sum(weights[i], axis=1, keepdims=True) for i in both}
        probs = {i: weights[i] * scale[i] for i in both}
        rounded = {i: probs[i].astype(BF16) for i in both}
        out = {(j, m): nn(rounded[j, m], v_s[j, m]) for j, m in both}
        diff = [out[j, 1] - out[j, 0].astype(BF16).astype(F32) for j in heads]
        total = diff[0] * diff[0]
        for d in diff[1:]:
            total = total + d * d
        loss_ref[...] += jnp.sum(total.reshape(block // 8, 8, HD), axis=0)
        dout = [(d * (2.0 / samples)).astype(BF16) for d in diff]
        dprobs = [nt(dout[j], v_s[j, 1]).astype(BF16).astype(F32) for j in heads]
        dv = [tn(rounded[j, 1], dout[j]) for j in heads]
        inner = [jnp.sum(dprobs[j] * probs[j, 1], axis=1, keepdims=True) for j in heads]
        dscores = [(probs[j, 1] * (dprobs[j] - inner[j]) * ROOT).astype(BF16) for j in heads]
        dq = [nn(dscores[j], k_s[j, 1]).astype(BF16).astype(F32) for j in heads]
        dk = [tn(dscores[j], q_ref[j, 1, at, :]) for j in heads]
        for j in heads:
            c = j * 3 * HD
            gq[at, c : c + HD] = norm_pull(x_ref[j, 0, at, :], gain_q, dq[j]).astype(BF16)
            if rows > block:
                dk_s[j] += dk[j][:rows]
                dv_s[j] += dv[j][:rows]
            else:
                dk_s[j] = dk[j][:rows]
                dv_s[j] = dv[j][:rows]

    over(rows, block, attend)

    def rest(start):
        at = pl.ds(start, block)
        for j in heads:
            c = j * 3 * HD
            dk = dk_s[j, at, :].astype(BF16).astype(F32)
            gq[at, c + HD : c + 2 * HD] = norm_pull(x_ref[j, 1, at, :], gain_k, dk).astype(BF16)
            gq[at, c + 2 * HD : c + 3 * HD] = dv_s[j, at, :].astype(BF16)

    over(rows, block, rest)


def attend(where, bias, gain, up, image, text):
    q, k, v, x, low, hs = image
    kt, vt = text
    (rank, img_cols), width = up.shape, hs.shape[1]
    count, _, rows, _ = q.shape
    trows = kt.shape[2]
    pair, steps = split(count)
    half, ic = rank // 2, pair * 3 * HD
    samples = lax.axis_size("grp") * lax.axis_size("dp")
    out_a, out_b = (half, width), (half, img_cols)
    return pl.pallas_call(
        functools.partial(attend_kernel, steps, pair, samples),
        in_specs=[pl.BlockSpec(memory_space=pltpu.SMEM)] + [VMEM] * 11,
        out_specs=[VMEM] * 5,
        out_shape=[
            jax.ShapeDtypeStruct(out_a, BF16),
            jax.ShapeDtypeStruct(out_a, F32),
            jax.ShapeDtypeStruct(out_b, BF16),
            jax.ShapeDtypeStruct(out_b, F32),
            jax.ShapeDtypeStruct((8, HD), F32),
        ],
        scratch_shapes=[
            pltpu.VMEM((rank, rows), BF16),
            pltpu.VMEM((rank, rows), F32),
            pltpu.VMEM((pair, 2, rows + trows, HD), BF16),
            pltpu.VMEM((pair, 2, rows + trows, HD), BF16),
            pltpu.VMEM((pair, rows, HD), F32),
            pltpu.VMEM((pair, rows, HD), F32),
            pltpu.VMEM((rows, ic), BF16),
            pltpu.VMEM((rank, max(width, ic)), F32),
        ],
        compiler_params=pltpu.CompilerParams(vmem_limit_bytes=2 * SMALL),
        cost_estimate=pl.CostEstimate(
            flops=16 * count * rows * (rows + trows) * HD,
            bytes_accessed=8_000_000,
            transcendentals=2 * count * rows * (rows + trows),
        ),
        name="attend",
    )(where, bias, gain, up, q, k, v, x, kt, vt, low, hs)


def modulation_kernel(emb_ref, weight_ref, part_ref):
    part_ref[...] = nn(emb_ref[...], weight_ref[...])[: part_ref.shape[0]]


def modulation(emb, weight):
    depth, cols = weight.shape
    steps = 2 if cols % 256 == 0 else 1
    return pl.pallas_call(
        modulation_kernel,
        grid=(steps,),
        in_specs=[
            pl.BlockSpec(emb.shape, lambda s: (0, 0)),
            pl.BlockSpec((depth, cols // steps), lambda s: (0, s)),
        ],
        out_specs=pl.BlockSpec((2, cols // steps), lambda s: (0, s)),
        out_shape=jax.ShapeDtypeStruct((2, cols), F32),
        compiler_params=params(10),
        cost_estimate=pl.CostEstimate(
            flops=4 * depth * cols, bytes_accessed=2 * weight.size, transcendentals=0
        ),
        name="modulation",
    )(emb, held(weight))


def noisy_kernel(sigma_ref, image_ref, noise_ref, after_ref, noisy_ref):
    sigma = sigma_ref[0]
    clean, noise = image_ref[...].astype(F32), noise_ref[...].astype(F32)
    noisy_ref[...] = ((1.0 - sigma) * clean + sigma * noise).astype(BF16)


def mix(sigma, image, noise, after):
    rows, width = image.shape
    steps = 2 if width % 256 == 0 else 1
    tokens = pl.BlockSpec((rows, width // steps), lambda s: (0, s))
    return pl.pallas_call(
        noisy_kernel,
        grid=(steps,),
        in_specs=[
            pl.BlockSpec(memory_space=pltpu.SMEM),
            tokens,
            tokens,
            pl.BlockSpec(memory_space=pl.ANY),
        ],
        out_specs=tokens,
        out_shape=jax.ShapeDtypeStruct((rows, width), BF16),
        compiler_params=params(10),
        cost_estimate=pl.CostEstimate(flops=0, bytes_accessed=6 * image.size, transcendentals=0),
        name="noisy",
    )(sigma, held(image), held(noise), after)


def finish_kernel(scale_a, scale_b, scale_loss, side_ref, a_ref, b_ref, sums_ref, got_ref, out_a, out_b, loss_ref):
    half = HD // 2
    rows, width, cols = a_ref.shape[0], a_ref.shape[1], b_ref.shape[1]
    at = rows // 8 * (width + cols)
    other = [got_ref[:, at + i * HD : at + (i + 1) * HD].astype(F32) for i in range(3)]
    total = jnp.sum(sums_ref[...] + (other[0] + other[1] + other[2]), axis=0, keepdims=True)
    loss_ref[...] = jnp.sum(total[:, :half], axis=1, keepdims=True) * scale_loss
    squares_b = jnp.sum(total[:, half:], axis=1, keepdims=True) * scale_b
    unit_b = lax.rsqrt(squares_b + EPS)
    blocks = range(rows // 8)
    mine = [lambda b=b: a_ref[8 * b : 8 * b + 8, :].astype(F32) for b in blocks]
    theirs = [lambda b=b: got_ref[:, b * width : (b + 1) * width].astype(F32) for b in blocks]

    def squares(parts):
        each = functools.reduce(lambda x, y: x + y, [p() * p() for p in parts])
        return jnp.sum(jnp.sum(each, axis=0, keepdims=True), axis=1, keepdims=True)

    unit_a = lax.rsqrt((squares(mine) + squares(theirs)) * scale_a + EPS)
    side = side_ref[0]
    at = rows // 8 * width
    for b in blocks:
        own = pl.ds(pl.multiple_of(side * rows + 8 * b, 8), 8)
        far = pl.ds(pl.multiple_of((1 - side) * rows + 8 * b, 8), 8)
        out_a[own, :] = mine[b]() * unit_a
        out_a[far, :] = theirs[b]() * unit_a
        out_b[own, :] = b_ref[8 * b : 8 * b + 8, :].astype(F32) * unit_b
        out_b[far, :] = got_ref[:, at + b * cols : at + (b + 1) * cols].astype(F32) * unit_b


def finish(side, grad_a, grad_b, sums, got, n, entries):
    (half, width), cols = grad_a.shape, grad_b.shape[1]
    rank = 2 * half
    return pl.pallas_call(
        functools.partial(finish_kernel, 1.0 / (rank * width), 1.0 / (rank * cols * n), 1.0 / entries),
        in_specs=[pl.BlockSpec(memory_space=pltpu.SMEM)] + [VMEM] * 4,
        compiler_params=pltpu.CompilerParams(vmem_limit_bytes=SMALL),
        out_shape=[
            jax.ShapeDtypeStruct((rank, width), F32),
            jax.ShapeDtypeStruct((rank, cols), F32),
            jax.ShapeDtypeStruct((1, 1), F32),
        ],
        name="finish",
    )(side, grad_a, grad_b, sums, got)


def shifted(x, axis, k):
    size = lax.axis_size(axis)
    return lax.ppermute(x, axis, [(i, (i + k) % size) for i in range(size)])


def packed(arrays):
    return len(arrays) > 1 and all(x.shape[0] % 8 == 0 and x.shape[1] % HD == 0 for x in arrays)


def pack(arrays):
    return jnp.concatenate([x[r : r + 8] for x in arrays for r in range(0, x.shape[0], 8)], 1)


def unpack(message, arrays):
    out, at = [], 0
    for x in arrays:
        blocks = []
        for _ in range(0, x.shape[0], 8):
            blocks.append(message[:, at : at + x.shape[1]])
            at += x.shape[1]
        out.append(blocks[0] if len(blocks) == 1 else jnp.concatenate(blocks, 0))
    return out


def send(arrays, group, hop):
    pairs = [(i, i ^ group.mask(hop)) for i in range(group.size)]
    if not packed(arrays):
        return [lax.ppermute(x, group.axes, pairs) for x in arrays]
    return unpack(lax.ppermute(pack(arrays), group.axes, pairs), arrays)


class Group:
    def __init__(self, *places):
        self.axes = tuple(a for a in ("grp", "seq", "dp") if any(a == p[0] for p in places))
        self.size = math.prod(lax.axis_size(a) for a in self.axes)
        self.places = places
        self.count = 1 << len(places)
        sides = [lax.rem(lax.div(lax.axis_index(a), bit), 2) for a, bit in places]
        self.me = functools.reduce(lambda total, side: 2 * total + side, sides, 0)

    def mask(self, hop):
        total = 0
        for i, (axis, bit) in enumerate(reversed(self.places)):
            if hop >> i & 1:
                below = self.axes[self.axes.index(axis) + 1 :]
                total ^= bit * math.prod(lax.axis_size(a) for a in below)
        return total


def cut_of(x, count):
    if x.shape[0] % (8 * count) == 0:
        return 0
    return 1 if x.shape[1] % (count * HD) == 0 else 0


def block(x, dim, count, index):
    each = x.shape[dim] // count
    return lax.dynamic_slice_in_dim(x, index * each, each, dim)


def scatter(wide, narrow=()):
    arrays, group = wide
    more, part = narrow or ([], None)
    dims = [cut_of(x, group.count) for x in arrays]
    more_dims = [cut_of(x, part.count) for x in more]
    sums = [block(x, d, group.count, group.me) for x, d in zip(arrays, dims)]
    more_sums = [block(x, d, part.count, part.me) for x, d in zip(more, more_dims)]
    for hop in range(1, group.count):
        out = [block(x, d, group.count, group.me ^ hop).astype(BF16) for x, d in zip(arrays, dims)]
        join = part is not None and hop < part.count
        if join:
            out += [block(x, d, part.count, part.me ^ hop).astype(BF16) for x, d in zip(more, more_dims)]
        got = [g.astype(F32) for g in send(out, group, hop)]
        sums = [t + g for t, g in zip(sums, got)]
        if join:
            more_sums = [t + g for t, g in zip(more_sums, got[len(sums) :])]
    return sums, dims, more_sums, more_dims


def to_all(blocks, axis):
    if packed(blocks[0]):
        got = lax.all_to_all(jnp.stack([pack(b) for b in blocks]), axis, 0, 0)
        return [unpack(got[j], blocks[0]) for j in range(len(blocks))]
    got = [lax.all_to_all(jnp.stack(x), axis, 0, 0) for x in zip(*blocks)]
    return [[x[j] for x in got] for j in range(len(blocks))]


def scatter_axis(arrays, axis):
    count, me = lax.axis_size(axis), lax.axis_index(axis)
    dims = [cut_of(x, count) for x in arrays]
    blocks = [[block(x, d, count, j).astype(BF16) for x, d in zip(arrays, dims)] for j in range(count)]
    sums = [block(x, d, count, me) for x, d in zip(arrays, dims)]
    for j, got in enumerate(to_all(blocks, axis)):
        sums = [t + jnp.where(me == j, 0.0, g.astype(F32)) for t, g in zip(sums, got)]
    return sums, dims


def gather_axis(arrays, dims, sums, axis):
    blocks = [[*arrays, pieces(sums)]] * lax.axis_size(axis)
    *parts, others = zip(*to_all(blocks, axis))
    others = [o.astype(F32) for o in others]
    totals = [o[:, :HD] + o[:, HD : 2 * HD] + o[:, 2 * HD :] for o in others]
    return (
        [jnp.concatenate(p, d) for p, d in zip(parts, dims)],
        functools.reduce(lambda x, y: x + y, totals),
    )


def ordered(parts, me):
    return [
        functools.reduce(
            lambda so_far, hop: jnp.where(me == j ^ hop, parts[hop], so_far), range(1, len(parts)), parts[0]
        )
        for j in range(len(parts))
    ]


def gather(wide, sums, narrow=()):
    arrays, dims, group = wide
    more, more_dims, part = narrow or ([], [], None)
    parts = [[x] for x in arrays]
    more_parts = [[x] for x in more]
    totals = [sums]
    for hop in range(1, group.count):
        join = part is not None and hop < part.count
        out = [*arrays, *(more if join else []), pieces(sums)]
        *got, other = send(out, group, hop)
        other = other.astype(F32)
        totals.append(other[:, :HD] + other[:, HD : 2 * HD] + other[:, 2 * HD :])
        for so_far, g in zip(parts + (more_parts if join else []), got):
            so_far.append(g)
    totals = ordered(totals, group.me)
    sums = functools.reduce(lambda x, y: x + y, totals)
    whole = [jnp.concatenate(ordered(p, group.me), d) for p, d in zip(parts, dims)]
    more_whole = [jnp.concatenate(ordered(p, part.me), d) for p, d in zip(more_parts, more_dims)]
    return whole, more_whole, sums


def pieces(value):
    first = lax.reduce_precision(value, 8, 7)
    rest = value - first
    second = lax.reduce_precision(rest, 8, 7)
    return jnp.concatenate([first, second, rest - second], 1).astype(BF16)


def bits(axis):
    size = lax.axis_size(axis)
    return [1 << i for i in range(size.bit_length() - 1)]


def fold(x):
    half = HD // 2
    return functools.reduce(
        lambda total, c: total + x[:, c : c + half], range(half, x.shape[1], half), x[:, :half]
    )


def on_device(
    image,
    noise,
    text,
    timestep,
    guidance,
    text_token_length,
    image_projection_weight,
    text_projection_weight,
    modulation_weight,
    query_key_norm_gain,
    adapter_down_weight,
    adapter_up_weight,
):
    emb_width = modulation_weight.shape[0]
    n, me = lax.axis_size("seq"), lax.axis_index("seq")
    samples = lax.axis_size("grp") * lax.axis_size("dp")
    sigma = (timestep[0].astype(F32) + 1.0) / STEPS
    time = timing(sigma, emb_width)
    guide = jnp.where(jnp.arange(16)[:, None] == 0, timing(guidance[0], emb_width)[None], 0.0)
    emb = jnp.concatenate([jnp.broadcast_to(time[None], guide.shape), guide], 1)
    emb = jax.nn.silu(emb).astype(BF16)
    part = modulation(emb, modulation_weight)
    noisy = mix(sigma[None], image[0], noise[0], part)
    mods = [part] + [shifted(part, "seq", k) for k in range(1, n)]
    noisy_parts = [noisy] + [shifted(noisy, "seq", k) for k in range(1, n)]
    words = text[0]
    text_parts = [words] + [shifted(words, "seq", k) for k in range(1, n)]
    origin = [lax.rem(me + n - k, n) for k in range(n)]
    ordered = [
        functools.reduce(
            lambda so_far, k: jnp.where(origin[k] == j, mods[k], so_far), range(1, n), mods[0]
        )
        for j in range(n)
    ]
    mod = jnp.concatenate(ordered, 1)
    img_part, txt_part = noisy.shape[0], words.shape[0]
    place = jnp.concatenate(
        [jnp.zeros((n * img_part,), jnp.int32)]
        + [origin[k] * txt_part + jnp.arange(txt_part, dtype=jnp.int32) for k in range(n)]
    )
    bias = jnp.where(place < text_token_length[0], 0.0, -1000000000.0).astype(F32)[None]
    core = lax.rem(lax.axis_index("grp"), 2).astype(jnp.int32)
    gain = query_key_norm_gain
    down, up = adapter_down_weight.T, adapter_up_weight
    weights, image_heads = [held(x) for x in (image_projection_weight, gain, down, up)], []
    for k in range(n):
        weight, gain, down, up = weights
        image_heads = project_image(k, n, image_heads, mod, gain, down, up, weight, noisy_parts[k])
        if k == 0:
            image_heads, weights = image_heads[:6], image_heads[6:]
    _, gain, _, up = weights
    text_heads = project_text(mod, gain, held(text_projection_weight), image_heads[0], text_parts)
    send_a, keep_a, send_b, keep_b, loss = attend(
        core[None], bias, gain, up, image_heads, text_heads
    )
    cores = Group(("grp", 1))
    (got_a,), (got_b,) = send([send_a], cores, 1), send([send_b], cores, 1)
    grad_a, grad_b = keep_a + got_a.astype(F32), keep_b + got_b.astype(F32)
    last, *far = bits("seq")
    far = [(Group(("seq", bit)), []) for bit in reversed(far)]
    for group, dims in far:
        (grad_a,), dims[:], _, _ = scatter(([grad_a], group))
    near, across = Group(("seq", last), ("grp", 2)), Group(("grp", 2))
    (grad_a,), dims_a, (grad_b,), dims_b = scatter(([grad_a], near), ([grad_b], across))
    (grad_a, grad_b), dims_z = scatter_axis([grad_a, grad_b], "dp")
    squares = fold(jnp.sum(grad_b.reshape(-1, min(grad_b.shape[0], 8), grad_b.shape[1]) ** 2, 0))
    squares = jnp.pad(squares, ((0, 8 - squares.shape[0]), (0, 0)))
    sums = jnp.concatenate([fold(loss), squares], 1)
    grads, sums = gather_axis([grad_a.astype(BF16), grad_b.astype(BF16)], dims_z, sums, "dp")
    (grad_a,), (grad_b,), sums = gather(
        (grads[:1], dims_a, near), sums, (grads[1:], dims_b, across)
    )
    for group, dims in reversed(far):
        (grad_a,), _, sums = gather(([grad_a], dims, group), sums)
    pairs = [(i, i ^ 1) for i in range(cores.size)]
    got = lax.ppermute(pack([grad_a, grad_b, pieces(sums)]), "grp", pairs)
    direction_a, direction_b, loss_mean = finish(
        core[None], grad_a, grad_b, sums, got, n, samples * n * img_part * HEADS * HD
    )
    return (direction_a.T, direction_b, loss_mean[0, 0])


def solution(mesh):
    in_specs = (
        P(("grp", "dp"), "seq", None),
        P(("grp", "dp"), "seq", None),
        P(("grp", "dp"), "seq", None),
        P(("grp", "dp")),
        P(("grp", "dp")),
        P(("grp", "dp")),
        P(None, "seq"),
        P(None, "seq"),
        P(None, "seq"),
        P(),
        P(),
        P(None, "seq"),
    )
    out_specs = (P(), P(None, "seq"), P())
    return jax.shard_map(
        on_device, mesh=mesh, in_specs=in_specs, out_specs=out_specs, check_vma=False
    )
```

```python
import functools
import math

import jax
import jax.numpy as jnp
from jax import lax
from jax.experimental import pallas as pl
from jax.experimental.pallas import tpu as pltpu
from jax.sharding import PartitionSpec as P

HD = 128
HEADS = 16
STEPS = 1000
EPS = 1e-06
F32 = jnp.float32
BF16 = jnp.bfloat16
ROOT = 1.0 / math.sqrt(HD)
LOG2E = 1.0 / math.log(2.0)
SMALL = 10 * 1024 * 1024


def timing(value, width):
    count = width // 4
    freqs = jnp.exp(-math.log(10000.0) * jnp.arange(count, dtype=F32) / count)
    angles = 1000.0 * value * freqs
    return jnp.concatenate([jnp.cos(angles), jnp.sin(angles)])


def nn(a, b):
    return lax.dot_general(a, b, (((1,), (0,)), ((), ())), preferred_element_type=F32)


def nt(a, b):
    return lax.dot_general(a, b, (((1,), (1,)), ((), ())), preferred_element_type=F32)


def tn(a, b):
    return lax.dot_general(a, b, (((0,), (0,)), ((), ())), preferred_element_type=F32)


def over(total, size, body):
    if total == size:
        body(0)
    else:

        @pl.loop(0, total // size)
        def _(i):
            body(pl.multiple_of(i * size, size))


def inverse_rms(x):
    return lax.rsqrt(jnp.mean(x * x, axis=-1, keepdims=True) + EPS)


def norm_pull(x, gain, dy):
    r = inverse_rms(x)
    u = gain * dy
    return r * (u - x * (r * r * jnp.mean(x * u, axis=-1, keepdims=True)))


def modulate(tokens, mod_ref, kind, width, dest, rows, base):
    size = tokens.shape[0]

    @pl.loop(0, size // 16)
    def _(i):
        v = tokens[pl.ds(pl.multiple_of(i * 16, 16), 16), :].astype(F32)
        center = v - jnp.mean(v, axis=1, keepdims=True)
        spread = jnp.mean(center * center, axis=1, keepdims=True)
        unit = center * lax.rsqrt(spread + EPS)
        for m in range(2):
            shift = mod_ref[m : m + 1, kind * width : (kind + 1) * width]
            scale = mod_ref[m : m + 1, (kind + 1) * width : (kind + 2) * width]
            at = pl.multiple_of(m * rows + base + i * 16, 16)
            dest[pl.ds(at, 16), :] = (unit * (1.0 + scale) + shift).astype(BF16)


def normed(x, gain):
    return (x * inverse_rms(x) * gain).astype(BF16)


def fetches(w_ref, out_ref, sems):
    cols = w_ref.shape[1] // sems.shape[0]
    return [
        pltpu.make_async_copy(
            w_ref.at[:, i * cols : (i + 1) * cols], out_ref.at[:, i * cols : (i + 1) * cols], sems.at[i]
        )
        for i in range(sems.shape[0])
    ]


def held(x):
    return pltpu.with_memory_space_constraint(x, pltpu.HBM)


def text_kernel(n, pair, mod_ref, gain_ref, w_ref, after_ref, *refs):
    parts, (k_ref, v_ref, ht, weights, sems) = refs[:n], refs[n:]
    copies = fetches(w_ref, weights, sems)
    for copy in copies:
        copy.start()
    rows = n * parts[0].shape[0]
    for k in range(n):
        modulate(parts[k], mod_ref, 2, w_ref.shape[0], ht, rows, k * parts[0].shape[0])
    cols = pair * 2 * HD
    size = min(rows, 96)
    for step, copy in enumerate(copies):
        copy.wait()

        def project(start, step=step):
            for j in range(pair):
                head, c = step * pair + j, step * cols + j * 2 * HD
                w = weights[:, c : c + 2 * HD]
                if size == rows:
                    both = nn(ht[...], w)
                    own = [both[:rows], both[rows:]]
                else:
                    own = [nn(ht[pl.ds(m * rows + start, size), :], w) for m in range(2)]
                for m, kv in enumerate(own):
                    k_ref[head, m, pl.ds(start, size), :] = normed(kv[:, :HD], gain_ref[2:3, :])
                    v_ref[head, m, pl.ds(start, size), :] = kv[:, HD:].astype(BF16)

        over(rows, size, project)


def split(count):
    pair = 2 if count % 2 == 0 else 1
    return pair, count // pair


def params(mib):
    return pltpu.CompilerParams(
        dimension_semantics=("arbitrary",), vmem_limit_bytes=mib * 1024 * 1024
    )


VMEM = pl.BlockSpec(memory_space=pltpu.VMEM)
HELD = pl.BlockSpec(memory_space=pltpu.HBM)


def project_text(mod, gain, w, after, parts):
    n, (part, width) = len(parts), parts[0].shape
    pair, steps = split(w.shape[1] // (2 * HD))
    out = pltpu.VMEM((pair * steps, 2, n * part, HD), BF16)
    return pl.pallas_call(
        functools.partial(text_kernel, n, pair),
        in_specs=[VMEM, VMEM, HELD, pl.BlockSpec(memory_space=pl.ANY)] + [VMEM] * n,
        out_specs=[VMEM] * 2,
        out_shape=[out, out],
        scratch_shapes=[
            pltpu.VMEM((2 * n * part, width), BF16),
            pltpu.VMEM(w.shape, w.dtype),
            pltpu.SemaphoreType.DMA((steps,)),
        ],
        compiler_params=pltpu.CompilerParams(vmem_limit_bytes=2 * SMALL),
        cost_estimate=pl.CostEstimate(
            flops=4 * n * part * w.size, bytes_accessed=2 * w.size, transcendentals=0
        ),
        name="project_text",
    )(mod, gain, w, after, *parts)


def image_kernel(pair, index, past, mod_ref, gain_ref, down_ref, up_ref, w_ref, tokens, *refs):
    first = past == 0
    q_ref, k_ref, v_ref, x_ref, low_ref, hs_ref, *rest = refs[past:]
    weights = w_ref
    if first:
        weights, *small, hi, sems, small_sems = rest
        given = (gain_ref, down_ref, up_ref)
        fetched = [
            pltpu.make_async_copy(g, s, small_sems.at[i]) for i, (g, s) in enumerate(zip(given, small))
        ]
        gain_ref, down_ref, up_ref = small
        for copy in fetched + fetches(w_ref, weights, sems):
            copy.start()
    else:
        (hi,) = rest
    rows = tokens.shape[0]
    part = slice(index * rows, (index + 1) * rows)
    modulate(tokens, mod_ref, 0, w_ref.shape[0], hi, rows, 0)
    if first:
        for copy in fetched:
            copy.wait()
    hs_ref[part, :] = hi[rows:, :]
    low_ref[part, :] = nt(hi[rows:, :], down_ref[...]).astype(BF16)
    cols = pair * 3 * HD

    def project(step):
        columns = pl.ds(pl.multiple_of(step * cols, cols), cols)
        if first:
            pltpu.make_async_copy(w_ref.at[:, columns], weights.at[:, columns], sems.at[step]).wait()
        out = nn(hi[...], weights[:, columns])
        student = out[rows:] + nn(low_ref[part, :], up_ref[:, columns])
        for j in range(pair):
            head, c = step * pair + j, j * 3 * HD
            for m, own in enumerate((out[:rows], student)):
                for kind, dest in enumerate((q_ref, k_ref)):
                    x = own[:, c + kind * HD : c + (kind + 1) * HD]
                    dest[head, m, part, :] = normed(x, gain_ref[kind : kind + 1, :])
                    if m == 1:
                        x_ref[head, kind, part, :] = x
                v_ref[head, m, part, :] = own[:, c + 2 * HD : c + 3 * HD].astype(BF16)

    pl.loop(0, w_ref.shape[1] // cols)(project)


def project_image(part, n, before, mod, gain, down, up, w, tokens):
    (rows, width), rank = tokens.shape, up.shape[0]
    pair, steps = split(w.shape[1] // (3 * HD))
    heads = (pair * steps, 2, n * rows, HD)
    shapes = [pltpu.VMEM(heads, BF16)] * 3 + [
        pltpu.VMEM(heads, F32),
        pltpu.VMEM((n * rows, rank), BF16),
        pltpu.VMEM((n * rows, width), BF16),
    ]
    scratch = [pltpu.VMEM((2 * rows, width), BF16)]
    if not before:
        shapes += [pltpu.VMEM(x.shape, x.dtype) for x in (w, gain, down, up)]
        scratch += [pltpu.SemaphoreType.DMA((steps,)), pltpu.SemaphoreType.DMA((3,))]
    return pl.pallas_call(
        functools.partial(image_kernel, pair, part, len(before)),
        in_specs=[VMEM] + [VMEM if before else HELD] * 4 + [VMEM] * (1 + len(before)),
        out_specs=[VMEM] * len(shapes),
        out_shape=shapes,
        input_output_aliases={6 + i: i for i in range(len(before))},
        scratch_shapes=scratch,
        compiler_params=pltpu.CompilerParams(vmem_limit_bytes=SMALL),
        cost_estimate=pl.CostEstimate(
            flops=4 * rows * w.size, bytes_accessed=2 * w.size, transcendentals=0
        ),
        name="project_image",
    )(mod, gain, down, up, w, tokens, *before)


def attend_kernel(
    steps, pair, samples, where_ref, bias_ref, gain_ref, up_ref, q_ref, k_ref, v_ref, x_ref, kt_ref, vt_ref,
    low_ref, hs_ref, send_a, keep_a, send_b, keep_b, loss_ref, lowt, glt, k_s, v_s, dk_s, dv_s, gq, whole
):
    core = where_ref[0]
    half = send_a.shape[0]
    lowt[...] = low_ref[...].astype(F32).T.astype(BF16)
    glt[...] = jnp.zeros_like(glt)
    loss_ref[...] = jnp.zeros_like(loss_ref)

    def share(value, columns, send, keep):
        whole[:, : value.shape[1]] = value
        mine = pl.ds(pl.multiple_of(core * half, 8), half)
        other = pl.ds(pl.multiple_of((1 - core) * half, 8), half)
        keep[:, columns] = whole[mine, : value.shape[1]]
        send[:, columns] = whole[other, : value.shape[1]].astype(send.dtype)

    @pl.loop(0, steps)
    def _(step):
        columns = pl.ds(pl.multiple_of(step * gq.shape[1], HD), gq.shape[1])
        group = pl.ds(step * pair, pair)
        attend_heads(
            pair, samples, bias_ref, gain_ref, *[r.at[group] for r in (q_ref, k_ref, v_ref, x_ref, kt_ref, vt_ref)],
            loss_ref, k_s, v_s, dk_s, dv_s, gq,
        )
        share(nn(lowt[...], gq[...]), columns, send_b, keep_b)
        glt[...] += nt(up_ref[:, columns], gq[...])

    g = glt[...]
    g1 = g.astype(BF16)
    rest = g - g1.astype(F32)
    g2 = rest.astype(BF16)
    g3 = (rest - g2.astype(F32)).astype(BF16)
    stack = jnp.concatenate([g1, g2, g3], 0)
    rank = g.shape[0]
    full = nn(stack, hs_ref[...])
    share(full[:rank] + full[rank : 2 * rank] + full[2 * rank :], slice(0, full.shape[1]), send_a, keep_a)


def attend_heads(
    pair, samples, bias_ref, gain_ref, q_ref, k_ref, v_ref, x_ref, kt_ref, vt_ref, loss_ref, k_s, v_s, dk_s, dv_s, gq
):
    rows = q_ref.shape[2]
    block = min(rows, 160)
    heads = range(pair)
    for j in heads:
        for m in range(2):
            k_s[j, m, :rows, :] = k_ref[j, m]
            k_s[j, m, rows:, :] = kt_ref[j, m]
            v_s[j, m, :rows, :] = v_ref[j, m]
            v_s[j, m, rows:, :] = vt_ref[j, m]
    if rows > block:
        dk_s[...] = jnp.zeros_like(dk_s)
        dv_s[...] = jnp.zeros_like(dv_s)
    gain_q, gain_k = gain_ref[0:1, :], gain_ref[1:2, :]

    def attend(start):
        at = pl.ds(start, block)
        both = [(j, m) for j in heads for m in range(2)]
        scores = {(j, m): nt(q_ref[j, m, at, :], k_s[j, m]) for j, m in both}
        weights = {i: jnp.exp2(scores[i] * (ROOT * LOG2E) + bias_ref[...]) for i in both}
        scale = {i: 1.0 / jnp.sum(weights[i], axis=1, keepdims=True) for i in both}
        probs = {i: weights[i] * scale[i] for i in both}
        rounded = {i: probs[i].astype(BF16) for i in both}
        out = {(j, m): nn(rounded[j, m], v_s[j, m]) for j, m in both}
        diff = [out[j, 1] - out[j, 0].astype(BF16).astype(F32) for j in heads]
        total = diff[0] * diff[0]
        for d in diff[1:]:
            total = total + d * d
        loss_ref[...] += jnp.sum(total.reshape(block // 8, 8, HD), axis=0)
        dout = [(d * (2.0 / samples)).astype(BF16) for d in diff]
        dprobs = [nt(dout[j], v_s[j, 1]).astype(BF16).astype(F32) for j in heads]
        dv = [tn(rounded[j, 1], dout[j]) for j in heads]
        inner = [jnp.sum(dprobs[j] * probs[j, 1], axis=1, keepdims=True) for j in heads]
        dscores = [(probs[j, 1] * (dprobs[j] - inner[j]) * ROOT).astype(BF16) for j in heads]
        dq = [nn(dscores[j], k_s[j, 1]).astype(BF16).astype(F32) for j in heads]
        dk = [tn(dscores[j], q_ref[j, 1, at, :]) for j in heads]
        for j in heads:
            c = j * 3 * HD
            gq[at, c : c + HD] = norm_pull(x_ref[j, 0, at, :], gain_q, dq[j]).astype(BF16)
            if rows > block:
                dk_s[j] += dk[j][:rows]
                dv_s[j] += dv[j][:rows]
            else:
                dk_s[j] = dk[j][:rows]
                dv_s[j] = dv[j][:rows]

    over(rows, block, attend)

    def rest(start):
        at = pl.ds(start, block)
        for j in heads:
            c = j * 3 * HD
            dk = dk_s[j, at, :].astype(BF16).astype(F32)
            gq[at, c + HD : c + 2 * HD] = norm_pull(x_ref[j, 1, at, :], gain_k, dk).astype(BF16)
            gq[at, c + 2 * HD : c + 3 * HD] = dv_s[j, at, :].astype(BF16)

    over(rows, block, rest)


def attend(where, bias, gain, up, image, text):
    q, k, v, x, low, hs = image
    kt, vt = text
    (rank, img_cols), width = up.shape, hs.shape[1]
    count, _, rows, _ = q.shape
    trows = kt.shape[2]
    pair, steps = split(count)
    half, ic = rank // 2, pair * 3 * HD
    samples = lax.axis_size("grp") * lax.axis_size("dp")
    out_a, out_b = (half, width), (half, img_cols)
    return pl.pallas_call(
        functools.partial(attend_kernel, steps, pair, samples),
        in_specs=[pl.BlockSpec(memory_space=pltpu.SMEM)] + [VMEM] * 11,
        out_specs=[VMEM] * 5,
        out_shape=[
            jax.ShapeDtypeStruct(out_a, BF16),
            jax.ShapeDtypeStruct(out_a, F32),
            jax.ShapeDtypeStruct(out_b, BF16),
            jax.ShapeDtypeStruct(out_b, F32),
            jax.ShapeDtypeStruct((8, HD), F32),
        ],
        scratch_shapes=[
            pltpu.VMEM((rank, rows), BF16),
            pltpu.VMEM((rank, rows), F32),
            pltpu.VMEM((pair, 2, rows + trows, HD), BF16),
            pltpu.VMEM((pair, 2, rows + trows, HD), BF16),
            pltpu.VMEM((pair, rows, HD), F32),
            pltpu.VMEM((pair, rows, HD), F32),
            pltpu.VMEM((rows, ic), BF16),
            pltpu.VMEM((rank, max(width, ic)), F32),
        ],
        compiler_params=pltpu.CompilerParams(vmem_limit_bytes=2 * SMALL),
        cost_estimate=pl.CostEstimate(
            flops=16 * count * rows * (rows + trows) * HD,
            bytes_accessed=8_000_000,
            transcendentals=2 * count * rows * (rows + trows),
        ),
        name="attend",
    )(where, bias, gain, up, q, k, v, x, kt, vt, low, hs)


def modulation_kernel(emb_ref, weight_ref, part_ref):
    part_ref[...] = nn(emb_ref[...], weight_ref[...])[: part_ref.shape[0]]


def modulation(emb, weight):
    depth, cols = weight.shape
    steps = 2 if cols % 256 == 0 else 1
    return pl.pallas_call(
        modulation_kernel,
        grid=(steps,),
        in_specs=[
            pl.BlockSpec(emb.shape, lambda s: (0, 0)),
            pl.BlockSpec((depth, cols // steps), lambda s: (0, s)),
        ],
        out_specs=pl.BlockSpec((2, cols // steps), lambda s: (0, s)),
        out_shape=jax.ShapeDtypeStruct((2, cols), F32),
        compiler_params=params(10),
        cost_estimate=pl.CostEstimate(
            flops=4 * depth * cols, bytes_accessed=2 * weight.size, transcendentals=0
        ),
        name="modulation",
    )(emb, held(weight))


def noisy_kernel(sigma_ref, image_ref, noise_ref, after_ref, noisy_ref):
    sigma = sigma_ref[0]
    clean, noise = image_ref[...].astype(F32), noise_ref[...].astype(F32)
    noisy_ref[...] = ((1.0 - sigma) * clean + sigma * noise).astype(BF16)


def mix(sigma, image, noise, after):
    rows, width = image.shape
    steps = 2 if width % 256 == 0 else 1
    tokens = pl.BlockSpec((rows, width // steps), lambda s: (0, s))
    return pl.pallas_call(
        noisy_kernel,
        grid=(steps,),
        in_specs=[
            pl.BlockSpec(memory_space=pltpu.SMEM),
            tokens,
            tokens,
            pl.BlockSpec(memory_space=pl.ANY),
        ],
        out_specs=tokens,
        out_shape=jax.ShapeDtypeStruct((rows, width), BF16),
        compiler_params=params(10),
        cost_estimate=pl.CostEstimate(flops=0, bytes_accessed=0, transcendentals=0),
        name="noisy",
    )(sigma, held(image), held(noise), after)


def finish_kernel(scale_a, scale_b, scale_loss, side_ref, a_ref, b_ref, sums_ref, got_ref, out_a, out_b, loss_ref):
    half = HD // 2
    rows, width, cols = a_ref.shape[0], a_ref.shape[1], b_ref.shape[1]
    at = rows // 8 * (width + cols)
    other = [got_ref[:, at + i * HD : at + (i + 1) * HD].astype(F32) for i in range(3)]
    total = jnp.sum(sums_ref[...] + (other[0] + other[1] + other[2]), axis=0, keepdims=True)
    loss_ref[...] = jnp.sum(total[:, :half], axis=1, keepdims=True) * scale_loss
    squares_b = jnp.sum(total[:, half:], axis=1, keepdims=True) * scale_b
    unit_b = lax.rsqrt(squares_b + EPS)
    blocks = range(rows // 8)
    mine = [lambda b=b: a_ref[8 * b : 8 * b + 8, :].astype(F32) for b in blocks]
    theirs = [lambda b=b: got_ref[:, b * width : (b + 1) * width].astype(F32) for b in blocks]

    def squares(parts):
        each = functools.reduce(lambda x, y: x + y, [p() * p() for p in parts])
        return jnp.sum(jnp.sum(each, axis=0, keepdims=True), axis=1, keepdims=True)

    unit_a = lax.rsqrt((squares(mine) + squares(theirs)) * scale_a + EPS)
    side = side_ref[0]
    at = rows // 8 * width
    for b in blocks:
        own = pl.ds(pl.multiple_of(side * rows + 8 * b, 8), 8)
        far = pl.ds(pl.multiple_of((1 - side) * rows + 8 * b, 8), 8)
        out_a[own, :] = mine[b]() * unit_a
        out_a[far, :] = theirs[b]() * unit_a
        out_b[own, :] = b_ref[8 * b : 8 * b + 8, :].astype(F32) * unit_b
        out_b[far, :] = got_ref[:, at + b * cols : at + (b + 1) * cols].astype(F32) * unit_b


def finish(side, grad_a, grad_b, sums, got, n, entries):
    (half, width), cols = grad_a.shape, grad_b.shape[1]
    rank = 2 * half
    return pl.pallas_call(
        functools.partial(finish_kernel, 1.0 / (rank * width), 1.0 / (rank * cols * n), 1.0 / entries),
        in_specs=[pl.BlockSpec(memory_space=pltpu.SMEM)] + [VMEM] * 4,
        compiler_params=pltpu.CompilerParams(vmem_limit_bytes=SMALL),
        out_shape=[
            jax.ShapeDtypeStruct((rank, width), F32),
            jax.ShapeDtypeStruct((rank, cols), F32),
            jax.ShapeDtypeStruct((1, 1), F32),
        ],
        name="finish",
    )(side, grad_a, grad_b, sums, got)


def shifted(x, axis, k):
    size = lax.axis_size(axis)
    return lax.ppermute(x, axis, [(i, (i + k) % size) for i in range(size)])


def packed(arrays):
    return len(arrays) > 1 and all(x.shape[0] % 8 == 0 and x.shape[1] % HD == 0 for x in arrays)


def pack(arrays):
    return jnp.concatenate([x[r : r + 8] for x in arrays for r in range(0, x.shape[0], 8)], 1)


def unpack(message, arrays):
    out, at = [], 0
    for x in arrays:
        blocks = []
        for _ in range(0, x.shape[0], 8):
            blocks.append(message[:, at : at + x.shape[1]])
            at += x.shape[1]
        out.append(blocks[0] if len(blocks) == 1 else jnp.concatenate(blocks, 0))
    return out


def send(arrays, group, hop):
    pairs = [(i, i ^ group.mask(hop)) for i in range(group.size)]
    if not packed(arrays):
        return [lax.ppermute(x, group.axes, pairs) for x in arrays]
    return unpack(lax.ppermute(pack(arrays), group.axes, pairs), arrays)


class Group:
    def __init__(self, *places):
        self.axes = tuple(a for a in ("grp", "seq", "dp") if any(a == p[0] for p in places))
        self.size = math.prod(lax.axis_size(a) for a in self.axes)
        self.places = places
        self.count = 1 << len(places)
        sides = [lax.rem(lax.div(lax.axis_index(a), bit), 2) for a, bit in places]
        self.me = functools.reduce(lambda total, side: 2 * total + side, sides, 0)

    def mask(self, hop):
        total = 0
        for i, (axis, bit) in enumerate(reversed(self.places)):
            if hop >> i & 1:
                below = self.axes[self.axes.index(axis) + 1 :]
                total ^= bit * math.prod(lax.axis_size(a) for a in below)
        return total


def cut_of(x, count):
    if x.shape[0] % (8 * count) == 0:
        return 0
    return 1 if x.shape[1] % (count * HD) == 0 else 0


def block(x, dim, count, index):
    each = x.shape[dim] // count
    return lax.dynamic_slice_in_dim(x, index * each, each, dim)


def scatter(wide, narrow=()):
    arrays, group = wide
    more, part = narrow or ([], None)
    dims = [cut_of(x, group.count) for x in arrays]
    more_dims = [cut_of(x, part.count) for x in more]
    sums = [block(x, d, group.count, group.me) for x, d in zip(arrays, dims)]
    more_sums = [block(x, d, part.count, part.me) for x, d in zip(more, more_dims)]
    for hop in range(1, group.count):
        out = [block(x, d, group.count, group.me ^ hop).astype(BF16) for x, d in zip(arrays, dims)]
        join = part is not None and hop < part.count
        if join:
            out += [block(x, d, part.count, part.me ^ hop).astype(BF16) for x, d in zip(more, more_dims)]
        got = [g.astype(F32) for g in send(out, group, hop)]
        sums = [t + g for t, g in zip(sums, got)]
        if join:
            more_sums = [t + g for t, g in zip(more_sums, got[len(sums) :])]
    return sums, dims, more_sums, more_dims


def ordered(parts, me):
    return [
        functools.reduce(
            lambda so_far, hop: jnp.where(me == j ^ hop, parts[hop], so_far), range(1, len(parts)), parts[0]
        )
        for j in range(len(parts))
    ]


def gather(wide, sums, narrow=()):
    arrays, dims, group = wide
    more, more_dims, part = narrow or ([], [], None)
    parts = [[x] for x in arrays]
    more_parts = [[x] for x in more]
    totals = [sums]
    for hop in range(1, group.count):
        join = part is not None and hop < part.count
        out = [*arrays, *(more if join else []), pieces(sums)]
        *got, other = send(out, group, hop)
        other = other.astype(F32)
        totals.append(other[:, :HD] + other[:, HD : 2 * HD] + other[:, 2 * HD :])
        for so_far, g in zip(parts + (more_parts if join else []), got):
            so_far.append(g)
    totals = ordered(totals, group.me)
    sums = functools.reduce(lambda x, y: x + y, totals)
    whole = [jnp.concatenate(ordered(p, group.me), d) for p, d in zip(parts, dims)]
    more_whole = [jnp.concatenate(ordered(p, part.me), d) for p, d in zip(more_parts, more_dims)]
    return whole, more_whole, sums


def pieces(value):
    first = lax.reduce_precision(value, 8, 7)
    rest = value - first
    second = lax.reduce_precision(rest, 8, 7)
    return jnp.concatenate([first, second, rest - second], 1).astype(BF16)


def bits(axis):
    size = lax.axis_size(axis)
    return [1 << i for i in range(size.bit_length() - 1)]


def fold(x):
    half = HD // 2
    return functools.reduce(
        lambda total, c: total + x[:, c : c + half], range(half, x.shape[1], half), x[:, :half]
    )


def on_device(
    image,
    noise,
    text,
    timestep,
    guidance,
    text_token_length,
    image_projection_weight,
    text_projection_weight,
    modulation_weight,
    query_key_norm_gain,
    adapter_down_weight,
    adapter_up_weight,
):
    emb_width = modulation_weight.shape[0]
    n, me = lax.axis_size("seq"), lax.axis_index("seq")
    samples = lax.axis_size("grp") * lax.axis_size("dp")
    sigma = (timestep[0].astype(F32) + 1.0) / STEPS
    time = timing(sigma, emb_width)
    guide = jnp.where(jnp.arange(16)[:, None] == 0, timing(guidance[0], emb_width)[None], 0.0)
    emb = jnp.concatenate([jnp.broadcast_to(time[None], guide.shape), guide], 1)
    emb = jax.nn.silu(emb).astype(BF16)
    part = modulation(emb, modulation_weight)
    noisy = mix(sigma[None], image[0], noise[0], part)
    mods = [part] + [shifted(part, "seq", k) for k in range(1, n)]
    noisy_parts = [noisy] + [shifted(noisy, "seq", k) for k in range(1, n)]
    words = text[0]
    text_parts = [words] + [shifted(words, "seq", k) for k in range(1, n)]
    origin = [lax.rem(me + n - k, n) for k in range(n)]
    ordered = [
        functools.reduce(
            lambda so_far, k: jnp.where(origin[k] == j, mods[k], so_far), range(1, n), mods[0]
        )
        for j in range(n)
    ]
    mod = jnp.concatenate(ordered, 1)
    img_part, txt_part = noisy.shape[0], words.shape[0]
    place = jnp.concatenate(
        [jnp.zeros((n * img_part,), jnp.int32)]
        + [origin[k] * txt_part + jnp.arange(txt_part, dtype=jnp.int32) for k in range(n)]
    )
    bias = jnp.where(place < text_token_length[0], 0.0, -1000000000.0).astype(F32)[None]
    core = lax.rem(lax.axis_index("grp"), 2).astype(jnp.int32)
    gain = query_key_norm_gain
    down, up = adapter_down_weight.T, adapter_up_weight
    weights, image_heads = [held(x) for x in (image_projection_weight, gain, down, up)], []
    for k in range(n):
        weight, gain, down, up = weights
        image_heads = project_image(k, n, image_heads, mod, gain, down, up, weight, noisy_parts[k])
        if k == 0:
            image_heads, weights = image_heads[:6], image_heads[6:]
    _, gain, _, up = weights
    text_heads = project_text(mod, gain, held(text_projection_weight), image_heads[0], text_parts)
    send_a, keep_a, send_b, keep_b, loss = attend(
        core[None], bias, gain, up, image_heads, text_heads
    )
    cores = Group(("grp", 1))
    (got_a,), (got_b,) = send([send_a], cores, 1), send([send_b], cores, 1)
    grad_a, grad_b = keep_a + got_a.astype(F32), keep_b + got_b.astype(F32)
    last, *far = bits("seq")
    far = [(Group(("seq", bit)), []) for bit in reversed(far)]
    for group, dims in far:
        (grad_a,), dims[:], _, _ = scatter(([grad_a], group))
    near, across = Group(("seq", last), ("grp", 2)), Group(("grp", 2))
    (grad_a,), dims_a, (grad_b,), dims_b = scatter(([grad_a], near), ([grad_b], across))
    line = Group(*[("dp", bit) for bit in reversed(bits("dp"))])
    (grad_a, grad_b), dims_z, _, _ = scatter(([grad_a, grad_b], line))
    squares = fold(jnp.sum(grad_b.reshape(-1, min(grad_b.shape[0], 8), grad_b.shape[1]) ** 2, 0))
    squares = jnp.pad(squares, ((0, 8 - squares.shape[0]), (0, 0)))
    sums = jnp.concatenate([fold(loss), squares], 1)
    grads, _, sums = gather(([grad_a.astype(BF16), grad_b.astype(BF16)], dims_z, line), sums)
    (grad_a,), (grad_b,), sums = gather(
        (grads[:1], dims_a, near), sums, (grads[1:], dims_b, across)
    )
    for group, dims in reversed(far):
        (grad_a,), _, sums = gather(([grad_a], dims, group), sums)
    pairs = [(i, i ^ 1) for i in range(cores.size)]
    got = lax.ppermute(pack([grad_a, grad_b, pieces(sums)]), "grp", pairs)
    direction_a, direction_b, loss_mean = finish(
        core[None], grad_a, grad_b, sums, got, n, samples * n * img_part * HEADS * HD
    )
    return (direction_a.T, direction_b, loss_mean[0, 0])


def solution(mesh):
    in_specs = (
        P(("grp", "dp"), "seq", None),
        P(("grp", "dp"), "seq", None),
        P(("grp", "dp"), "seq", None),
        P(("grp", "dp")),
        P(("grp", "dp")),
        P(("grp", "dp")),
        P(None, "seq"),
        P(None, "seq"),
        P(None, "seq"),
        P(),
        P(),
        P(None, "seq"),
    )
    out_specs = (P(), P(None, "seq"), P())
    return jax.shard_map(
        on_device, mesh=mesh, in_specs=in_specs, out_specs=out_specs, check_vma=False
    )
```

```python
import functools
import math

import jax
import jax.numpy as jnp
from jax import lax
from jax.experimental import pallas as pl
from jax.experimental.pallas import tpu as pltpu
from jax.sharding import PartitionSpec as P

HD = 128
HEADS = 16
STEPS = 1000
EPS = 1e-06
F32 = jnp.float32
BF16 = jnp.bfloat16
ROOT = 1.0 / math.sqrt(HD)
LOG2E = 1.0 / math.log(2.0)
SMALL = 10 * 1024 * 1024
VMEM = pl.BlockSpec(memory_space=pltpu.VMEM)
HELD = pl.BlockSpec(memory_space=pltpu.HBM)


def nn(a, b):
    return lax.dot_general(a, b, (((1,), (0,)), ((), ())), preferred_element_type=F32)


def nt(a, b):
    return lax.dot_general(a, b, (((1,), (1,)), ((), ())), preferred_element_type=F32)


def tn(a, b):
    return lax.dot_general(a, b, (((0,), (0,)), ((), ())), preferred_element_type=F32)


def over(total, size, body):
    if total == size:
        body(0)
    else:

        @pl.loop(0, total // size)
        def _(i):
            body(pl.multiple_of(i * size, size))


def inverse_rms(x):
    return lax.rsqrt(jnp.mean(x * x, axis=-1, keepdims=True) + EPS)


def norm_pull(x, gain, dy):
    r = inverse_rms(x)
    u = gain * dy
    return r * (u - x * (r * r * jnp.mean(x * u, axis=-1, keepdims=True)))


def modulate(tokens, mod_ref, kind, width, dest, rows, base):
    size = tokens.shape[0]

    @pl.loop(0, size // 16)
    def _(i):
        v = tokens[pl.ds(pl.multiple_of(i * 16, 16), 16), :].astype(F32)
        center = v - jnp.mean(v, axis=1, keepdims=True)
        spread = jnp.mean(center * center, axis=1, keepdims=True)
        unit = center * lax.rsqrt(spread + EPS)
        for m in range(2):
            shift = mod_ref[m : m + 1, kind * width : (kind + 1) * width]
            scale = mod_ref[m : m + 1, (kind + 1) * width : (kind + 2) * width]
            at = pl.multiple_of(m * rows + base + i * 16, 16)
            dest[pl.ds(at, 16), :] = (unit * (1.0 + scale) + shift).astype(BF16)


def normed(x, gain):
    return (x * inverse_rms(x) * gain).astype(BF16)


def held(x):
    return pltpu.with_memory_space_constraint(x, pltpu.HBM)


def text_kernel(n, pair, mod_ref, gain_ref, w_ref, *refs):
    parts, (k_ref, v_ref, ht) = refs[:n], refs[n:]
    rows = n * parts[0].shape[0]
    for k in range(n):
        modulate(parts[k], mod_ref, 2, w_ref.shape[0], ht, rows, k * parts[0].shape[0])
    cols = pair * 2 * HD
    size = min(rows, 96)

    @pl.loop(0, w_ref.shape[1] // cols)
    def _(step):
        def project(start):
            for j in range(pair):
                head = step * pair + j
                w = w_ref[:, pl.ds(pl.multiple_of(head * 2 * HD, 2 * HD), 2 * HD)]
                if size == rows:
                    both = nn(ht[...], w)
                    own = [both[:rows], both[rows:]]
                else:
                    own = [nn(ht[pl.ds(m * rows + start, size), :], w) for m in range(2)]
                for m, kv in enumerate(own):
                    k_ref[head, m, pl.ds(start, size), :] = normed(kv[:, :HD], gain_ref[2:3, :])
                    v_ref[head, m, pl.ds(start, size), :] = kv[:, HD:].astype(BF16)

        over(rows, size, project)


def split(count):
    pair = 2 if count % 2 == 0 else 1
    return pair, count // pair


def params(mib):
    return pltpu.CompilerParams(
        dimension_semantics=("arbitrary",), vmem_limit_bytes=mib * 1024 * 1024
    )


def project_text(mod, gain, w, parts):
    n, (part, width) = len(parts), parts[0].shape
    pair, steps = split(w.shape[1] // (2 * HD))
    out = pltpu.VMEM((pair * steps, 2, n * part, HD), BF16)
    return pl.pallas_call(
        functools.partial(text_kernel, n, pair),
        in_specs=[VMEM] * (3 + n),
        out_specs=[VMEM] * 2,
        out_shape=[out, out],
        scratch_shapes=[pltpu.VMEM((2 * n * part, width), BF16)],
        compiler_params=pltpu.CompilerParams(vmem_limit_bytes=SMALL),
        cost_estimate=pl.CostEstimate(
            flops=4 * n * part * w.size, bytes_accessed=2 * w.size, transcendentals=0
        ),
        name="project_text",
    )(mod, gain, w, *parts)


def chunk(w_ref, out_ref, sems, index):
    cols = w_ref.shape[1] // sems.shape[0]
    at = pl.ds(index * cols if isinstance(index, int) else pl.multiple_of(index * cols, cols), cols)
    return pltpu.make_async_copy(w_ref.at[:, at], out_ref.at[:, at], sems.at[index])


def fetch_kernel(after_ref, *refs):
    *given, last_sems, sems = refs
    count = len(given) // 2
    copies = [
        pltpu.make_async_copy(given[i], given[count + i], sems.at[i]) for i in range(count - 1)
    ]
    copies.append(chunk(given[count - 1], given[-1], last_sems, 0))
    for copy in copies:
        copy.start()
    for copy in copies:
        copy.wait()


def fetch(small, w, steps, after):
    arrays = [*small, w]
    return pl.pallas_call(
        fetch_kernel,
        in_specs=[pl.BlockSpec(memory_space=pl.ANY)] + [HELD] * len(arrays),
        out_specs=[VMEM] * len(arrays),
        out_shape=[pltpu.VMEM(x.shape, x.dtype) for x in arrays],
        scratch_shapes=[pltpu.SemaphoreType.DMA((steps,)), pltpu.SemaphoreType.DMA((len(small),))],
        compiler_params=pltpu.CompilerParams(vmem_limit_bytes=SMALL),
        cost_estimate=pl.CostEstimate(
            flops=0, bytes_accessed=2 * w.size // steps, transcendentals=0
        ),
        name="fetch",
    )(after, *[held(x) for x in arrays])


def image_kernel(pair, index, n, mod_ref, gain_ref, down_ref, up_ref, w_ref, tokens, *refs):
    first, last = index == 0, index == n - 1
    refs = list(refs)
    more = refs.pop(0) if first or last else None
    refs = refs[1 if first else 6 :]
    q_ref, k_ref, v_ref, x_ref, low_ref, hs_ref, *rest = refs
    weights = w_ref
    if first or last:
        into, hi, sems = rest
        copies = [chunk(more, into, sems, i) for i in range(1 if first else 0, sems.shape[0])]
        for copy in copies:
            copy.start()
        weights = into if first else w_ref
    else:
        (hi,) = rest
    rows = tokens.shape[0]
    part = slice(index * rows, (index + 1) * rows)
    modulate(tokens, mod_ref, 0, w_ref.shape[0], hi, rows, 0)
    hs_ref[part, :] = hi[rows:, :]
    low_ref[part, :] = nt(hi[rows:, :], down_ref[...]).astype(BF16)
    cols = pair * 3 * HD

    def project(step):
        columns = pl.ds(pl.multiple_of(step * cols, cols), cols)
        if first:

            @pl.when(step > 0)
            def _():
                chunk(more, into, sems, step).wait()

        out = nn(hi[...], weights[:, columns])
        student = out[rows:] + nn(low_ref[part, :], up_ref[:, columns])
        for j in range(pair):
            head, c = step * pair + j, j * 3 * HD
            for m, own in enumerate((out[:rows], student)):
                for kind, dest in enumerate((q_ref, k_ref)):
                    x = own[:, c + kind * HD : c + (kind + 1) * HD]
                    dest[head, m, part, :] = normed(x, gain_ref[kind : kind + 1, :])
                    if m == 1:
                        x_ref[head, kind, part, :] = x
                v_ref[head, m, part, :] = own[:, c + 2 * HD : c + 3 * HD].astype(BF16)

    pl.loop(0, w_ref.shape[1] // cols)(project)
    if last and not first:
        for copy in copies:
            copy.wait()


def project_image(part, n, before, mod, gain, down, up, w, tokens, more):
    (rows, width), rank = tokens.shape, up.shape[0]
    pair, steps = split(w.shape[1] // (3 * HD))
    heads = (pair * steps, 2, n * rows, HD)
    shapes = [pltpu.VMEM(heads, BF16)] * 3 + [
        pltpu.VMEM(heads, F32),
        pltpu.VMEM((n * rows, rank), BF16),
        pltpu.VMEM((n * rows, width), BF16),
    ]
    scratch = [pltpu.VMEM((2 * rows, width), BF16)]
    operands, specs, aliases = [mod, gain, down, up, w, tokens], [VMEM] * 6, {}
    if part == 0 or part == n - 1:
        operands.append(more)
        specs.append(HELD)
        shapes.append(pltpu.VMEM(more.shape, more.dtype))
        scratch.append(pltpu.SemaphoreType.DMA((steps,)))
    if part == 0:
        operands[4] = more
        specs[4] = HELD
        aliases = {len(operands): 6}
        before = [w]
    else:
        aliases = {len(operands) + i: i for i in range(len(before))}
    return pl.pallas_call(
        functools.partial(image_kernel, pair, part, n),
        in_specs=specs + [VMEM] * len(before),
        out_specs=[VMEM] * len(shapes),
        out_shape=shapes,
        input_output_aliases=aliases,
        scratch_shapes=scratch,
        compiler_params=pltpu.CompilerParams(vmem_limit_bytes=SMALL),
        cost_estimate=pl.CostEstimate(
            flops=4 * rows * w.size, bytes_accessed=2 * w.size, transcendentals=0
        ),
        name="project_image",
    )(*operands, *before)


def attend_kernel(
    steps, pair, samples, where_ref, bias_ref, gain_ref, up_ref, q_ref, k_ref, v_ref, x_ref, kt_ref, vt_ref,
    low_ref, hs_ref, send_a, keep_a, send_b, keep_b, loss_ref, lowt, glt, k_s, v_s, dk_s, dv_s, gq, whole
):
    core = where_ref[0]
    half = send_a.shape[0]
    lowt[...] = low_ref[...].astype(F32).T.astype(BF16)
    glt[...] = jnp.zeros_like(glt)
    loss_ref[...] = jnp.zeros_like(loss_ref)

    def share(value, columns, send, keep):
        whole[:, : value.shape[1]] = value
        mine = pl.ds(pl.multiple_of(core * half, 8), half)
        other = pl.ds(pl.multiple_of((1 - core) * half, 8), half)
        keep[:, columns] = whole[mine, : value.shape[1]]
        send[:, columns] = whole[other, : value.shape[1]].astype(send.dtype)

    @pl.loop(0, steps)
    def _(step):
        columns = pl.ds(pl.multiple_of(step * gq.shape[1], HD), gq.shape[1])
        group = pl.ds(step * pair, pair)
        attend_heads(
            pair, samples, bias_ref, gain_ref, *[r.at[group] for r in (q_ref, k_ref, v_ref, x_ref, kt_ref, vt_ref)],
            loss_ref, k_s, v_s, dk_s, dv_s, gq,
        )
        share(nn(lowt[...], gq[...]), columns, send_b, keep_b)
        glt[...] += nt(up_ref[:, columns], gq[...])

    g = glt[...]
    g1 = g.astype(BF16)
    rest = g - g1.astype(F32)
    g2 = rest.astype(BF16)
    g3 = (rest - g2.astype(F32)).astype(BF16)
    stack = jnp.concatenate([g1, g2, g3], 0)
    rank = g.shape[0]
    full = nn(stack, hs_ref[...])
    share(full[:rank] + full[rank : 2 * rank] + full[2 * rank :], slice(0, full.shape[1]), send_a, keep_a)


def attend_heads(
    pair, samples, bias_ref, gain_ref, q_ref, k_ref, v_ref, x_ref, kt_ref, vt_ref, loss_ref, k_s, v_s, dk_s, dv_s, gq
):
    rows = q_ref.shape[2]
    block = min(rows, 160)
    heads = range(pair)
    for j in heads:
        for m in range(2):
            k_s[j, m, :rows, :] = k_ref[j, m]
            k_s[j, m, rows:, :] = kt_ref[j, m]
            v_s[j, m, :rows, :] = v_ref[j, m]
            v_s[j, m, rows:, :] = vt_ref[j, m]
    if rows > block:
        dk_s[...] = jnp.zeros_like(dk_s)
        dv_s[...] = jnp.zeros_like(dv_s)
    gain_q, gain_k = gain_ref[0:1, :], gain_ref[1:2, :]

    def attend(start):
        at = pl.ds(start, block)
        both = [(j, m) for j in heads for m in range(2)]
        scores = {(j, m): nt(q_ref[j, m, at, :], k_s[j, m]) for j, m in both}
        weights = {i: jnp.exp2(scores[i] * (ROOT * LOG2E) + bias_ref[...]) for i in both}
        scale = {i: 1.0 / jnp.sum(weights[i], axis=1, keepdims=True) for i in both}
        probs = {i: weights[i] * scale[i] for i in both}
        rounded = {i: probs[i].astype(BF16) for i in both}
        out = {(j, m): nn(rounded[j, m], v_s[j, m]) for j, m in both}
        diff = [out[j, 1] - out[j, 0].astype(BF16).astype(F32) for j in heads]
        total = diff[0] * diff[0]
        for d in diff[1:]:
            total = total + d * d
        loss_ref[...] += jnp.sum(total.reshape(block // 8, 8, HD), axis=0)
        dout = [(d * (2.0 / samples)).astype(BF16) for d in diff]
        dprobs = [nt(dout[j], v_s[j, 1]).astype(BF16).astype(F32) for j in heads]
        dv = [tn(rounded[j, 1], dout[j]) for j in heads]
        inner = [jnp.sum(dprobs[j] * probs[j, 1], axis=1, keepdims=True) for j in heads]
        dscores = [(probs[j, 1] * (dprobs[j] - inner[j]) * ROOT).astype(BF16) for j in heads]
        dq = [nn(dscores[j], k_s[j, 1]).astype(BF16).astype(F32) for j in heads]
        dk = [tn(dscores[j], q_ref[j, 1, at, :]) for j in heads]
        for j in heads:
            c = j * 3 * HD
            gq[at, c : c + HD] = norm_pull(x_ref[j, 0, at, :], gain_q, dq[j]).astype(BF16)
            if rows > block:
                dk_s[j] += dk[j][:rows]
                dv_s[j] += dv[j][:rows]
            else:
                dk_s[j] = dk[j][:rows]
                dv_s[j] = dv[j][:rows]

    over(rows, block, attend)

    def rest(start):
        at = pl.ds(start, block)
        for j in heads:
            c = j * 3 * HD
            dk = dk_s[j, at, :].astype(BF16).astype(F32)
            gq[at, c + HD : c + 2 * HD] = norm_pull(x_ref[j, 1, at, :], gain_k, dk).astype(BF16)
            gq[at, c + 2 * HD : c + 3 * HD] = dv_s[j, at, :].astype(BF16)

    over(rows, block, rest)


def attend(where, bias, gain, up, image, text):
    q, k, v, x, low, hs = image
    kt, vt = text
    (rank, img_cols), width = up.shape, hs.shape[1]
    count, _, rows, _ = q.shape
    trows = kt.shape[2]
    pair, steps = split(count)
    half, ic = rank // 2, pair * 3 * HD
    samples = lax.axis_size("grp") * lax.axis_size("dp")
    out_a, out_b = (half, width), (half, img_cols)
    return pl.pallas_call(
        functools.partial(attend_kernel, steps, pair, samples),
        in_specs=[pl.BlockSpec(memory_space=pltpu.SMEM)] + [VMEM] * 11,
        out_specs=[VMEM] * 5,
        out_shape=[
            jax.ShapeDtypeStruct(out_a, BF16),
            jax.ShapeDtypeStruct(out_a, F32),
            jax.ShapeDtypeStruct(out_b, BF16),
            jax.ShapeDtypeStruct(out_b, F32),
            jax.ShapeDtypeStruct((8, HD), F32),
        ],
        scratch_shapes=[
            pltpu.VMEM((rank, rows), BF16),
            pltpu.VMEM((rank, rows), F32),
            pltpu.VMEM((pair, 2, rows + trows, HD), BF16),
            pltpu.VMEM((pair, 2, rows + trows, HD), BF16),
            pltpu.VMEM((pair, rows, HD), F32),
            pltpu.VMEM((pair, rows, HD), F32),
            pltpu.VMEM((rows, ic), BF16),
            pltpu.VMEM((rank, max(width, ic)), F32),
        ],
        compiler_params=pltpu.CompilerParams(vmem_limit_bytes=2 * SMALL),
        cost_estimate=pl.CostEstimate(
            flops=16 * count * rows * (rows + trows) * HD,
            bytes_accessed=8_000_000,
            transcendentals=2 * count * rows * (rows + trows),
        ),
        name="attend",
    )(where, bias, gain, up, q, k, v, x, kt, vt, low, hs)


def noise_level(step_ref, shape):
    return (jnp.full(shape, step_ref[0], jnp.int32).astype(F32) + 1.0) / STEPS


def embedding(value):
    count = value.shape[1] // 2
    lane = lax.broadcasted_iota(jnp.int32, value.shape, 1)
    place = lax.rem(lane, count).astype(F32)
    angles = 1000.0 * value * jnp.exp(-math.log(10000.0) * place / count)
    wave = jnp.where(lane < count, jnp.cos(angles), jnp.sin(angles))
    return wave / (1.0 + jnp.exp(-wave))


def modulation_kernel(step_ref, guidance_ref, weight_ref, part_ref, emb):
    @pl.when(pl.program_id(0) == 0)
    def _():
        half = emb.shape[1] // 2
        time = embedding(noise_level(step_ref, (1, half)))
        guide = embedding(jnp.full((1, half), guidance_ref[0], F32))
        row = lax.broadcasted_iota(jnp.int32, (emb.shape[0], half), 0)
        emb[:, :half] = jnp.where(row >= 0, time, 0.0).astype(BF16)
        emb[:, half:] = jnp.where(row == 0, guide, 0.0).astype(BF16)

    part_ref[...] = nn(emb[...], weight_ref[...])[: part_ref.shape[0]]


SCALAR = pl.BlockSpec(memory_space=pltpu.SMEM)


def modulation(timestep, guidance, weight):
    depth, cols = weight.shape
    steps = 2 if cols % 256 == 0 else 1
    return pl.pallas_call(
        modulation_kernel,
        grid=(steps,),
        in_specs=[SCALAR, SCALAR, pl.BlockSpec((depth, cols // steps), lambda s: (0, s))],
        out_specs=pl.BlockSpec((2, cols // steps), lambda s: (0, s)),
        out_shape=jax.ShapeDtypeStruct((2, cols), F32),
        scratch_shapes=[pltpu.VMEM((16, depth), BF16)],
        compiler_params=params(10),
        cost_estimate=pl.CostEstimate(
            flops=4 * depth * cols, bytes_accessed=2 * weight.size, transcendentals=0
        ),
        name="modulation",
    )(timestep, guidance, held(weight))


def noisy_kernel(step_ref, image_ref, noise_ref, after_ref, noisy_ref):
    sigma = noise_level(step_ref, (1, image_ref.shape[1]))
    clean, noise = image_ref[...].astype(F32), noise_ref[...].astype(F32)
    noisy_ref[...] = ((1.0 - sigma) * clean + sigma * noise).astype(BF16)


def mix(timestep, image, noise, after):
    rows, width = image.shape
    steps = 2 if width % 256 == 0 else 1
    tokens = pl.BlockSpec((rows, width // steps), lambda s: (0, s))
    return pl.pallas_call(
        noisy_kernel,
        grid=(steps,),
        in_specs=[SCALAR, tokens, tokens, pl.BlockSpec(memory_space=pl.ANY)],
        out_specs=tokens,
        out_shape=jax.ShapeDtypeStruct((rows, width), BF16),
        compiler_params=params(10),
        cost_estimate=pl.CostEstimate(flops=0, bytes_accessed=6 * image.size, transcendentals=0),
        name="noisy",
    )(timestep, held(image), held(noise), after)


def finish_kernel(scale_a, scale_b, scale_loss, side_ref, a_ref, b_ref, sums_ref, got_ref, out_a, out_b, loss_ref):
    half = HD // 2
    rows, width, cols = a_ref.shape[0], a_ref.shape[1], b_ref.shape[1]
    at = rows // 8 * (width + cols)
    other = [got_ref[:, at + i * HD : at + (i + 1) * HD].astype(F32) for i in range(3)]
    total = jnp.sum(sums_ref[...] + (other[0] + other[1] + other[2]), axis=0, keepdims=True)
    loss_ref[...] = jnp.sum(total[:, :half], axis=1, keepdims=True) * scale_loss
    squares_b = jnp.sum(total[:, half:], axis=1, keepdims=True) * scale_b
    unit_b = lax.rsqrt(squares_b + EPS)
    blocks = range(rows // 8)
    mine = [lambda b=b: a_ref[8 * b : 8 * b + 8, :].astype(F32) for b in blocks]
    theirs = [lambda b=b: got_ref[:, b * width : (b + 1) * width].astype(F32) for b in blocks]

    def squares(parts):
        each = functools.reduce(lambda x, y: x + y, [p() * p() for p in parts])
        return jnp.sum(jnp.sum(each, axis=0, keepdims=True), axis=1, keepdims=True)

    unit_a = lax.rsqrt((squares(mine) + squares(theirs)) * scale_a + EPS)
    side = side_ref[0]
    at = rows // 8 * width
    for b in blocks:
        own = pl.ds(pl.multiple_of(side * rows + 8 * b, 8), 8)
        far = pl.ds(pl.multiple_of((1 - side) * rows + 8 * b, 8), 8)
        out_a[own, :] = mine[b]() * unit_a
        out_a[far, :] = theirs[b]() * unit_a
        out_b[own, :] = b_ref[8 * b : 8 * b + 8, :].astype(F32) * unit_b
        out_b[far, :] = got_ref[:, at + b * cols : at + (b + 1) * cols].astype(F32) * unit_b


def finish(side, grad_a, grad_b, sums, got, n, entries):
    (half, width), cols = grad_a.shape, grad_b.shape[1]
    rank = 2 * half
    return pl.pallas_call(
        functools.partial(finish_kernel, 1.0 / (rank * width), 1.0 / (rank * cols * n), 1.0 / entries),
        in_specs=[pl.BlockSpec(memory_space=pltpu.SMEM)] + [VMEM] * 4,
        compiler_params=pltpu.CompilerParams(vmem_limit_bytes=SMALL),
        out_shape=[
            jax.ShapeDtypeStruct((rank, width), F32),
            jax.ShapeDtypeStruct((rank, cols), F32),
            jax.ShapeDtypeStruct((1, 1), F32),
        ],
        name="finish",
    )(side, grad_a, grad_b, sums, got)


def shifted(x, axis, k):
    size = lax.axis_size(axis)
    return lax.ppermute(x, axis, [(i, (i + k) % size) for i in range(size)])


def packed(arrays):
    return len(arrays) > 1 and all(x.shape[0] % 8 == 0 and x.shape[1] % HD == 0 for x in arrays)


def pack(arrays):
    return jnp.concatenate([x[r : r + 8] for x in arrays for r in range(0, x.shape[0], 8)], 1)


def unpack(message, arrays):
    out, at = [], 0
    for x in arrays:
        blocks = []
        for _ in range(0, x.shape[0], 8):
            blocks.append(message[:, at : at + x.shape[1]])
            at += x.shape[1]
        out.append(blocks[0] if len(blocks) == 1 else jnp.concatenate(blocks, 0))
    return out


def send(arrays, group, hop):
    pairs = [(i, i ^ group.mask(hop)) for i in range(group.size)]
    if not packed(arrays):
        return [lax.ppermute(x, group.axes, pairs) for x in arrays]
    return unpack(lax.ppermute(pack(arrays), group.axes, pairs), arrays)


class Group:
    def __init__(self, *places):
        self.axes = tuple(a for a in ("grp", "seq", "dp") if any(a == p[0] for p in places))
        self.size = math.prod(lax.axis_size(a) for a in self.axes)
        self.places = places
        self.count = 1 << len(places)
        sides = [lax.rem(lax.div(lax.axis_index(a), bit), 2) for a, bit in places]
        self.me = functools.reduce(lambda total, side: 2 * total + side, sides, 0)

    def mask(self, hop):
        total = 0
        for i, (axis, bit) in enumerate(reversed(self.places)):
            if hop >> i & 1:
                below = self.axes[self.axes.index(axis) + 1 :]
                total ^= bit * math.prod(lax.axis_size(a) for a in below)
        return total


def cut_of(x, count):
    if x.shape[0] % (8 * count) == 0:
        return 0
    return 1 if x.shape[1] % (count * HD) == 0 else 0


def block(x, dim, count, index):
    each = x.shape[dim] // count
    return lax.dynamic_slice_in_dim(x, index * each, each, dim)


def scatter(wide, narrow=()):
    arrays, group = wide
    more, part = narrow or ([], None)
    dims = [cut_of(x, group.count) for x in arrays]
    more_dims = [cut_of(x, part.count) for x in more]
    sums = [block(x, d, group.count, group.me) for x, d in zip(arrays, dims)]
    more_sums = [block(x, d, part.count, part.me) for x, d in zip(more, more_dims)]
    for hop in range(1, group.count):
        out = [block(x, d, group.count, group.me ^ hop).astype(BF16) for x, d in zip(arrays, dims)]
        join = part is not None and hop < part.count
        if join:
            out += [block(x, d, part.count, part.me ^ hop).astype(BF16) for x, d in zip(more, more_dims)]
        got = [g.astype(F32) for g in send(out, group, hop)]
        sums = [t + g for t, g in zip(sums, got)]
        if join:
            more_sums = [t + g for t, g in zip(more_sums, got[len(sums) :])]
    return sums, dims, more_sums, more_dims


def ordered(parts, me):
    return [
        functools.reduce(
            lambda so_far, hop: jnp.where(me == j ^ hop, parts[hop], so_far), range(1, len(parts)), parts[0]
        )
        for j in range(len(parts))
    ]


def gather(wide, sums, narrow=()):
    arrays, dims, group = wide
    more, more_dims, part = narrow or ([], [], None)
    parts = [[x] for x in arrays]
    more_parts = [[x] for x in more]
    totals = [sums]
    for hop in range(1, group.count):
        join = part is not None and hop < part.count
        out = [*arrays, *(more if join else []), pieces(sums)]
        *got, other = send(out, group, hop)
        other = other.astype(F32)
        totals.append(other[:, :HD] + other[:, HD : 2 * HD] + other[:, 2 * HD :])
        for so_far, g in zip(parts + (more_parts if join else []), got):
            so_far.append(g)
    totals = ordered(totals, group.me)
    sums = functools.reduce(lambda x, y: x + y, totals)
    whole = [jnp.concatenate(ordered(p, group.me), d) for p, d in zip(parts, dims)]
    more_whole = [jnp.concatenate(ordered(p, part.me), d) for p, d in zip(more_parts, more_dims)]
    return whole, more_whole, sums


def pieces(value):
    first = lax.reduce_precision(value, 8, 7)
    rest = value - first
    second = lax.reduce_precision(rest, 8, 7)
    return jnp.concatenate([first, second, rest - second], 1).astype(BF16)


def bits(axis):
    size = lax.axis_size(axis)
    return [1 << i for i in range(size.bit_length() - 1)]


def fold(x):
    half = HD // 2
    return functools.reduce(
        lambda total, c: total + x[:, c : c + half], range(half, x.shape[1], half), x[:, :half]
    )


def on_device(
    image,
    noise,
    text,
    timestep,
    guidance,
    text_token_length,
    image_projection_weight,
    text_projection_weight,
    modulation_weight,
    query_key_norm_gain,
    adapter_down_weight,
    adapter_up_weight,
):
    n, me = lax.axis_size("seq"), lax.axis_index("seq")
    samples = lax.axis_size("grp") * lax.axis_size("dp")
    part = modulation(timestep, guidance, modulation_weight)
    noisy = mix(timestep, image[0], noise[0], part)
    mods = [part] + [shifted(part, "seq", k) for k in range(1, n)]
    noisy_parts = [noisy] + [shifted(noisy, "seq", k) for k in range(1, n)]
    words = text[0]
    text_parts = [words] + [shifted(words, "seq", k) for k in range(1, n)]
    origin = [lax.rem(me + n - k, n) for k in range(n)]
    ordered = [
        functools.reduce(
            lambda so_far, k: jnp.where(origin[k] == j, mods[k], so_far), range(1, n), mods[0]
        )
        for j in range(n)
    ]
    mod = jnp.concatenate(ordered, 1)
    img_part, txt_part = noisy.shape[0], words.shape[0]
    place = jnp.concatenate(
        [jnp.zeros((n * img_part,), jnp.int32)]
        + [origin[k] * txt_part + jnp.arange(txt_part, dtype=jnp.int32) for k in range(n)]
    )
    bias = jnp.where(place < text_token_length[0], 0.0, -1000000000.0).astype(F32)[None]
    core = lax.rem(lax.axis_index("grp"), 2).astype(jnp.int32)
    gain = query_key_norm_gain
    steps = split(image_projection_weight.shape[1] // (3 * HD))[1]
    gain, down, up, weights = fetch(
        [gain, adapter_down_weight.T, adapter_up_weight], image_projection_weight, steps, noisy
    )
    far_weights, image_heads = held(image_projection_weight), []
    for k in range(n):
        if k == n - 1:
            far_weights = held(text_projection_weight)
        image_heads = project_image(
            k, n, image_heads, mod, gain, down, up, weights, noisy_parts[k], far_weights
        )
        if k == 0:
            *image_heads, weights = image_heads
    *image_heads, text_weights = image_heads
    text_heads = project_text(mod, gain, text_weights, text_parts)
    send_a, keep_a, send_b, keep_b, loss = attend(
        core[None], bias, gain, up, image_heads, text_heads
    )
    cores = Group(("grp", 1))
    (got_a,), (got_b,) = send([send_a], cores, 1), send([send_b], cores, 1)
    grad_a, grad_b = keep_a + got_a.astype(F32), keep_b + got_b.astype(F32)
    last, *far = bits("seq")
    far = [(Group(("seq", bit)), []) for bit in reversed(far)]
    for group, dims in far:
        (grad_a,), dims[:], _, _ = scatter(([grad_a], group))
    near, across = Group(("seq", last), ("grp", 2)), Group(("grp", 2))
    (grad_a,), dims_a, (grad_b,), dims_b = scatter(([grad_a], near), ([grad_b], across))
    line = Group(*[("dp", bit) for bit in reversed(bits("dp"))])
    (grad_a, grad_b), dims_z, _, _ = scatter(([grad_a, grad_b], line))
    squares = fold(jnp.sum(grad_b.reshape(-1, min(grad_b.shape[0], 8), grad_b.shape[1]) ** 2, 0))
    squares = jnp.pad(squares, ((0, 8 - squares.shape[0]), (0, 0)))
    sums = jnp.concatenate([fold(loss), squares], 1)
    grads, _, sums = gather(([grad_a.astype(BF16), grad_b.astype(BF16)], dims_z, line), sums)
    (grad_a,), (grad_b,), sums = gather(
        (grads[:1], dims_a, near), sums, (grads[1:], dims_b, across)
    )
    for group, dims in reversed(far):
        (grad_a,), _, sums = gather(([grad_a], dims, group), sums)
    pairs = [(i, i ^ 1) for i in range(cores.size)]
    got = lax.ppermute(pack([grad_a, grad_b, pieces(sums)]), "grp", pairs)
    direction_a, direction_b, loss_mean = finish(
        core[None], grad_a, grad_b, sums, got, n, samples * n * img_part * HEADS * HD
    )
    return (direction_a.T, direction_b, loss_mean[0, 0])


def solution(mesh):
    in_specs = (
        P(("grp", "dp"), "seq", None),
        P(("grp", "dp"), "seq", None),
        P(("grp", "dp"), "seq", None),
        P(("grp", "dp")),
        P(("grp", "dp")),
        P(("grp", "dp")),
        P(None, "seq"),
        P(None, "seq"),
        P(None, "seq"),
        P(),
        P(),
        P(None, "seq"),
    )
    out_specs = (P(), P(None, "seq"), P())
    return jax.shard_map(
        on_device, mesh=mesh, in_specs=in_specs, out_specs=out_specs, check_vma=False
    )
```

```python
import functools
import math

import jax
import jax.numpy as jnp
from jax import lax
from jax.experimental import pallas as pl
from jax.experimental.pallas import tpu as pltpu
from jax.sharding import PartitionSpec as P

HD = 128
HEADS = 16
STEPS = 1000
EPS = 1e-06
F32 = jnp.float32
BF16 = jnp.bfloat16
ROOT = 1.0 / math.sqrt(HD)
LOG2E = 1.0 / math.log(2.0)
SMALL = 10 * 1024 * 1024
VMEM = pl.BlockSpec(memory_space=pltpu.VMEM)
HELD = pl.BlockSpec(memory_space=pltpu.HBM)


def nn(a, b):
    return lax.dot_general(a, b, (((1,), (0,)), ((), ())), preferred_element_type=F32)


def nt(a, b):
    return lax.dot_general(a, b, (((1,), (1,)), ((), ())), preferred_element_type=F32)


def tn(a, b):
    return lax.dot_general(a, b, (((0,), (0,)), ((), ())), preferred_element_type=F32)


def over(total, size, body):
    if total == size:
        body(0)
    else:

        @pl.loop(0, total // size)
        def _(i):
            body(pl.multiple_of(i * size, size))


def inverse_rms(x):
    return lax.rsqrt(jnp.mean(x * x, axis=-1, keepdims=True) + EPS)


def norm_pull(x, gain, dy):
    r = inverse_rms(x)
    u = gain * dy
    return r * (u - x * (r * r * jnp.mean(x * u, axis=-1, keepdims=True)))


def modulate(tokens, mod_ref, kind, width, dest, rows, base):
    size = tokens.shape[0]

    @pl.loop(0, size // 16)
    def _(i):
        v = tokens[pl.ds(pl.multiple_of(i * 16, 16), 16), :].astype(F32)
        center = v - jnp.mean(v, axis=1, keepdims=True)
        spread = jnp.mean(center * center, axis=1, keepdims=True)
        unit = center * lax.rsqrt(spread + EPS)
        for m in range(2):
            shift = mod_ref[m : m + 1, kind * width : (kind + 1) * width]
            scale = mod_ref[m : m + 1, (kind + 1) * width : (kind + 2) * width]
            at = pl.multiple_of(m * rows + base + i * 16, 16)
            dest[pl.ds(at, 16), :] = (unit * (1.0 + scale) + shift).astype(BF16)


def normed(x, gain):
    return (x * inverse_rms(x) * gain).astype(BF16)


def held(x):
    return pltpu.with_memory_space_constraint(x, pltpu.HBM)


def text_kernel(n, pair, mod_ref, gain_ref, w_ref, after_ref, *refs):
    parts, (k_ref, v_ref, ht, weights, sems) = refs[:n], refs[n:]
    copies = [chunk(w_ref, weights, sems, i) for i in range(sems.shape[0])]
    for copy in copies:
        copy.start()
    rows = n * parts[0].shape[0]
    for k in range(n):
        modulate(parts[k], mod_ref, 2, w_ref.shape[0], ht, rows, k * parts[0].shape[0])
    cols = pair * 2 * HD
    size = min(rows, 96)
    for step, copy in enumerate(copies):
        copy.wait()

        def project(start, step=step):
            for j in range(pair):
                head, c = step * pair + j, step * cols + j * 2 * HD
                w = weights[:, c : c + 2 * HD]
                if size == rows:
                    both = nn(ht[...], w)
                    own = [both[:rows], both[rows:]]
                else:
                    own = [nn(ht[pl.ds(m * rows + start, size), :], w) for m in range(2)]
                for m, kv in enumerate(own):
                    k_ref[head, m, pl.ds(start, size), :] = normed(kv[:, :HD], gain_ref[2:3, :])
                    v_ref[head, m, pl.ds(start, size), :] = kv[:, HD:].astype(BF16)

        over(rows, size, project)


def split(count):
    pair = 2 if count % 2 == 0 else 1
    return pair, count // pair


def params(mib):
    return pltpu.CompilerParams(
        dimension_semantics=("arbitrary",), vmem_limit_bytes=mib * 1024 * 1024
    )


def project_text(mod, gain, w, after, parts):
    n, (part, width) = len(parts), parts[0].shape
    pair, steps = split(w.shape[1] // (2 * HD))
    out = pltpu.VMEM((pair * steps, 2, n * part, HD), BF16)
    return pl.pallas_call(
        functools.partial(text_kernel, n, pair),
        in_specs=[VMEM, VMEM, HELD, pl.BlockSpec(memory_space=pl.ANY)] + [VMEM] * n,
        out_specs=[VMEM] * 2,
        out_shape=[out, out],
        scratch_shapes=[
            pltpu.VMEM((2 * n * part, width), BF16),
            pltpu.VMEM(w.shape, w.dtype),
            pltpu.SemaphoreType.DMA((steps,)),
        ],
        compiler_params=pltpu.CompilerParams(vmem_limit_bytes=2 * SMALL),
        cost_estimate=pl.CostEstimate(
            flops=4 * n * part * w.size, bytes_accessed=2 * w.size, transcendentals=0
        ),
        name="project_text",
    )(mod, gain, w, after, *parts)


def chunk(w_ref, out_ref, sems, index):
    cols = w_ref.shape[1] // sems.shape[0]
    at = pl.ds(index * cols if isinstance(index, int) else pl.multiple_of(index * cols, cols), cols)
    return pltpu.make_async_copy(w_ref.at[:, at], out_ref.at[:, at], sems.at[index])


def fetch_kernel(after_ref, *refs):
    *given, last_sems, sems = refs
    count = len(given) // 2
    copies = [
        pltpu.make_async_copy(given[i], given[count + i], sems.at[i]) for i in range(count - 1)
    ]
    copies.append(chunk(given[count - 1], given[-1], last_sems, 0))
    for copy in copies:
        copy.start()
    for copy in copies:
        copy.wait()


def fetch(small, w, steps, after):
    arrays = [*small, w]
    return pl.pallas_call(
        fetch_kernel,
        in_specs=[pl.BlockSpec(memory_space=pl.ANY)] + [HELD] * len(arrays),
        out_specs=[VMEM] * len(arrays),
        out_shape=[pltpu.VMEM(x.shape, x.dtype) for x in arrays],
        scratch_shapes=[pltpu.SemaphoreType.DMA((steps,)), pltpu.SemaphoreType.DMA((len(small),))],
        compiler_params=pltpu.CompilerParams(vmem_limit_bytes=SMALL),
        cost_estimate=pl.CostEstimate(
            flops=0, bytes_accessed=2 * w.size // steps, transcendentals=0
        ),
        name="fetch",
    )(after, *[held(x) for x in arrays])


def image_kernel(pair, index, mod_ref, gain_ref, down_ref, up_ref, w_ref, tokens, *refs):
    first = index == 0
    q_ref, k_ref, v_ref, x_ref, low_ref, hs_ref, *rest = refs[1 if first else 6 :]
    weights = w_ref
    if first:
        weights, hi, sems = rest
        for i in range(1, sems.shape[0]):
            chunk(w_ref, weights, sems, i).start()
    else:
        (hi,) = rest
    rows = tokens.shape[0]
    part = slice(index * rows, (index + 1) * rows)
    modulate(tokens, mod_ref, 0, w_ref.shape[0], hi, rows, 0)
    hs_ref[part, :] = hi[rows:, :]
    low_ref[part, :] = nt(hi[rows:, :], down_ref[...]).astype(BF16)
    cols = pair * 3 * HD

    def project(step):
        columns = pl.ds(pl.multiple_of(step * cols, cols), cols)
        if first:

            @pl.when(step > 0)
            def _():
                chunk(w_ref, weights, sems, step).wait()

        out = nn(hi[...], weights[:, columns])
        student = out[rows:] + nn(low_ref[part, :], up_ref[:, columns])
        for j in range(pair):
            head, c = step * pair + j, j * 3 * HD
            for m, own in enumerate((out[:rows], student)):
                for kind, dest in enumerate((q_ref, k_ref)):
                    x = own[:, c + kind * HD : c + (kind + 1) * HD]
                    dest[head, m, part, :] = normed(x, gain_ref[kind : kind + 1, :])
                    if m == 1:
                        x_ref[head, kind, part, :] = x
                v_ref[head, m, part, :] = own[:, c + 2 * HD : c + 3 * HD].astype(BF16)

    pl.loop(0, w_ref.shape[1] // cols)(project)


def project_image(part, n, before, mod, gain, down, up, w, tokens, far):
    (rows, width), rank = tokens.shape, up.shape[0]
    pair, steps = split(w.shape[1] // (3 * HD))
    heads = (pair * steps, 2, n * rows, HD)
    shapes = [pltpu.VMEM(heads, BF16)] * 3 + [
        pltpu.VMEM(heads, F32),
        pltpu.VMEM((n * rows, rank), BF16),
        pltpu.VMEM((n * rows, width), BF16),
    ]
    scratch = [pltpu.VMEM((2 * rows, width), BF16)]
    operands, specs = [mod, gain, down, up, w, tokens], [VMEM] * 6
    aliases = {6 + i: i for i in range(len(before))}
    if part == 0:
        operands[4], specs[4] = far, HELD
        before, aliases = [w], {6: 6}
        shapes.append(pltpu.VMEM(w.shape, w.dtype))
        scratch.append(pltpu.SemaphoreType.DMA((steps,)))
    return pl.pallas_call(
        functools.partial(image_kernel, pair, part),
        in_specs=specs + [VMEM] * len(before),
        out_specs=[VMEM] * len(shapes),
        out_shape=shapes,
        input_output_aliases=aliases,
        scratch_shapes=scratch,
        compiler_params=pltpu.CompilerParams(vmem_limit_bytes=SMALL),
        cost_estimate=pl.CostEstimate(
            flops=4 * rows * w.size, bytes_accessed=2 * w.size, transcendentals=0
        ),
        name="project_image",
    )(*operands, *before)


def attend_kernel(
    steps, pair, samples, where_ref, bias_ref, gain_ref, up_ref, q_ref, k_ref, v_ref, x_ref, kt_ref, vt_ref,
    low_ref, hs_ref, send_a, keep_a, send_b, keep_b, loss_ref, lowt, glt, k_s, v_s, dk_s, dv_s, gq, whole
):
    core = where_ref[0]
    half = send_a.shape[0]
    lowt[...] = low_ref[...].astype(F32).T.astype(BF16)
    glt[...] = jnp.zeros_like(glt)
    loss_ref[...] = jnp.zeros_like(loss_ref)

    def share(value, columns, send, keep):
        whole[:, : value.shape[1]] = value
        mine = pl.ds(pl.multiple_of(core * half, 8), half)
        other = pl.ds(pl.multiple_of((1 - core) * half, 8), half)
        keep[:, columns] = whole[mine, : value.shape[1]]
        send[:, columns] = whole[other, : value.shape[1]].astype(send.dtype)

    @pl.loop(0, steps)
    def _(step):
        columns = pl.ds(pl.multiple_of(step * gq.shape[1], HD), gq.shape[1])
        group = pl.ds(step * pair, pair)
        attend_heads(
            pair, samples, bias_ref, gain_ref, *[r.at[group] for r in (q_ref, k_ref, v_ref, x_ref, kt_ref, vt_ref)],
            loss_ref, k_s, v_s, dk_s, dv_s, gq,
        )
        share(nn(lowt[...], gq[...]), columns, send_b, keep_b)
        glt[...] += nt(up_ref[:, columns], gq[...])

    g = glt[...]
    g1 = g.astype(BF16)
    rest = g - g1.astype(F32)
    g2 = rest.astype(BF16)
    g3 = (rest - g2.astype(F32)).astype(BF16)
    stack = jnp.concatenate([g1, g2, g3], 0)
    rank = g.shape[0]
    full = nn(stack, hs_ref[...])
    share(full[:rank] + full[rank : 2 * rank] + full[2 * rank :], slice(0, full.shape[1]), send_a, keep_a)


def attend_heads(
    pair, samples, bias_ref, gain_ref, q_ref, k_ref, v_ref, x_ref, kt_ref, vt_ref, loss_ref, k_s, v_s, dk_s, dv_s, gq
):
    rows = q_ref.shape[2]
    block = min(rows, 160)
    heads = range(pair)
    for j in heads:
        for m in range(2):
            k_s[j, m, :rows, :] = k_ref[j, m]
            k_s[j, m, rows:, :] = kt_ref[j, m]
            v_s[j, m, :rows, :] = v_ref[j, m]
            v_s[j, m, rows:, :] = vt_ref[j, m]
    if rows > block:
        dk_s[...] = jnp.zeros_like(dk_s)
        dv_s[...] = jnp.zeros_like(dv_s)
    gain_q, gain_k = gain_ref[0:1, :], gain_ref[1:2, :]

    def attend(start):
        at = pl.ds(start, block)
        both = [(j, m) for j in heads for m in range(2)]
        scores = {(j, m): nt(q_ref[j, m, at, :], k_s[j, m]) for j, m in both}
        weights = {i: jnp.exp2(scores[i] * (ROOT * LOG2E) + bias_ref[...]) for i in both}
        scale = {i: 1.0 / jnp.sum(weights[i], axis=1, keepdims=True) for i in both}
        probs = {i: weights[i] * scale[i] for i in both}
        rounded = {i: probs[i].astype(BF16) for i in both}
        out = {(j, m): nn(rounded[j, m], v_s[j, m]) for j, m in both}
        diff = [out[j, 1] - out[j, 0].astype(BF16).astype(F32) for j in heads]
        total = diff[0] * diff[0]
        for d in diff[1:]:
            total = total + d * d
        loss_ref[...] += jnp.sum(total.reshape(block // 8, 8, HD), axis=0)
        dout = [(d * (2.0 / samples)).astype(BF16) for d in diff]
        dprobs = [nt(dout[j], v_s[j, 1]).astype(BF16).astype(F32) for j in heads]
        dv = [tn(rounded[j, 1], dout[j]) for j in heads]
        inner = [jnp.sum(dprobs[j] * probs[j, 1], axis=1, keepdims=True) for j in heads]
        dscores = [(probs[j, 1] * (dprobs[j] - inner[j]) * ROOT).astype(BF16) for j in heads]
        dq = [nn(dscores[j], k_s[j, 1]).astype(BF16).astype(F32) for j in heads]
        dk = [tn(dscores[j], q_ref[j, 1, at, :]) for j in heads]
        for j in heads:
            c = j * 3 * HD
            gq[at, c : c + HD] = norm_pull(x_ref[j, 0, at, :], gain_q, dq[j]).astype(BF16)
            if rows > block:
                dk_s[j] += dk[j][:rows]
                dv_s[j] += dv[j][:rows]
            else:
                dk_s[j] = dk[j][:rows]
                dv_s[j] = dv[j][:rows]

    over(rows, block, attend)

    def rest(start):
        at = pl.ds(start, block)
        for j in heads:
            c = j * 3 * HD
            dk = dk_s[j, at, :].astype(BF16).astype(F32)
            gq[at, c + HD : c + 2 * HD] = norm_pull(x_ref[j, 1, at, :], gain_k, dk).astype(BF16)
            gq[at, c + 2 * HD : c + 3 * HD] = dv_s[j, at, :].astype(BF16)

    over(rows, block, rest)


def attend(where, bias, gain, up, image, text):
    q, k, v, x, low, hs = image
    kt, vt = text
    (rank, img_cols), width = up.shape, hs.shape[1]
    count, _, rows, _ = q.shape
    trows = kt.shape[2]
    pair, steps = split(count)
    half, ic = rank // 2, pair * 3 * HD
    samples = lax.axis_size("grp") * lax.axis_size("dp")
    out_a, out_b = (half, width), (half, img_cols)
    return pl.pallas_call(
        functools.partial(attend_kernel, steps, pair, samples),
        in_specs=[pl.BlockSpec(memory_space=pltpu.SMEM)] + [VMEM] * 11,
        out_specs=[VMEM] * 5,
        out_shape=[
            jax.ShapeDtypeStruct(out_a, BF16),
            jax.ShapeDtypeStruct(out_a, F32),
            jax.ShapeDtypeStruct(out_b, BF16),
            jax.ShapeDtypeStruct(out_b, F32),
            jax.ShapeDtypeStruct((8, HD), F32),
        ],
        scratch_shapes=[
            pltpu.VMEM((rank, rows), BF16),
            pltpu.VMEM((rank, rows), F32),
            pltpu.VMEM((pair, 2, rows + trows, HD), BF16),
            pltpu.VMEM((pair, 2, rows + trows, HD), BF16),
            pltpu.VMEM((pair, rows, HD), F32),
            pltpu.VMEM((pair, rows, HD), F32),
            pltpu.VMEM((rows, ic), BF16),
            pltpu.VMEM((rank, max(width, ic)), F32),
        ],
        compiler_params=pltpu.CompilerParams(vmem_limit_bytes=2 * SMALL),
        cost_estimate=pl.CostEstimate(
            flops=16 * count * rows * (rows + trows) * HD,
            bytes_accessed=8_000_000,
            transcendentals=2 * count * rows * (rows + trows),
        ),
        name="attend",
    )(where, bias, gain, up, q, k, v, x, kt, vt, low, hs)


def noise_level(step_ref, shape):
    return (jnp.full(shape, step_ref[0], jnp.int32).astype(F32) + 1.0) / STEPS


def embedding(value):
    count = value.shape[1] // 2
    lane = lax.broadcasted_iota(jnp.int32, value.shape, 1)
    place = lax.rem(lane, count).astype(F32)
    angles = 1000.0 * value * jnp.exp(-math.log(10000.0) * place / count)
    wave = jnp.where(lane < count, jnp.cos(angles), jnp.sin(angles))
    return wave / (1.0 + jnp.exp(-wave))


def modulation_kernel(step_ref, guidance_ref, weight_ref, part_ref, emb):
    @pl.when(pl.program_id(0) == 0)
    def _():
        half = emb.shape[1] // 2
        time = embedding(noise_level(step_ref, (1, half)))
        guide = embedding(jnp.full((1, half), guidance_ref[0], F32))
        row = lax.broadcasted_iota(jnp.int32, (emb.shape[0], half), 0)
        emb[:, :half] = jnp.where(row >= 0, time, 0.0).astype(BF16)
        emb[:, half:] = jnp.where(row == 0, guide, 0.0).astype(BF16)

    part_ref[...] = nn(emb[...], weight_ref[...])[: part_ref.shape[0]]


SCALAR = pl.BlockSpec(memory_space=pltpu.SMEM)


def modulation(timestep, guidance, weight):
    depth, cols = weight.shape
    steps = 2 if cols % 256 == 0 else 1
    return pl.pallas_call(
        modulation_kernel,
        grid=(steps,),
        in_specs=[SCALAR, SCALAR, pl.BlockSpec((depth, cols // steps), lambda s: (0, s))],
        out_specs=pl.BlockSpec((2, cols // steps), lambda s: (0, s)),
        out_shape=jax.ShapeDtypeStruct((2, cols), F32),
        scratch_shapes=[pltpu.VMEM((16, depth), BF16)],
        compiler_params=params(10),
        cost_estimate=pl.CostEstimate(
            flops=4 * depth * cols, bytes_accessed=2 * weight.size, transcendentals=0
        ),
        name="modulation",
    )(timestep, guidance, held(weight))


def noisy_kernel(step_ref, image_ref, noise_ref, after_ref, noisy_ref):
    sigma = noise_level(step_ref, (1, image_ref.shape[1]))
    clean, noise = image_ref[...].astype(F32), noise_ref[...].astype(F32)
    noisy_ref[...] = ((1.0 - sigma) * clean + sigma * noise).astype(BF16)


def mix(timestep, image, noise, after):
    rows, width = image.shape
    steps = 2 if width % 256 == 0 else 1
    tokens = pl.BlockSpec((rows, width // steps), lambda s: (0, s))
    return pl.pallas_call(
        noisy_kernel,
        grid=(steps,),
        in_specs=[SCALAR, tokens, tokens, pl.BlockSpec(memory_space=pl.ANY)],
        out_specs=tokens,
        out_shape=jax.ShapeDtypeStruct((rows, width), BF16),
        compiler_params=params(10),
        cost_estimate=pl.CostEstimate(flops=0, bytes_accessed=6 * image.size, transcendentals=0),
        name="noisy",
    )(timestep, held(image), held(noise), after)


def finish_kernel(scale_a, scale_b, scale_loss, side_ref, a_ref, b_ref, sums_ref, got_ref, out_a, out_b, loss_ref):
    half = HD // 2
    rows, width, cols = a_ref.shape[0], a_ref.shape[1], b_ref.shape[1]
    at = rows // 8 * (width + cols)
    other = [got_ref[:, at + i * HD : at + (i + 1) * HD].astype(F32) for i in range(3)]
    total = jnp.sum(sums_ref[...] + (other[0] + other[1] + other[2]), axis=0, keepdims=True)
    loss_ref[...] = jnp.sum(total[:, :half], axis=1, keepdims=True) * scale_loss
    squares_b = jnp.sum(total[:, half:], axis=1, keepdims=True) * scale_b
    unit_b = lax.rsqrt(squares_b + EPS)
    blocks = range(rows // 8)
    mine = [lambda b=b: a_ref[8 * b : 8 * b + 8, :].astype(F32) for b in blocks]
    theirs = [lambda b=b: got_ref[:, b * width : (b + 1) * width].astype(F32) for b in blocks]

    def squares(parts):
        each = functools.reduce(lambda x, y: x + y, [p() * p() for p in parts])
        return jnp.sum(jnp.sum(each, axis=0, keepdims=True), axis=1, keepdims=True)

    unit_a = lax.rsqrt((squares(mine) + squares(theirs)) * scale_a + EPS)
    side = side_ref[0]
    at = rows // 8 * width
    for b in blocks:
        own = pl.ds(pl.multiple_of(side * rows + 8 * b, 8), 8)
        far = pl.ds(pl.multiple_of((1 - side) * rows + 8 * b, 8), 8)
        out_a[own, :] = mine[b]() * unit_a
        out_a[far, :] = theirs[b]() * unit_a
        out_b[own, :] = b_ref[8 * b : 8 * b + 8, :].astype(F32) * unit_b
        out_b[far, :] = got_ref[:, at + b * cols : at + (b + 1) * cols].astype(F32) * unit_b


def finish(side, grad_a, grad_b, sums, got, n, entries):
    (half, width), cols = grad_a.shape, grad_b.shape[1]
    rank = 2 * half
    return pl.pallas_call(
        functools.partial(finish_kernel, 1.0 / (rank * width), 1.0 / (rank * cols * n), 1.0 / entries),
        in_specs=[pl.BlockSpec(memory_space=pltpu.SMEM)] + [VMEM] * 4,
        compiler_params=pltpu.CompilerParams(vmem_limit_bytes=SMALL),
        out_shape=[
            jax.ShapeDtypeStruct((rank, width), F32),
            jax.ShapeDtypeStruct((rank, cols), F32),
            jax.ShapeDtypeStruct((1, 1), F32),
        ],
        name="finish",
    )(side, grad_a, grad_b, sums, got)


def shifted(x, axis, k):
    size = lax.axis_size(axis)
    return lax.ppermute(x, axis, [(i, (i + k) % size) for i in range(size)])


def packed(arrays):
    return len(arrays) > 1 and all(x.shape[0] % 8 == 0 and x.shape[1] % HD == 0 for x in arrays)


def pack(arrays):
    return jnp.concatenate([x[r : r + 8] for x in arrays for r in range(0, x.shape[0], 8)], 1)


def unpack(message, arrays):
    out, at = [], 0
    for x in arrays:
        blocks = []
        for _ in range(0, x.shape[0], 8):
            blocks.append(message[:, at : at + x.shape[1]])
            at += x.shape[1]
        out.append(blocks[0] if len(blocks) == 1 else jnp.concatenate(blocks, 0))
    return out


def send(arrays, group, hop):
    pairs = [(i, i ^ group.mask(hop)) for i in range(group.size)]
    if not packed(arrays):
        return [lax.ppermute(x, group.axes, pairs) for x in arrays]
    return unpack(lax.ppermute(pack(arrays), group.axes, pairs), arrays)


class Group:
    def __init__(self, *places):
        self.axes = tuple(a for a in ("grp", "seq", "dp") if any(a == p[0] for p in places))
        self.size = math.prod(lax.axis_size(a) for a in self.axes)
        self.places = places
        self.count = 1 << len(places)
        sides = [lax.rem(lax.div(lax.axis_index(a), bit), 2) for a, bit in places]
        self.me = functools.reduce(lambda total, side: 2 * total + side, sides, 0)

    def mask(self, hop):
        total = 0
        for i, (axis, bit) in enumerate(reversed(self.places)):
            if hop >> i & 1:
                below = self.axes[self.axes.index(axis) + 1 :]
                total ^= bit * math.prod(lax.axis_size(a) for a in below)
        return total


def cut_of(x, count):
    if x.shape[0] % (8 * count) == 0:
        return 0
    return 1 if x.shape[1] % (count * HD) == 0 else 0


def block(x, dim, count, index):
    each = x.shape[dim] // count
    return lax.dynamic_slice_in_dim(x, index * each, each, dim)


def scatter(wide, narrow=()):
    arrays, group = wide
    more, part = narrow or ([], None)
    dims = [cut_of(x, group.count) for x in arrays]
    more_dims = [cut_of(x, part.count) for x in more]
    sums = [block(x, d, group.count, group.me) for x, d in zip(arrays, dims)]
    more_sums = [block(x, d, part.count, part.me) for x, d in zip(more, more_dims)]
    for hop in range(1, group.count):
        out = [block(x, d, group.count, group.me ^ hop).astype(BF16) for x, d in zip(arrays, dims)]
        join = part is not None and hop < part.count
        if join:
            out += [block(x, d, part.count, part.me ^ hop).astype(BF16) for x, d in zip(more, more_dims)]
        got = [g.astype(F32) for g in send(out, group, hop)]
        sums = [t + g for t, g in zip(sums, got)]
        if join:
            more_sums = [t + g for t, g in zip(more_sums, got[len(sums) :])]
    return sums, dims, more_sums, more_dims


def ordered(parts, me):
    return [
        functools.reduce(
            lambda so_far, hop: jnp.where(me == j ^ hop, parts[hop], so_far), range(1, len(parts)), parts[0]
        )
        for j in range(len(parts))
    ]


def gather(wide, sums, narrow=()):
    arrays, dims, group = wide
    more, more_dims, part = narrow or ([], [], None)
    parts = [[x] for x in arrays]
    more_parts = [[x] for x in more]
    totals = [sums]
    for hop in range(1, group.count):
        join = part is not None and hop < part.count
        out = [*arrays, *(more if join else []), pieces(sums)]
        *got, other = send(out, group, hop)
        other = other.astype(F32)
        totals.append(other[:, :HD] + other[:, HD : 2 * HD] + other[:, 2 * HD :])
        for so_far, g in zip(parts + (more_parts if join else []), got):
            so_far.append(g)
    totals = ordered(totals, group.me)
    sums = functools.reduce(lambda x, y: x + y, totals)
    whole = [jnp.concatenate(ordered(p, group.me), d) for p, d in zip(parts, dims)]
    more_whole = [jnp.concatenate(ordered(p, part.me), d) for p, d in zip(more_parts, more_dims)]
    return whole, more_whole, sums


def pieces(value):
    first = lax.reduce_precision(value, 8, 7)
    rest = value - first
    second = lax.reduce_precision(rest, 8, 7)
    return jnp.concatenate([first, second, rest - second], 1).astype(BF16)


def bits(axis):
    size = lax.axis_size(axis)
    return [1 << i for i in range(size.bit_length() - 1)]


def fold(x):
    half = HD // 2
    return functools.reduce(
        lambda total, c: total + x[:, c : c + half], range(half, x.shape[1], half), x[:, :half]
    )


def on_device(
    image,
    noise,
    text,
    timestep,
    guidance,
    text_token_length,
    image_projection_weight,
    text_projection_weight,
    modulation_weight,
    query_key_norm_gain,
    adapter_down_weight,
    adapter_up_weight,
):
    n, me = lax.axis_size("seq"), lax.axis_index("seq")
    samples = lax.axis_size("grp") * lax.axis_size("dp")
    part = modulation(timestep, guidance, modulation_weight)
    noisy = mix(timestep, image[0], noise[0], part)
    mods = [part] + [shifted(part, "seq", k) for k in range(1, n)]
    noisy_parts = [noisy] + [shifted(noisy, "seq", k) for k in range(1, n)]
    steps = split(image_projection_weight.shape[1] // (3 * HD))[1]
    gain, down, up, words, weights = fetch(
        [query_key_norm_gain, adapter_down_weight.T, adapter_up_weight, text[0]],
        image_projection_weight,
        steps,
        noisy,
    )
    text_parts = [words] + [shifted(words, "seq", k) for k in range(1, n)]
    origin = [lax.rem(me + n - k, n) for k in range(n)]
    ordered = [
        functools.reduce(
            lambda so_far, k: jnp.where(origin[k] == j, mods[k], so_far), range(1, n), mods[0]
        )
        for j in range(n)
    ]
    mod = jnp.concatenate(ordered, 1)
    img_part, txt_part = noisy.shape[0], words.shape[0]
    place = jnp.concatenate(
        [jnp.zeros((n * img_part,), jnp.int32)]
        + [origin[k] * txt_part + jnp.arange(txt_part, dtype=jnp.int32) for k in range(n)]
    )
    bias = jnp.where(place < text_token_length[0], 0.0, -1000000000.0).astype(F32)[None]
    core = lax.rem(lax.axis_index("grp"), 2).astype(jnp.int32)
    far_weights, image_heads = held(image_projection_weight), []
    for k in range(n):
        image_heads = project_image(
            k, n, image_heads, mod, gain, down, up, weights, noisy_parts[k], far_weights
        )
        if k == 0:
            *image_heads, weights = image_heads
    text_heads = project_text(mod, gain, held(text_projection_weight), image_heads[0], text_parts)
    send_a, keep_a, send_b, keep_b, loss = attend(
        core[None], bias, gain, up, image_heads, text_heads
    )
    cores = Group(("grp", 1))
    (got_a,), (got_b,) = send([send_a], cores, 1), send([send_b], cores, 1)
    grad_a, grad_b = keep_a + got_a.astype(F32), keep_b + got_b.astype(F32)
    last, *far = bits("seq")
    far = [(Group(("seq", bit)), []) for bit in reversed(far)]
    for group, dims in far:
        (grad_a,), dims[:], _, _ = scatter(([grad_a], group))
    near, across = Group(("seq", last), ("grp", 2)), Group(("grp", 2))
    (grad_a,), dims_a, (grad_b,), dims_b = scatter(([grad_a], near), ([grad_b], across))
    line = Group(*[("dp", bit) for bit in reversed(bits("dp"))])
    (grad_a, grad_b), dims_z, _, _ = scatter(([grad_a, grad_b], line))
    squares = fold(jnp.sum(grad_b.reshape(-1, min(grad_b.shape[0], 8), grad_b.shape[1]) ** 2, 0))
    squares = jnp.pad(squares, ((0, 8 - squares.shape[0]), (0, 0)))
    sums = jnp.concatenate([fold(loss), squares], 1)
    grads, _, sums = gather(([grad_a.astype(BF16), grad_b.astype(BF16)], dims_z, line), sums)
    (grad_a,), (grad_b,), sums = gather(
        (grads[:1], dims_a, near), sums, (grads[1:], dims_b, across)
    )
    for group, dims in reversed(far):
        (grad_a,), _, sums = gather(([grad_a], dims, group), sums)
    pairs = [(i, i ^ 1) for i in range(cores.size)]
    got = lax.ppermute(pack([grad_a, grad_b, pieces(sums)]), "grp", pairs)
    direction_a, direction_b, loss_mean = finish(
        core[None], grad_a, grad_b, sums, got, n, samples * n * img_part * HEADS * HD
    )
    return (direction_a.T, direction_b, loss_mean[0, 0])


def solution(mesh):
    in_specs = (
        P(("grp", "dp"), "seq", None),
        P(("grp", "dp"), "seq", None),
        P(("grp", "dp"), "seq", None),
        P(("grp", "dp")),
        P(("grp", "dp")),
        P(("grp", "dp")),
        P(None, "seq"),
        P(None, "seq"),
        P(None, "seq"),
        P(),
        P(),
        P(None, "seq"),
    )
    out_specs = (P(), P(None, "seq"), P())
    return jax.shard_map(
        on_device, mesh=mesh, in_specs=in_specs, out_specs=out_specs, check_vma=False
    )
```

```python
import functools
import math

import jax
import jax.numpy as jnp
from jax import lax
from jax.experimental import pallas as pl
from jax.experimental.pallas import tpu as pltpu
from jax.sharding import PartitionSpec as P

HD = 128
HEADS = 16
STEPS = 1000
EPS = 1e-06
F32 = jnp.float32
BF16 = jnp.bfloat16
ROOT = 1.0 / math.sqrt(HD)
LOG2E = 1.0 / math.log(2.0)
SMALL = 10 * 1024 * 1024


def nn(a, b):
    return lax.dot_general(a, b, (((1,), (0,)), ((), ())), preferred_element_type=F32)


def nt(a, b):
    return lax.dot_general(a, b, (((1,), (1,)), ((), ())), preferred_element_type=F32)


def tn(a, b):
    return lax.dot_general(a, b, (((0,), (0,)), ((), ())), preferred_element_type=F32)


def over(total, size, body):
    if total == size:
        body(0)
    else:

        @pl.loop(0, total // size)
        def _(i):
            body(pl.multiple_of(i * size, size))


def inverse_rms(x):
    return lax.rsqrt(jnp.mean(x * x, axis=-1, keepdims=True) + EPS)


def norm_pull(x, gain, dy):
    r = inverse_rms(x)
    u = gain * dy
    return r * (u - x * (r * r * jnp.mean(x * u, axis=-1, keepdims=True)))


def modulate(tokens, mod_ref, kind, width, dest, rows, base):
    size = tokens.shape[0]

    @pl.loop(0, size // 16)
    def _(i):
        v = tokens[pl.ds(pl.multiple_of(i * 16, 16), 16), :].astype(F32)
        center = v - jnp.mean(v, axis=1, keepdims=True)
        spread = jnp.mean(center * center, axis=1, keepdims=True)
        unit = center * lax.rsqrt(spread + EPS)
        for m in range(2):
            shift = mod_ref[m : m + 1, kind * width : (kind + 1) * width]
            scale = mod_ref[m : m + 1, (kind + 1) * width : (kind + 2) * width]
            at = pl.multiple_of(m * rows + base + i * 16, 16)
            dest[pl.ds(at, 16), :] = (unit * (1.0 + scale) + shift).astype(BF16)


def normed(x, gain):
    return (x * inverse_rms(x) * gain).astype(BF16)


def fetches(w_ref, out_ref, sems):
    cols = w_ref.shape[1] // sems.shape[0]
    return [
        pltpu.make_async_copy(
            w_ref.at[:, i * cols : (i + 1) * cols], out_ref.at[:, i * cols : (i + 1) * cols], sems.at[i]
        )
        for i in range(sems.shape[0])
    ]


def held(x):
    return pltpu.with_memory_space_constraint(x, pltpu.HBM)


def text_kernel(n, pair, mod_ref, gain_ref, w_ref, after_ref, *refs):
    parts, (k_ref, v_ref, ht, weights, sems) = refs[:n], refs[n:]
    copies = fetches(w_ref, weights, sems)
    for copy in copies:
        copy.start()
    rows = n * parts[0].shape[0]
    for k in range(n):
        modulate(parts[k], mod_ref, 2, w_ref.shape[0], ht, rows, k * parts[0].shape[0])
    cols = pair * 2 * HD
    size = min(rows, 96)
    for step, copy in enumerate(copies):
        copy.wait()

        def project(start, step=step):
            for j in range(pair):
                head, c = step * pair + j, step * cols + j * 2 * HD
                w = weights[:, c : c + 2 * HD]
                if size == rows:
                    both = nn(ht[...], w)
                    own = [both[:rows], both[rows:]]
                else:
                    own = [nn(ht[pl.ds(m * rows + start, size), :], w) for m in range(2)]
                for m, kv in enumerate(own):
                    k_ref[head, m, pl.ds(start, size), :] = normed(kv[:, :HD], gain_ref[2:3, :])
                    v_ref[head, m, pl.ds(start, size), :] = kv[:, HD:].astype(BF16)

        over(rows, size, project)


def split(count):
    pair = 2 if count % 2 == 0 else 1
    return pair, count // pair


def params(mib):
    return pltpu.CompilerParams(
        dimension_semantics=("arbitrary",), vmem_limit_bytes=mib * 1024 * 1024
    )


VMEM = pl.BlockSpec(memory_space=pltpu.VMEM)
HELD = pl.BlockSpec(memory_space=pltpu.HBM)


def project_text(mod, gain, w, after, parts):
    n, (part, width) = len(parts), parts[0].shape
    pair, steps = split(w.shape[1] // (2 * HD))
    out = pltpu.VMEM((pair * steps, 2, n * part, HD), BF16)
    return pl.pallas_call(
        functools.partial(text_kernel, n, pair),
        in_specs=[VMEM, VMEM, HELD, pl.BlockSpec(memory_space=pl.ANY)] + [VMEM] * n,
        out_specs=[VMEM] * 2,
        out_shape=[out, out],
        scratch_shapes=[
            pltpu.VMEM((2 * n * part, width), BF16),
            pltpu.VMEM(w.shape, w.dtype),
            pltpu.SemaphoreType.DMA((steps,)),
        ],
        compiler_params=pltpu.CompilerParams(vmem_limit_bytes=2 * SMALL),
        cost_estimate=pl.CostEstimate(
            flops=4 * n * part * w.size, bytes_accessed=2 * w.size, transcendentals=0
        ),
        name="project_text",
    )(mod, gain, w, after, *parts)


def image_kernel(pair, index, past, mod_ref, gain_ref, down_ref, up_ref, w_ref, tokens, *refs):
    first = past == 0
    q_ref, k_ref, v_ref, x_ref, low_ref, hs_ref, *rest = refs[past:]
    weights = w_ref
    if first:
        weights, *small, hi, sems, small_sems = rest
        given = (gain_ref, down_ref, up_ref)
        fetched = [
            pltpu.make_async_copy(g, s, small_sems.at[i]) for i, (g, s) in enumerate(zip(given, small))
        ]
        gain_ref, down_ref, up_ref = small
        for copy in fetched + fetches(w_ref, weights, sems)[:2]:
            copy.start()
    else:
        (hi,) = rest
    rows = tokens.shape[0]
    part = slice(index * rows, (index + 1) * rows)
    modulate(tokens, mod_ref, 0, w_ref.shape[0], hi, rows, 0)
    if first:
        for copy in fetched:
            copy.wait()
    hs_ref[part, :] = hi[rows:, :]
    low_ref[part, :] = nt(hi[rows:, :], down_ref[...]).astype(BF16)
    cols = pair * 3 * HD

    def project(step):
        columns = pl.ds(pl.multiple_of(step * cols, cols), cols)
        if first:
            pltpu.make_async_copy(w_ref.at[:, columns], weights.at[:, columns], sems.at[step]).wait()

            @pl.when(step + 2 < w_ref.shape[1] // cols)
            def _():
                later = pl.ds(pl.multiple_of((step + 2) * cols, cols), cols)
                pltpu.make_async_copy(w_ref.at[:, later], weights.at[:, later], sems.at[step + 2]).start()

        out = nn(hi[...], weights[:, columns])
        student = out[rows:] + nn(low_ref[part, :], up_ref[:, columns])
        for j in range(pair):
            head, c = step * pair + j, j * 3 * HD
            for m, own in enumerate((out[:rows], student)):
                for kind, dest in enumerate((q_ref, k_ref)):
                    x = own[:, c + kind * HD : c + (kind + 1) * HD]
                    dest[head, m, part, :] = normed(x, gain_ref[kind : kind + 1, :])
                    if m == 1:
                        x_ref[head, kind, part, :] = x
                v_ref[head, m, part, :] = own[:, c + 2 * HD : c + 3 * HD].astype(BF16)

    pl.loop(0, w_ref.shape[1] // cols)(project)


def project_image(part, n, before, mod, gain, down, up, w, tokens):
    (rows, width), rank = tokens.shape, up.shape[0]
    pair, steps = split(w.shape[1] // (3 * HD))
    heads = (pair * steps, 2, n * rows, HD)
    shapes = [pltpu.VMEM(heads, BF16)] * 3 + [
        pltpu.VMEM(heads, F32),
        pltpu.VMEM((n * rows, rank), BF16),
        pltpu.VMEM((n * rows, width), BF16),
    ]
    scratch = [pltpu.VMEM((2 * rows, width), BF16)]
    if not before:
        shapes += [pltpu.VMEM(x.shape, x.dtype) for x in (w, gain, down, up)]
        scratch += [pltpu.SemaphoreType.DMA((steps,)), pltpu.SemaphoreType.DMA((3,))]
    return pl.pallas_call(
        functools.partial(image_kernel, pair, part, len(before)),
        in_specs=[VMEM] + [VMEM if before else HELD] * 4 + [VMEM] * (1 + len(before)),
        out_specs=[VMEM] * len(shapes),
        out_shape=shapes,
        input_output_aliases={6 + i: i for i in range(len(before))},
        scratch_shapes=scratch,
        compiler_params=pltpu.CompilerParams(vmem_limit_bytes=SMALL),
        cost_estimate=pl.CostEstimate(
            flops=4 * rows * w.size, bytes_accessed=2 * w.size, transcendentals=0
        ),
        name="project_image",
    )(mod, gain, down, up, w, tokens, *before)


def attend_kernel(
    steps, pair, samples, where_ref, bias_ref, gain_ref, up_ref, q_ref, k_ref, v_ref, x_ref, kt_ref, vt_ref,
    low_ref, hs_ref, send_a, keep_a, send_b, keep_b, loss_ref, lowt, glt, k_s, v_s, dk_s, dv_s, gq, whole
):
    core = where_ref[0]
    half = send_a.shape[0]
    lowt[...] = low_ref[...].astype(F32).T.astype(BF16)
    glt[...] = jnp.zeros_like(glt)
    loss_ref[...] = jnp.zeros_like(loss_ref)

    def share(value, columns, send, keep):
        whole[:, : value.shape[1]] = value
        mine = pl.ds(pl.multiple_of(core * half, 8), half)
        other = pl.ds(pl.multiple_of((1 - core) * half, 8), half)
        keep[:, columns] = whole[mine, : value.shape[1]]
        send[:, columns] = whole[other, : value.shape[1]].astype(send.dtype)

    @pl.loop(0, steps)
    def _(step):
        columns = pl.ds(pl.multiple_of(step * gq.shape[1], HD), gq.shape[1])
        group = pl.ds(step * pair, pair)
        attend_heads(
            pair, samples, bias_ref, gain_ref, *[r.at[group] for r in (q_ref, k_ref, v_ref, x_ref, kt_ref, vt_ref)],
            loss_ref, k_s, v_s, dk_s, dv_s, gq,
        )
        share(nn(lowt[...], gq[...]), columns, send_b, keep_b)
        glt[...] += nt(up_ref[:, columns], gq[...])

    g = glt[...]
    g1 = g.astype(BF16)
    rest = g - g1.astype(F32)
    g2 = rest.astype(BF16)
    g3 = (rest - g2.astype(F32)).astype(BF16)
    stack = jnp.concatenate([g1, g2, g3], 0)
    rank = g.shape[0]
    full = nn(stack, hs_ref[...])
    share(full[:rank] + full[rank : 2 * rank] + full[2 * rank :], slice(0, full.shape[1]), send_a, keep_a)


def attend_heads(
    pair, samples, bias_ref, gain_ref, q_ref, k_ref, v_ref, x_ref, kt_ref, vt_ref, loss_ref, k_s, v_s, dk_s, dv_s, gq
):
    rows = q_ref.shape[2]
    block = min(rows, 160)
    heads = range(pair)
    for j in heads:
        for m in range(2):
            k_s[j, m, :rows, :] = k_ref[j, m]
            k_s[j, m, rows:, :] = kt_ref[j, m]
            v_s[j, m, :rows, :] = v_ref[j, m]
            v_s[j, m, rows:, :] = vt_ref[j, m]
    if rows > block:
        dk_s[...] = jnp.zeros_like(dk_s)
        dv_s[...] = jnp.zeros_like(dv_s)
    gain_q, gain_k = gain_ref[0:1, :], gain_ref[1:2, :]

    def attend(start):
        at = pl.ds(start, block)
        both = [(j, m) for j in heads for m in range(2)]
        scores = {(j, m): nt(q_ref[j, m, at, :], k_s[j, m]) for j, m in both}
        weights = {i: jnp.exp2(scores[i] * (ROOT * LOG2E) + bias_ref[...]) for i in both}
        scale = {i: 1.0 / jnp.sum(weights[i], axis=1, keepdims=True) for i in both}
        probs = {i: weights[i] * scale[i] for i in both}
        rounded = {i: probs[i].astype(BF16) for i in both}
        out = {(j, m): nn(rounded[j, m], v_s[j, m]) for j, m in both}
        diff = [out[j, 1] - out[j, 0].astype(BF16).astype(F32) for j in heads]
        total = diff[0] * diff[0]
        for d in diff[1:]:
            total = total + d * d
        loss_ref[...] += jnp.sum(total.reshape(block // 8, 8, HD), axis=0)
        dout = [(d * (2.0 / samples)).astype(BF16) for d in diff]
        dprobs = [nt(dout[j], v_s[j, 1]).astype(BF16).astype(F32) for j in heads]
        dv = [tn(rounded[j, 1], dout[j]) for j in heads]
        inner = [jnp.sum(dprobs[j] * probs[j, 1], axis=1, keepdims=True) for j in heads]
        dscores = [(probs[j, 1] * (dprobs[j] - inner[j]) * ROOT).astype(BF16) for j in heads]
        dq = [nn(dscores[j], k_s[j, 1]).astype(BF16).astype(F32) for j in heads]
        dk = [tn(dscores[j], q_ref[j, 1, at, :]) for j in heads]
        for j in heads:
            c = j * 3 * HD
            gq[at, c : c + HD] = norm_pull(x_ref[j, 0, at, :], gain_q, dq[j]).astype(BF16)
            if rows > block:
                dk_s[j] += dk[j][:rows]
                dv_s[j] += dv[j][:rows]
            else:
                dk_s[j] = dk[j][:rows]
                dv_s[j] = dv[j][:rows]

    over(rows, block, attend)

    def rest(start):
        at = pl.ds(start, block)
        for j in heads:
            c = j * 3 * HD
            dk = dk_s[j, at, :].astype(BF16).astype(F32)
            gq[at, c + HD : c + 2 * HD] = norm_pull(x_ref[j, 1, at, :], gain_k, dk).astype(BF16)
            gq[at, c + 2 * HD : c + 3 * HD] = dv_s[j, at, :].astype(BF16)

    over(rows, block, rest)


def attend(where, bias, gain, up, image, text):
    q, k, v, x, low, hs = image
    kt, vt = text
    (rank, img_cols), width = up.shape, hs.shape[1]
    count, _, rows, _ = q.shape
    trows = kt.shape[2]
    pair, steps = split(count)
    half, ic = rank // 2, pair * 3 * HD
    samples = lax.axis_size("grp") * lax.axis_size("dp")
    out_a, out_b = (half, width), (half, img_cols)
    return pl.pallas_call(
        functools.partial(attend_kernel, steps, pair, samples),
        in_specs=[pl.BlockSpec(memory_space=pltpu.SMEM)] + [VMEM] * 11,
        out_specs=[VMEM] * 5,
        out_shape=[
            jax.ShapeDtypeStruct(out_a, BF16),
            jax.ShapeDtypeStruct(out_a, F32),
            jax.ShapeDtypeStruct(out_b, BF16),
            jax.ShapeDtypeStruct(out_b, F32),
            jax.ShapeDtypeStruct((8, HD), F32),
        ],
        scratch_shapes=[
            pltpu.VMEM((rank, rows), BF16),
            pltpu.VMEM((rank, rows), F32),
            pltpu.VMEM((pair, 2, rows + trows, HD), BF16),
            pltpu.VMEM((pair, 2, rows + trows, HD), BF16),
            pltpu.VMEM((pair, rows, HD), F32),
            pltpu.VMEM((pair, rows, HD), F32),
            pltpu.VMEM((rows, ic), BF16),
            pltpu.VMEM((rank, max(width, ic)), F32),
        ],
        compiler_params=pltpu.CompilerParams(vmem_limit_bytes=2 * SMALL),
        cost_estimate=pl.CostEstimate(
            flops=16 * count * rows * (rows + trows) * HD,
            bytes_accessed=8_000_000,
            transcendentals=2 * count * rows * (rows + trows),
        ),
        name="attend",
    )(where, bias, gain, up, q, k, v, x, kt, vt, low, hs)


def noise_level(step_ref, shape):
    return (jnp.full(shape, step_ref[0], jnp.int32).astype(F32) + 1.0) / STEPS


def embedding(value):
    count = value.shape[1] // 2
    lane = lax.broadcasted_iota(jnp.int32, value.shape, 1)
    place = lax.rem(lane, count).astype(F32)
    angles = 1000.0 * value * jnp.exp(-math.log(10000.0) * place / count)
    wave = jnp.where(lane < count, jnp.cos(angles), jnp.sin(angles))
    return wave / (1.0 + jnp.exp(-wave))


def modulation_kernel(step_ref, guidance_ref, weight_ref, part_ref, emb):
    @pl.when(pl.program_id(0) == 0)
    def _():
        half = emb.shape[1] // 2
        time = embedding(noise_level(step_ref, (1, half)))
        guide = embedding(jnp.full((1, half), guidance_ref[0], F32))
        row = lax.broadcasted_iota(jnp.int32, (emb.shape[0], half), 0)
        emb[:, :half] = jnp.where(row >= 0, time, 0.0).astype(BF16)
        emb[:, half:] = jnp.where(row == 0, guide, 0.0).astype(BF16)

    part_ref[...] = nn(emb[...], weight_ref[...])[: part_ref.shape[0]]


SCALAR = pl.BlockSpec(memory_space=pltpu.SMEM)


def modulation(timestep, guidance, weight):
    depth, cols = weight.shape
    steps = 2 if cols % 256 == 0 else 1
    return pl.pallas_call(
        modulation_kernel,
        grid=(steps,),
        in_specs=[SCALAR, SCALAR, pl.BlockSpec((depth, cols // steps), lambda s: (0, s))],
        out_specs=pl.BlockSpec((2, cols // steps), lambda s: (0, s)),
        out_shape=jax.ShapeDtypeStruct((2, cols), F32),
        scratch_shapes=[pltpu.VMEM((16, depth), BF16)],
        compiler_params=params(10),
        cost_estimate=pl.CostEstimate(
            flops=4 * depth * cols, bytes_accessed=2 * weight.size, transcendentals=0
        ),
        name="modulation",
    )(timestep, guidance, held(weight))


def noisy_kernel(step_ref, image_ref, noise_ref, after_ref, noisy_ref):
    sigma = noise_level(step_ref, (1, image_ref.shape[1]))
    clean, noise = image_ref[...].astype(F32), noise_ref[...].astype(F32)
    noisy_ref[...] = ((1.0 - sigma) * clean + sigma * noise).astype(BF16)


def mix(timestep, image, noise, after):
    rows, width = image.shape
    steps = 2 if width % 256 == 0 else 1
    tokens = pl.BlockSpec((rows, width // steps), lambda s: (0, s))
    return pl.pallas_call(
        noisy_kernel,
        grid=(steps,),
        in_specs=[SCALAR, tokens, tokens, pl.BlockSpec(memory_space=pl.ANY)],
        out_specs=tokens,
        out_shape=jax.ShapeDtypeStruct((rows, width), BF16),
        compiler_params=params(10),
        cost_estimate=pl.CostEstimate(flops=0, bytes_accessed=6 * image.size, transcendentals=0),
        name="noisy",
    )(timestep, held(image), held(noise), after)


def finish_kernel(scale_a, scale_b, scale_loss, side_ref, a_ref, b_ref, sums_ref, got_ref, out_a, out_b, loss_ref):
    half = HD // 2
    rows, width, cols = a_ref.shape[0], a_ref.shape[1], b_ref.shape[1]
    at = rows // 8 * (width + cols)
    other = [got_ref[:, at + i * HD : at + (i + 1) * HD].astype(F32) for i in range(3)]
    total = jnp.sum(sums_ref[...] + (other[0] + other[1] + other[2]), axis=0, keepdims=True)
    loss_ref[...] = jnp.sum(total[:, :half], axis=1, keepdims=True) * scale_loss
    squares_b = jnp.sum(total[:, half:], axis=1, keepdims=True) * scale_b
    unit_b = lax.rsqrt(squares_b + EPS)
    blocks = range(rows // 8)
    mine = [lambda b=b: a_ref[8 * b : 8 * b + 8, :].astype(F32) for b in blocks]
    theirs = [lambda b=b: got_ref[:, b * width : (b + 1) * width].astype(F32) for b in blocks]

    def squares(parts):
        each = functools.reduce(lambda x, y: x + y, [p() * p() for p in parts])
        return jnp.sum(jnp.sum(each, axis=0, keepdims=True), axis=1, keepdims=True)

    unit_a = lax.rsqrt((squares(mine) + squares(theirs)) * scale_a + EPS)
    side = side_ref[0]
    at = rows // 8 * width
    for b in blocks:
        own = pl.ds(pl.multiple_of(side * rows + 8 * b, 8), 8)
        far = pl.ds(pl.multiple_of((1 - side) * rows + 8 * b, 8), 8)
        out_a[own, :] = mine[b]() * unit_a
        out_a[far, :] = theirs[b]() * unit_a
        out_b[own, :] = b_ref[8 * b : 8 * b + 8, :].astype(F32) * unit_b
        out_b[far, :] = got_ref[:, at + b * cols : at + (b + 1) * cols].astype(F32) * unit_b


def finish(side, grad_a, grad_b, sums, got, n, entries):
    (half, width), cols = grad_a.shape, grad_b.shape[1]
    rank = 2 * half
    return pl.pallas_call(
        functools.partial(finish_kernel, 1.0 / (rank * width), 1.0 / (rank * cols * n), 1.0 / entries),
        in_specs=[pl.BlockSpec(memory_space=pltpu.SMEM)] + [VMEM] * 4,
        compiler_params=pltpu.CompilerParams(vmem_limit_bytes=SMALL),
        out_shape=[
            jax.ShapeDtypeStruct((rank, width), F32),
            jax.ShapeDtypeStruct((rank, cols), F32),
            jax.ShapeDtypeStruct((1, 1), F32),
        ],
        name="finish",
    )(side, grad_a, grad_b, sums, got)


def shifted(x, axis, k):
    size = lax.axis_size(axis)
    return lax.ppermute(x, axis, [(i, (i + k) % size) for i in range(size)])


def packed(arrays):
    return len(arrays) > 1 and all(x.shape[0] % 8 == 0 and x.shape[1] % HD == 0 for x in arrays)


def pack(arrays):
    return jnp.concatenate([x[r : r + 8] for x in arrays for r in range(0, x.shape[0], 8)], 1)


def unpack(message, arrays):
    out, at = [], 0
    for x in arrays:
        blocks = []
        for _ in range(0, x.shape[0], 8):
            blocks.append(message[:, at : at + x.shape[1]])
            at += x.shape[1]
        out.append(blocks[0] if len(blocks) == 1 else jnp.concatenate(blocks, 0))
    return out


def send(arrays, group, hop):
    pairs = [(i, i ^ group.mask(hop)) for i in range(group.size)]
    if not packed(arrays):
        return [lax.ppermute(x, group.axes, pairs) for x in arrays]
    return unpack(lax.ppermute(pack(arrays), group.axes, pairs), arrays)


class Group:
    def __init__(self, *places):
        self.axes = tuple(a for a in ("grp", "seq", "dp") if any(a == p[0] for p in places))
        self.size = math.prod(lax.axis_size(a) for a in self.axes)
        self.places = places
        self.count = 1 << len(places)
        sides = [lax.rem(lax.div(lax.axis_index(a), bit), 2) for a, bit in places]
        self.me = functools.reduce(lambda total, side: 2 * total + side, sides, 0)

    def mask(self, hop):
        total = 0
        for i, (axis, bit) in enumerate(reversed(self.places)):
            if hop >> i & 1:
                below = self.axes[self.axes.index(axis) + 1 :]
                total ^= bit * math.prod(lax.axis_size(a) for a in below)
        return total


def cut_of(x, count):
    if x.shape[0] % (8 * count) == 0:
        return 0
    return 1 if x.shape[1] % (count * HD) == 0 else 0


def block(x, dim, count, index):
    each = x.shape[dim] // count
    return lax.dynamic_slice_in_dim(x, index * each, each, dim)


def scatter(wide, narrow=()):
    arrays, group = wide
    more, part = narrow or ([], None)
    dims = [cut_of(x, group.count) for x in arrays]
    more_dims = [cut_of(x, part.count) for x in more]
    sums = [block(x, d, group.count, group.me) for x, d in zip(arrays, dims)]
    more_sums = [block(x, d, part.count, part.me) for x, d in zip(more, more_dims)]
    for hop in range(1, group.count):
        out = [block(x, d, group.count, group.me ^ hop).astype(BF16) for x, d in zip(arrays, dims)]
        join = part is not None and hop < part.count
        if join:
            out += [block(x, d, part.count, part.me ^ hop).astype(BF16) for x, d in zip(more, more_dims)]
        got = [g.astype(F32) for g in send(out, group, hop)]
        sums = [t + g for t, g in zip(sums, got)]
        if join:
            more_sums = [t + g for t, g in zip(more_sums, got[len(sums) :])]
    return sums, dims, more_sums, more_dims


def ordered(parts, me):
    return [
        functools.reduce(
            lambda so_far, hop: jnp.where(me == j ^ hop, parts[hop], so_far), range(1, len(parts)), parts[0]
        )
        for j in range(len(parts))
    ]


def gather(wide, sums, narrow=()):
    arrays, dims, group = wide
    more, more_dims, part = narrow or ([], [], None)
    parts = [[x] for x in arrays]
    more_parts = [[x] for x in more]
    totals = [sums]
    for hop in range(1, group.count):
        join = part is not None and hop < part.count
        out = [*arrays, *(more if join else []), pieces(sums)]
        *got, other = send(out, group, hop)
        other = other.astype(F32)
        totals.append(other[:, :HD] + other[:, HD : 2 * HD] + other[:, 2 * HD :])
        for so_far, g in zip(parts + (more_parts if join else []), got):
            so_far.append(g)
    totals = ordered(totals, group.me)
    sums = functools.reduce(lambda x, y: x + y, totals)
    whole = [jnp.concatenate(ordered(p, group.me), d) for p, d in zip(parts, dims)]
    more_whole = [jnp.concatenate(ordered(p, part.me), d) for p, d in zip(more_parts, more_dims)]
    return whole, more_whole, sums


def pieces(value):
    first = lax.reduce_precision(value, 8, 7)
    rest = value - first
    second = lax.reduce_precision(rest, 8, 7)
    return jnp.concatenate([first, second, rest - second], 1).astype(BF16)


def bits(axis):
    size = lax.axis_size(axis)
    return [1 << i for i in range(size.bit_length() - 1)]


def fold(x):
    half = HD // 2
    return functools.reduce(
        lambda total, c: total + x[:, c : c + half], range(half, x.shape[1], half), x[:, :half]
    )


def on_device(
    image,
    noise,
    text,
    timestep,
    guidance,
    text_token_length,
    image_projection_weight,
    text_projection_weight,
    modulation_weight,
    query_key_norm_gain,
    adapter_down_weight,
    adapter_up_weight,
):
    n, me = lax.axis_size("seq"), lax.axis_index("seq")
    samples = lax.axis_size("grp") * lax.axis_size("dp")
    part = modulation(timestep, guidance, modulation_weight)
    noisy = mix(timestep, image[0], noise[0], part)
    mods = [part] + [shifted(part, "seq", k) for k in range(1, n)]
    noisy_parts = [noisy] + [shifted(noisy, "seq", k) for k in range(1, n)]
    words = text[0]
    text_parts = [words] + [shifted(words, "seq", k) for k in range(1, n)]
    origin = [lax.rem(me + n - k, n) for k in range(n)]
    ordered = [
        functools.reduce(
            lambda so_far, k: jnp.where(origin[k] == j, mods[k], so_far), range(1, n), mods[0]
        )
        for j in range(n)
    ]
    mod = jnp.concatenate(ordered, 1)
    img_part, txt_part = noisy.shape[0], words.shape[0]
    place = jnp.concatenate(
        [jnp.zeros((n * img_part,), jnp.int32)]
        + [origin[k] * txt_part + jnp.arange(txt_part, dtype=jnp.int32) for k in range(n)]
    )
    bias = jnp.where(place < text_token_length[0], 0.0, -1000000000.0).astype(F32)[None]
    core = lax.rem(lax.axis_index("grp"), 2).astype(jnp.int32)
    gain = query_key_norm_gain
    down, up = adapter_down_weight.T, adapter_up_weight
    weights, image_heads = [held(x) for x in (image_projection_weight, gain, down, up)], []
    for k in range(n):
        weight, gain, down, up = weights
        image_heads = project_image(k, n, image_heads, mod, gain, down, up, weight, noisy_parts[k])
        if k == 0:
            image_heads, weights = image_heads[:6], image_heads[6:]
    _, gain, _, up = weights
    text_heads = project_text(mod, gain, held(text_projection_weight), image_heads[0], text_parts)
    send_a, keep_a, send_b, keep_b, loss = attend(
        core[None], bias, gain, up, image_heads, text_heads
    )
    cores = Group(("grp", 1))
    (got_a,), (got_b,) = send([send_a], cores, 1), send([send_b], cores, 1)
    grad_a, grad_b = keep_a + got_a.astype(F32), keep_b + got_b.astype(F32)
    last, *far = bits("seq")
    far = [(Group(("seq", bit)), []) for bit in reversed(far)]
    for group, dims in far:
        (grad_a,), dims[:], _, _ = scatter(([grad_a], group))
    near, across = Group(("seq", last), ("grp", 2)), Group(("grp", 2))
    (grad_a,), dims_a, (grad_b,), dims_b = scatter(([grad_a], near), ([grad_b], across))
    line = Group(*[("dp", bit) for bit in reversed(bits("dp"))])
    (grad_a, grad_b), dims_z, _, _ = scatter(([grad_a, grad_b], line))
    squares = fold(jnp.sum(grad_b.reshape(-1, min(grad_b.shape[0], 8), grad_b.shape[1]) ** 2, 0))
    squares = jnp.pad(squares, ((0, 8 - squares.shape[0]), (0, 0)))
    sums = jnp.concatenate([fold(loss), squares], 1)
    grads, _, sums = gather(([grad_a.astype(BF16), grad_b.astype(BF16)], dims_z, line), sums)
    (grad_a,), (grad_b,), sums = gather(
        (grads[:1], dims_a, near), sums, (grads[1:], dims_b, across)
    )
    for group, dims in reversed(far):
        (grad_a,), _, sums = gather(([grad_a], dims, group), sums)
    pairs = [(i, i ^ 1) for i in range(cores.size)]
    got = lax.ppermute(pack([grad_a, grad_b, pieces(sums)]), "grp", pairs)
    direction_a, direction_b, loss_mean = finish(
        core[None], grad_a, grad_b, sums, got, n, samples * n * img_part * HEADS * HD
    )
    return (direction_a.T, direction_b, loss_mean[0, 0])


def solution(mesh):
    in_specs = (
        P(("grp", "dp"), "seq", None),
        P(("grp", "dp"), "seq", None),
        P(("grp", "dp"), "seq", None),
        P(("grp", "dp")),
        P(("grp", "dp")),
        P(("grp", "dp")),
        P(None, "seq"),
        P(None, "seq"),
        P(None, "seq"),
        P(),
        P(),
        P(None, "seq"),
    )
    out_specs = (P(), P(None, "seq"), P())
    return jax.shard_map(
        on_device, mesh=mesh, in_specs=in_specs, out_specs=out_specs, check_vma=False
    )
```

```python
import functools
import math

import jax
import jax.numpy as jnp
from jax import lax
from jax.experimental import pallas as pl
from jax.experimental.pallas import tpu as pltpu
from jax.sharding import PartitionSpec as P

HD = 128
HEADS = 16
STEPS = 1000
EPS = 1e-06
F32 = jnp.float32
BF16 = jnp.bfloat16
ROOT = 1.0 / math.sqrt(HD)
LOG2E = 1.0 / math.log(2.0)
SMALL = 10 * 1024 * 1024


def nn(a, b):
    return lax.dot_general(a, b, (((1,), (0,)), ((), ())), preferred_element_type=F32)


def nt(a, b):
    return lax.dot_general(a, b, (((1,), (1,)), ((), ())), preferred_element_type=F32)


def tn(a, b):
    return lax.dot_general(a, b, (((0,), (0,)), ((), ())), preferred_element_type=F32)


def over(total, size, body):
    if total == size:
        body(0)
    else:

        @pl.loop(0, total // size)
        def _(i):
            body(pl.multiple_of(i * size, size))


def inverse_rms(x):
    return lax.rsqrt(jnp.mean(x * x, axis=-1, keepdims=True) + EPS)


def norm_pull(x, gain, dy):
    r = inverse_rms(x)
    u = gain * dy
    return r * (u - x * (r * r * jnp.mean(x * u, axis=-1, keepdims=True)))


def modulate(tokens, mod_ref, kind, width, dest, rows, base):
    size = tokens.shape[0]

    @pl.loop(0, size // 16)
    def _(i):
        v = tokens[pl.ds(pl.multiple_of(i * 16, 16), 16), :].astype(F32)
        center = v - jnp.mean(v, axis=1, keepdims=True)
        spread = jnp.mean(center * center, axis=1, keepdims=True)
        unit = center * lax.rsqrt(spread + EPS)
        for m in range(2):
            shift = mod_ref[m : m + 1, kind * width : (kind + 1) * width]
            scale = mod_ref[m : m + 1, (kind + 1) * width : (kind + 2) * width]
            at = pl.multiple_of(m * rows + base + i * 16, 16)
            dest[pl.ds(at, 16), :] = (unit * (1.0 + scale) + shift).astype(BF16)


def normed(x, gain):
    return (x * inverse_rms(x) * gain).astype(BF16)


def fetches(w_ref, out_ref, sems):
    cols = w_ref.shape[1] // sems.shape[0]
    return [
        pltpu.make_async_copy(
            w_ref.at[:, i * cols : (i + 1) * cols], out_ref.at[:, i * cols : (i + 1) * cols], sems.at[i]
        )
        for i in range(sems.shape[0])
    ]


def held(x):
    return pltpu.with_memory_space_constraint(x, pltpu.HBM)


def text_kernel(n, pair, mod_ref, gain_ref, w_ref, after_ref, *refs):
    parts, (k_ref, v_ref, ht, weights, sems) = refs[:n], refs[n:]
    copies = fetches(w_ref, weights, sems)
    for copy in copies:
        copy.start()
    rows = n * parts[0].shape[0]
    for k in range(n):
        modulate(parts[k], mod_ref, 2, w_ref.shape[0], ht, rows, k * parts[0].shape[0])
    cols = pair * 2 * HD
    size = min(rows, 96)
    for step, copy in enumerate(copies):
        copy.wait()

        def project(start, step=step):
            for j in range(pair):
                head, c = step * pair + j, step * cols + j * 2 * HD
                w = weights[:, c : c + 2 * HD]
                if size == rows:
                    both = nn(ht[...], w)
                    own = [both[:rows], both[rows:]]
                else:
                    own = [nn(ht[pl.ds(m * rows + start, size), :], w) for m in range(2)]
                for m, kv in enumerate(own):
                    k_ref[head, m, pl.ds(start, size), :] = normed(kv[:, :HD], gain_ref[2:3, :])
                    v_ref[head, m, pl.ds(start, size), :] = kv[:, HD:].astype(BF16)

        over(rows, size, project)


def split(count):
    pair = 2 if count % 2 == 0 else 1
    return pair, count // pair


def params(mib):
    return pltpu.CompilerParams(
        dimension_semantics=("arbitrary",), vmem_limit_bytes=mib * 1024 * 1024
    )


VMEM = pl.BlockSpec(memory_space=pltpu.VMEM)
HELD = pl.BlockSpec(memory_space=pltpu.HBM)


def project_text(mod, gain, w, after, parts):
    n, (part, width) = len(parts), parts[0].shape
    pair, steps = split(w.shape[1] // (2 * HD))
    out = pltpu.VMEM((pair * steps, 2, n * part, HD), BF16)
    return pl.pallas_call(
        functools.partial(text_kernel, n, pair),
        in_specs=[VMEM, VMEM, HELD, pl.BlockSpec(memory_space=pl.ANY)] + [VMEM] * n,
        out_specs=[VMEM] * 2,
        out_shape=[out, out],
        scratch_shapes=[
            pltpu.VMEM((2 * n * part, width), BF16),
            pltpu.VMEM(w.shape, w.dtype),
            pltpu.SemaphoreType.DMA((steps,)),
        ],
        compiler_params=pltpu.CompilerParams(vmem_limit_bytes=2 * SMALL),
        cost_estimate=pl.CostEstimate(
            flops=4 * n * part * w.size, bytes_accessed=2 * w.size, transcendentals=0
        ),
        name="project_text",
    )(mod, gain, w, after, *parts)


def image_kernel(pair, index, past, mod_ref, gain_ref, down_ref, up_ref, w_ref, tokens, *refs):
    first = past == 0
    q_ref, k_ref, v_ref, x_ref, low_ref, hs_ref, *rest = refs[past:]
    weights = w_ref
    if first:
        weights, *small, hi, sems, small_sems = rest
        given = (gain_ref, down_ref, up_ref)
        fetched = [
            pltpu.make_async_copy(g, s, small_sems.at[i]) for i, (g, s) in enumerate(zip(given, small))
        ]
        gain_ref, down_ref, up_ref = small
        for copy in fetched + fetches(w_ref, weights, sems)[:2]:
            copy.start()
    else:
        (hi,) = rest
    rows = tokens.shape[0]
    part = slice(index * rows, (index + 1) * rows)
    modulate(tokens, mod_ref, 0, w_ref.shape[0], hi, rows, 0)
    if first:
        for copy in fetched:
            copy.wait()
    hs_ref[part, :] = hi[rows:, :]
    low_ref[part, :] = nt(hi[rows:, :], down_ref[...]).astype(BF16)
    cols = pair * 3 * HD

    def project(step):
        columns = pl.ds(pl.multiple_of(step * cols, cols), cols)
        if first:
            pltpu.make_async_copy(w_ref.at[:, columns], weights.at[:, columns], sems.at[step]).wait()

            @pl.when(step + 2 < w_ref.shape[1] // cols)
            def _():
                later = pl.ds(pl.multiple_of((step + 2) * cols, cols), cols)
                pltpu.make_async_copy(w_ref.at[:, later], weights.at[:, later], sems.at[step + 2]).start()

        out = nn(hi[...], weights[:, columns])
        student = out[rows:] + nn(low_ref[part, :], up_ref[:, columns])
        for j in range(pair):
            head, c = step * pair + j, j * 3 * HD
            for m, own in enumerate((out[:rows], student)):
                for kind, dest in enumerate((q_ref, k_ref)):
                    x = own[:, c + kind * HD : c + (kind + 1) * HD]
                    dest[head, m, part, :] = normed(x, gain_ref[kind : kind + 1, :])
                    if m == 1:
                        x_ref[head, kind, part, :] = x
                v_ref[head, m, part, :] = own[:, c + 2 * HD : c + 3 * HD].astype(BF16)

    pl.loop(0, w_ref.shape[1] // cols)(project)


def project_image(part, n, before, mod, gain, down, up, w, tokens):
    (rows, width), rank = tokens.shape, up.shape[0]
    pair, steps = split(w.shape[1] // (3 * HD))
    heads = (pair * steps, 2, n * rows, HD)
    shapes = [pltpu.VMEM(heads, BF16)] * 3 + [
        pltpu.VMEM(heads, F32),
        pltpu.VMEM((n * rows, rank), BF16),
        pltpu.VMEM((n * rows, width), BF16),
    ]
    scratch = [pltpu.VMEM((2 * rows, width), BF16)]
    if not before:
        shapes += [pltpu.VMEM(x.shape, x.dtype) for x in (w, gain, down, up)]
        scratch += [pltpu.SemaphoreType.DMA((steps,)), pltpu.SemaphoreType.DMA((3,))]
    return pl.pallas_call(
        functools.partial(image_kernel, pair, part, len(before)),
        in_specs=[VMEM] + [VMEM if before else HELD] * 4 + [VMEM] * (1 + len(before)),
        out_specs=[VMEM] * len(shapes),
        out_shape=shapes,
        input_output_aliases={6 + i: i for i in range(len(before))},
        scratch_shapes=scratch,
        compiler_params=pltpu.CompilerParams(vmem_limit_bytes=SMALL),
        cost_estimate=pl.CostEstimate(
            flops=4 * rows * w.size, bytes_accessed=2 * w.size, transcendentals=0
        ),
        name="project_image",
    )(mod, gain, down, up, w, tokens, *before)


def attend_kernel(
    steps, pair, samples, where_ref, bias_ref, gain_ref, up_ref, q_ref, k_ref, v_ref, x_ref, kt_ref, vt_ref,
    low_ref, hs_ref, send_a, keep_a, send_b, keep_b, loss_ref, lowt, glt, k_s, v_s, dk_s, dv_s, gq, whole
):
    core = where_ref[0]
    half = send_a.shape[0]
    lowt[...] = low_ref[...].astype(F32).T.astype(BF16)
    glt[...] = jnp.zeros_like(glt)
    loss_ref[...] = jnp.zeros_like(loss_ref)

    def share(value, columns, send, keep):
        whole[:, : value.shape[1]] = value
        mine = pl.ds(pl.multiple_of(core * half, 8), half)
        other = pl.ds(pl.multiple_of((1 - core) * half, 8), half)
        keep[:, columns] = whole[mine, : value.shape[1]]
        send[:, columns] = whole[other, : value.shape[1]].astype(send.dtype)

    @pl.loop(0, steps)
    def _(step):
        columns = pl.ds(pl.multiple_of(step * gq.shape[1], HD), gq.shape[1])
        group = pl.ds(step * pair, pair)
        attend_heads(
            pair, samples, bias_ref, gain_ref, *[r.at[group] for r in (q_ref, k_ref, v_ref, x_ref, kt_ref, vt_ref)],
            loss_ref, k_s, v_s, dk_s, dv_s, gq,
        )
        share(nn(lowt[...], gq[...]), columns, send_b, keep_b)
        glt[...] += nt(up_ref[:, columns], gq[...])

    g = glt[...]
    g1 = g.astype(BF16)
    rest = g - g1.astype(F32)
    g2 = rest.astype(BF16)
    g3 = (rest - g2.astype(F32)).astype(BF16)
    stack = jnp.concatenate([g1, g2, g3], 0)
    rank = g.shape[0]
    full = nn(stack, hs_ref[...])
    share(full[:rank] + full[rank : 2 * rank] + full[2 * rank :], slice(0, full.shape[1]), send_a, keep_a)


def attend_heads(
    pair, samples, bias_ref, gain_ref, q_ref, k_ref, v_ref, x_ref, kt_ref, vt_ref, loss_ref, k_s, v_s, dk_s, dv_s, gq
):
    rows = q_ref.shape[2]
    block = min(rows, 160)
    heads = range(pair)
    for j in heads:
        for m in range(2):
            k_s[j, m, :rows, :] = k_ref[j, m]
            k_s[j, m, rows:, :] = kt_ref[j, m]
            v_s[j, m, :rows, :] = v_ref[j, m]
            v_s[j, m, rows:, :] = vt_ref[j, m]
    if rows > block:
        dk_s[...] = jnp.zeros_like(dk_s)
        dv_s[...] = jnp.zeros_like(dv_s)
    gain_q, gain_k = gain_ref[0:1, :], gain_ref[1:2, :]

    def attend(start):
        at = pl.ds(start, block)
        both = [(j, m) for j in heads for m in range(2)]
        scores = {(j, m): nt(q_ref[j, m, at, :], k_s[j, m]) for j, m in both}
        weights = {i: jnp.exp2(scores[i] * (ROOT * LOG2E) + bias_ref[...]) for i in both}
        scale = {i: 1.0 / jnp.sum(weights[i], axis=1, keepdims=True) for i in both}
        probs = {i: weights[i] * scale[i] for i in both}
        rounded = {i: probs[i].astype(BF16) for i in both}
        out = {(j, m): nn(rounded[j, m], v_s[j, m]) for j, m in both}
        diff = [out[j, 1] - out[j, 0].astype(BF16).astype(F32) for j in heads]
        total = diff[0] * diff[0]
        for d in diff[1:]:
            total = total + d * d
        loss_ref[...] += jnp.sum(total.reshape(block // 8, 8, HD), axis=0)
        dout = [(d * (2.0 / samples)).astype(BF16) for d in diff]
        dprobs = [nt(dout[j], v_s[j, 1]).astype(BF16).astype(F32) for j in heads]
        dv = [tn(rounded[j, 1], dout[j]) for j in heads]
        inner = [jnp.sum(dprobs[j] * probs[j, 1], axis=1, keepdims=True) for j in heads]
        dscores = [(probs[j, 1] * (dprobs[j] - inner[j]) * ROOT).astype(BF16) for j in heads]
        dq = [nn(dscores[j], k_s[j, 1]).astype(BF16).astype(F32) for j in heads]
        dk = [tn(dscores[j], q_ref[j, 1, at, :]) for j in heads]
        for j in heads:
            c = j * 3 * HD
            gq[at, c : c + HD] = norm_pull(x_ref[j, 0, at, :], gain_q, dq[j]).astype(BF16)
            if rows > block:
                dk_s[j] += dk[j][:rows]
                dv_s[j] += dv[j][:rows]
            else:
                dk_s[j] = dk[j][:rows]
                dv_s[j] = dv[j][:rows]

    over(rows, block, attend)

    def rest(start):
        at = pl.ds(start, block)
        for j in heads:
            c = j * 3 * HD
            dk = dk_s[j, at, :].astype(BF16).astype(F32)
            gq[at, c + HD : c + 2 * HD] = norm_pull(x_ref[j, 1, at, :], gain_k, dk).astype(BF16)
            gq[at, c + 2 * HD : c + 3 * HD] = dv_s[j, at, :].astype(BF16)

    over(rows, block, rest)


def attend(where, bias, gain, up, image, text):
    q, k, v, x, low, hs = image
    kt, vt = text
    (rank, img_cols), width = up.shape, hs.shape[1]
    count, _, rows, _ = q.shape
    trows = kt.shape[2]
    pair, steps = split(count)
    half, ic = rank // 2, pair * 3 * HD
    samples = lax.axis_size("grp") * lax.axis_size("dp")
    out_a, out_b = (half, width), (half, img_cols)
    return pl.pallas_call(
        functools.partial(attend_kernel, steps, pair, samples),
        in_specs=[pl.BlockSpec(memory_space=pltpu.SMEM)] + [VMEM] * 11,
        out_specs=[VMEM] * 5,
        out_shape=[
            jax.ShapeDtypeStruct(out_a, BF16),
            jax.ShapeDtypeStruct(out_a, F32),
            jax.ShapeDtypeStruct(out_b, BF16),
            jax.ShapeDtypeStruct(out_b, F32),
            jax.ShapeDtypeStruct((8, HD), F32),
        ],
        scratch_shapes=[
            pltpu.VMEM((rank, rows), BF16),
            pltpu.VMEM((rank, rows), F32),
            pltpu.VMEM((pair, 2, rows + trows, HD), BF16),
            pltpu.VMEM((pair, 2, rows + trows, HD), BF16),
            pltpu.VMEM((pair, rows, HD), F32),
            pltpu.VMEM((pair, rows, HD), F32),
            pltpu.VMEM((rows, ic), BF16),
            pltpu.VMEM((rank, max(width, ic)), F32),
        ],
        compiler_params=pltpu.CompilerParams(vmem_limit_bytes=2 * SMALL),
        cost_estimate=pl.CostEstimate(
            flops=16 * count * rows * (rows + trows) * HD,
            bytes_accessed=8_000_000,
            transcendentals=2 * count * rows * (rows + trows),
        ),
        name="attend",
    )(where, bias, gain, up, q, k, v, x, kt, vt, low, hs)


def noise_level(step_ref, shape):
    return (jnp.full(shape, step_ref[0], jnp.int32).astype(F32) + 1.0) / STEPS


def embedding(value):
    count = value.shape[1] // 2
    lane = lax.broadcasted_iota(jnp.int32, value.shape, 1)
    place = lax.rem(lane, count).astype(F32)
    angles = 1000.0 * value * jnp.exp(-math.log(10000.0) * place / count)
    wave = jnp.where(lane < count, jnp.cos(angles), jnp.sin(angles))
    return wave / (1.0 + jnp.exp(-wave))


def modulation_kernel(step_ref, guidance_ref, weight_ref, part_ref, emb):
    @pl.when(pl.program_id(0) == 0)
    def _():
        half = emb.shape[1] // 2
        time = embedding(noise_level(step_ref, (1, half)))
        guide = embedding(jnp.full((1, half), guidance_ref[0], F32))
        row = lax.broadcasted_iota(jnp.int32, (emb.shape[0], half), 0)
        emb[:, :half] = jnp.where(row >= 0, time, 0.0).astype(BF16)
        emb[:, half:] = jnp.where(row == 0, guide, 0.0).astype(BF16)

    part_ref[...] = nn(emb[...], weight_ref[...])[: part_ref.shape[0]]


SCALAR = pl.BlockSpec(memory_space=pltpu.SMEM)


def modulation(timestep, guidance, weight):
    depth, cols = weight.shape
    steps = 2 if cols % 256 == 0 else 1
    return pl.pallas_call(
        modulation_kernel,
        grid=(steps,),
        in_specs=[SCALAR, SCALAR, pl.BlockSpec((depth, cols // steps), lambda s: (0, s))],
        out_specs=pl.BlockSpec((2, cols // steps), lambda s: (0, s)),
        out_shape=jax.ShapeDtypeStruct((2, cols), F32),
        scratch_shapes=[pltpu.VMEM((16, depth), BF16)],
        compiler_params=params(10),
        cost_estimate=pl.CostEstimate(
            flops=4 * depth * cols, bytes_accessed=2 * weight.size, transcendentals=0
        ),
        name="modulation",
    )(timestep, guidance, held(weight))


def noisy_kernel(step_ref, image_ref, noise_ref, after_ref, noisy_ref):
    sigma = noise_level(step_ref, (1, image_ref.shape[1]))
    clean, noise = image_ref[...].astype(F32), noise_ref[...].astype(F32)
    noisy_ref[...] = ((1.0 - sigma) * clean + sigma * noise).astype(BF16)


def mix(timestep, image, noise, after):
    rows, width = image.shape
    steps = 2 if width % 256 == 0 else 1
    tokens = pl.BlockSpec((rows, width // steps), lambda s: (0, s))
    return pl.pallas_call(
        noisy_kernel,
        grid=(steps,),
        in_specs=[SCALAR, tokens, tokens, pl.BlockSpec(memory_space=pl.ANY)],
        out_specs=tokens,
        out_shape=jax.ShapeDtypeStruct((rows, width), BF16),
        compiler_params=params(10),
        cost_estimate=pl.CostEstimate(flops=0, bytes_accessed=6 * image.size, transcendentals=0),
        name="noisy",
    )(timestep, held(image), held(noise), after)


def finish_kernel(scale_a, scale_b, scale_loss, side_ref, a_ref, b_ref, sums_ref, got_ref, out_a, out_b, loss_ref):
    half = HD // 2
    rows, width, cols = a_ref.shape[0], a_ref.shape[1], b_ref.shape[1]
    at = rows // 8 * (width + cols)
    other = [got_ref[:, at + i * HD : at + (i + 1) * HD].astype(F32) for i in range(3)]
    total = jnp.sum(sums_ref[...] + (other[0] + other[1] + other[2]), axis=0, keepdims=True)
    loss_ref[...] = jnp.sum(total[:, :half], axis=1, keepdims=True) * scale_loss
    squares_b = jnp.sum(total[:, half:], axis=1, keepdims=True) * scale_b
    unit_b = lax.rsqrt(squares_b + EPS)
    blocks = range(rows // 8)
    mine = [lambda b=b: a_ref[8 * b : 8 * b + 8, :].astype(F32) for b in blocks]
    theirs = [lambda b=b: got_ref[:, b * width : (b + 1) * width].astype(F32) for b in blocks]

    def squares(parts):
        each = functools.reduce(lambda x, y: x + y, [p() * p() for p in parts])
        return jnp.sum(jnp.sum(each, axis=0, keepdims=True), axis=1, keepdims=True)

    unit_a = lax.rsqrt((squares(mine) + squares(theirs)) * scale_a + EPS)
    side = side_ref[0]
    at = rows // 8 * width
    for b in blocks:
        own = pl.ds(pl.multiple_of(side * rows + 8 * b, 8), 8)
        far = pl.ds(pl.multiple_of((1 - side) * rows + 8 * b, 8), 8)
        out_a[own, :] = mine[b]() * unit_a
        out_a[far, :] = theirs[b]() * unit_a
        out_b[own, :] = b_ref[8 * b : 8 * b + 8, :].astype(F32) * unit_b
        out_b[far, :] = got_ref[:, at + b * cols : at + (b + 1) * cols].astype(F32) * unit_b


def finish(side, grad_a, grad_b, sums, got, n, entries):
    (half, width), cols = grad_a.shape, grad_b.shape[1]
    rank = 2 * half
    return pl.pallas_call(
        functools.partial(finish_kernel, 1.0 / (rank * width), 1.0 / (rank * cols * n), 1.0 / entries),
        in_specs=[pl.BlockSpec(memory_space=pltpu.SMEM)] + [VMEM] * 4,
        compiler_params=pltpu.CompilerParams(vmem_limit_bytes=SMALL),
        out_shape=[
            jax.ShapeDtypeStruct((rank, width), F32),
            jax.ShapeDtypeStruct((rank, cols), F32),
            jax.ShapeDtypeStruct((1, 1), F32),
        ],
        name="finish",
    )(side, grad_a, grad_b, sums, got)


def shifted(x, axis, k):
    size = lax.axis_size(axis)
    return lax.ppermute(x, axis, [(i, (i + k) % size) for i in range(size)])


def packed(arrays):
    return len(arrays) > 1 and all(x.shape[0] % 8 == 0 and x.shape[1] % HD == 0 for x in arrays)


def pack(arrays):
    return jnp.concatenate([x[r : r + 8] for x in arrays for r in range(0, x.shape[0], 8)], 1)


def unpack(message, arrays):
    out, at = [], 0
    for x in arrays:
        blocks = []
        for _ in range(0, x.shape[0], 8):
            blocks.append(message[:, at : at + x.shape[1]])
            at += x.shape[1]
        out.append(blocks[0] if len(blocks) == 1 else jnp.concatenate(blocks, 0))
    return out


def send(arrays, group, hop):
    pairs = [(i, i ^ group.mask(hop)) for i in range(group.size)]
    if not packed(arrays):
        return [lax.ppermute(x, group.axes, pairs) for x in arrays]
    return unpack(lax.ppermute(pack(arrays), group.axes, pairs), arrays)


class Group:
    def __init__(self, *places):
        self.axes = tuple(a for a in ("grp", "seq", "dp") if any(a == p[0] for p in places))
        self.size = math.prod(lax.axis_size(a) for a in self.axes)
        self.places = places
        self.count = 1 << len(places)
        sides = [lax.rem(lax.div(lax.axis_index(a), bit), 2) for a, bit in places]
        self.me = functools.reduce(lambda total, side: 2 * total + side, sides, 0)

    def mask(self, hop):
        total = 0
        for i, (axis, bit) in enumerate(reversed(self.places)):
            if hop >> i & 1:
                below = self.axes[self.axes.index(axis) + 1 :]
                total ^= bit * math.prod(lax.axis_size(a) for a in below)
        return total


def cut_of(x, count):
    if x.shape[0] % (8 * count) == 0:
        return 0
    return 1 if x.shape[1] % (count * HD) == 0 else 0


def block(x, dim, count, index):
    each = x.shape[dim] // count
    return lax.dynamic_slice_in_dim(x, index * each, each, dim)


def scatter(wide, narrow=()):
    arrays, group = wide
    more, part = narrow or ([], None)
    dims = [cut_of(x, group.count) for x in arrays]
    more_dims = [cut_of(x, part.count) for x in more]
    sums = [block(x, d, group.count, group.me) for x, d in zip(arrays, dims)]
    more_sums = [block(x, d, part.count, part.me) for x, d in zip(more, more_dims)]
    for hop in range(1, group.count):
        out = [block(x, d, group.count, group.me ^ hop).astype(BF16) for x, d in zip(arrays, dims)]
        join = part is not None and hop < part.count
        if join:
            out += [block(x, d, part.count, part.me ^ hop).astype(BF16) for x, d in zip(more, more_dims)]
        got = [g.astype(F32) for g in send(out, group, hop)]
        sums = [t + g for t, g in zip(sums, got)]
        if join:
            more_sums = [t + g for t, g in zip(more_sums, got[len(sums) :])]
    return sums, dims, more_sums, more_dims


def ordered(parts, me):
    return [
        functools.reduce(
            lambda so_far, hop: jnp.where(me == j ^ hop, parts[hop], so_far), range(1, len(parts)), parts[0]
        )
        for j in range(len(parts))
    ]


def gather(wide, sums, narrow=()):
    arrays, dims, group = wide
    more, more_dims, part = narrow or ([], [], None)
    parts = [[x] for x in arrays]
    more_parts = [[x] for x in more]
    totals = [sums]
    for hop in range(1, group.count):
        join = part is not None and hop < part.count
        out = [*arrays, *(more if join else []), pieces(sums)]
        *got, other = send(out, group, hop)
        other = other.astype(F32)
        totals.append(other[:, :HD] + other[:, HD : 2 * HD] + other[:, 2 * HD :])
        for so_far, g in zip(parts + (more_parts if join else []), got):
            so_far.append(g)
    totals = ordered(totals, group.me)
    sums = functools.reduce(lambda x, y: x + y, totals)
    whole = [jnp.concatenate(ordered(p, group.me), d) for p, d in zip(parts, dims)]
    more_whole = [jnp.concatenate(ordered(p, part.me), d) for p, d in zip(more_parts, more_dims)]
    return whole, more_whole, sums


def pieces(value):
    first = lax.reduce_precision(value, 8, 7)
    rest = value - first
    second = lax.reduce_precision(rest, 8, 7)
    return jnp.concatenate([first, second, rest - second], 1).astype(BF16)


def bits(axis):
    size = lax.axis_size(axis)
    return [1 << i for i in range(size.bit_length() - 1)]


def fold(x):
    half = HD // 2
    return functools.reduce(
        lambda total, c: total + x[:, c : c + half], range(half, x.shape[1], half), x[:, :half]
    )


def on_device(
    image,
    noise,
    text,
    timestep,
    guidance,
    text_token_length,
    image_projection_weight,
    text_projection_weight,
    modulation_weight,
    query_key_norm_gain,
    adapter_down_weight,
    adapter_up_weight,
):
    n, me = lax.axis_size("seq"), lax.axis_index("seq")
    samples = lax.axis_size("grp") * lax.axis_size("dp")
    part = modulation(timestep, guidance, modulation_weight)
    noisy = mix(timestep, image[0], noise[0], part)
    mods = [part] + [shifted(part, "seq", k) for k in range(1, n)]
    noisy_parts = [noisy] + [shifted(noisy, "seq", k) for k in range(1, n)]
    words = text[0]
    origin = [lax.rem(me + n - k, n) for k in range(n)]
    ordered = [
        functools.reduce(
            lambda so_far, k: jnp.where(origin[k] == j, mods[k], so_far), range(1, n), mods[0]
        )
        for j in range(n)
    ]
    mod = jnp.concatenate(ordered, 1)
    img_part, txt_part = noisy.shape[0], words.shape[0]
    place = jnp.concatenate(
        [jnp.zeros((n * img_part,), jnp.int32)]
        + [origin[k] * txt_part + jnp.arange(txt_part, dtype=jnp.int32) for k in range(n)]
    )
    bias = jnp.where(place < text_token_length[0], 0.0, -1000000000.0).astype(F32)[None]
    core = lax.rem(lax.axis_index("grp"), 2).astype(jnp.int32)
    gain = query_key_norm_gain
    down, up = adapter_down_weight.T, adapter_up_weight
    weights, image_heads = [held(x) for x in (image_projection_weight, gain, down, up)], []
    for k in range(n):
        weight, gain, down, up = weights
        image_heads = project_image(k, n, image_heads, mod, gain, down, up, weight, noisy_parts[k])
        if k == 0:
            image_heads, weights = image_heads[:6], image_heads[6:]
            later, _ = lax.optimization_barrier((words, image_heads[4]))
            text_parts = [words] + [shifted(later, "seq", hop) for hop in range(1, n)]
    _, gain, _, up = weights
    text_heads = project_text(mod, gain, held(text_projection_weight), image_heads[0], text_parts)
    send_a, keep_a, send_b, keep_b, loss = attend(
        core[None], bias, gain, up, image_heads, text_heads
    )
    cores = Group(("grp", 1))
    (got_a,), (got_b,) = send([send_a], cores, 1), send([send_b], cores, 1)
    grad_a, grad_b = keep_a + got_a.astype(F32), keep_b + got_b.astype(F32)
    last, *far = bits("seq")
    far = [(Group(("seq", bit)), []) for bit in reversed(far)]
    for group, dims in far:
        (grad_a,), dims[:], _, _ = scatter(([grad_a], group))
    near, across = Group(("seq", last), ("grp", 2)), Group(("grp", 2))
    (grad_a,), dims_a, (grad_b,), dims_b = scatter(([grad_a], near), ([grad_b], across))
    line = Group(*[("dp", bit) for bit in reversed(bits("dp"))])
    (grad_a, grad_b), dims_z, _, _ = scatter(([grad_a, grad_b], line))
    squares = fold(jnp.sum(grad_b.reshape(-1, min(grad_b.shape[0], 8), grad_b.shape[1]) ** 2, 0))
    squares = jnp.pad(squares, ((0, 8 - squares.shape[0]), (0, 0)))
    sums = jnp.concatenate([fold(loss), squares], 1)
    grads, _, sums = gather(([grad_a.astype(BF16), grad_b.astype(BF16)], dims_z, line), sums)
    (grad_a,), (grad_b,), sums = gather(
        (grads[:1], dims_a, near), sums, (grads[1:], dims_b, across)
    )
    for group, dims in reversed(far):
        (grad_a,), _, sums = gather(([grad_a], dims, group), sums)
    pairs = [(i, i ^ 1) for i in range(cores.size)]
    got = lax.ppermute(pack([grad_a, grad_b, pieces(sums)]), "grp", pairs)
    direction_a, direction_b, loss_mean = finish(
        core[None], grad_a, grad_b, sums, got, n, samples * n * img_part * HEADS * HD
    )
    return (direction_a.T, direction_b, loss_mean[0, 0])


def solution(mesh):
    in_specs = (
        P(("grp", "dp"), "seq", None),
        P(("grp", "dp"), "seq", None),
        P(("grp", "dp"), "seq", None),
        P(("grp", "dp")),
        P(("grp", "dp")),
        P(("grp", "dp")),
        P(None, "seq"),
        P(None, "seq"),
        P(None, "seq"),
        P(),
        P(),
        P(None, "seq"),
    )
    out_specs = (P(), P(None, "seq"), P())
    return jax.shard_map(
        on_device, mesh=mesh, in_specs=in_specs, out_specs=out_specs, check_vma=False
    )
```
